32 devices in a mesh: dp: 8 (over z, core), tensor: 4 (over y, x).
Axes of the slice: x: 2, y: 2, z: 4, core: 2. Of those that a mesh axis runs over, the one named last changes fastest.
Arguments:
- tokens: bfloat16 [12288, 1024], P('dp'), may hold values from -6 to 6
- image_ids: int32 [12288], P('dp'), may hold values from 0 to 8, never falling along the last dimension, each value on 1 to 1370 neighbouring positions
- cotangent: bfloat16 [12288, 1024], P('dp'), may hold values from -6 to 6
- ln1_gain: float32 [2, 1024], replicated, may hold values from 0.25 to 1.75
- ln1_bias: float32 [2, 1024], replicated, may hold values from -3 to 3
- qkv_weight: bfloat16 [2, 1024, 3, 1024], P(None, None, None, 'tensor'), may hold values from -0.1875 to 0.1875
- qv_bias: float32 [2, 2, 1024], P(None, None, 'tensor'), may hold values from -3 to 3
- proj_weight: bfloat16 [2, 1024, 1024], P(None, 'tensor'), may hold values from -3 to 3
- proj_bias: float32 [2, 1024], replicated, may hold values from -5 to 5
- scale_attn: float32 [2, 1024], replicated, may hold values from 0.3 to 1.5
- ln2_gain: float32 [2, 1024], replicated, may hold values from 0.25 to 1.75
- ln2_bias: float32 [2, 1024], replicated, may hold values from -2 to 2
- fc1_weight: bfloat16 [2, 1024, 4096], P(None, None, 'tensor'), may hold values from -0.1875 to 0.1875
- fc1_bias: float32 [2, 4096], P(None, 'tensor'), may hold values from -3 to 3
- fc2_weight: bfloat16 [2, 4096, 1024], P(None, 'tensor'), may hold values from -0.09375 to 0.09375
- fc2_bias: float32 [2, 1024], replicated, may hold values from -2 to 2
- scale_mlp: float32 [2, 1024], replicated, may hold values from 0.3 to 1.5
Outputs:
- output: float32 [12288, 1024], P('dp')
- grad_tokens: float32 [12288, 1024], P('dp')
- grad_ln1_gain: float32 [2, 1024], replicated
- grad_ln1_bias: float32 [2, 1024], replicated
- grad_qkv_weight: float32 [2, 1024, 3, 1024], P(None, None, None, 'tensor')
- grad_qv_bias: float32 [2, 2, 1024], P(None, None, 'tensor')
- grad_proj_weight: float32 [2, 1024, 1024], P(None, 'tensor')
- grad_proj_bias: float32 [2, 1024], replicated
- grad_scale_attn: float32 [2, 1024], replicated
- grad_ln2_gain: float32 [2, 1024], replicated
- grad_ln2_bias: float32 [2, 1024], replicated
- grad_fc1_weight: float32 [2, 1024, 4096], P(None, None, 'tensor')
- grad_fc1_bias: float32 [2, 4096], P(None, 'tensor')
- grad_fc2_weight: float32 [2, 4096, 1024], P(None, 'tensor')
- grad_fc2_bias: float32 [2, 1024], replicated
- grad_scale_mlp: float32 [2, 1024], replicated
The draws below stay inside these ranges and needn't reach their ends.
Inputs may be any that keep to these rules, and one draw needn't show every extreme that they name: `image_ids`: images are consecutive runs of tokens numbered in order; each image has at most 1370 tokens and one has exactly 1370.
All inputs are finite; a program needn't handle non-finite values.
Results may differ from the reference program's by a relative error of at most 0.02.
The reference program's roundings to bfloat16 on the way count: a program that leaves them out, or rounds other values in their place, can miss the bound.
Values may be sent and summed in bfloat16 or wider, within the bound.
A program may use at most 384 MiB of HBM per device.

```python
import math
import jax
import jax.numpy as jnp
import numpy as np
from jax import lax

D = 1024
HEADS = 16
HD = 64
FF = 4096
LAYERS = 2
MAXLEN = 1370
TOK_DEV = 1536
TOKENS = 12288
IMAGES = 9


def shard_levels(rng, extent, split, least, largest):
    factor_of = 1.0
    for axis_at, blocks in split:
        draws = jax.random.uniform(jax.random.fold_in(jax.random.fold_in(rng, 6), axis_at), (blocks,), jnp.float32, least / len(split), largest / len(split))
        factor_of = factor_of * jnp.repeat(jnp.exp(draws), extent[axis_at] // blocks).reshape((-1,) + (1,) * (len(extent) - 1 - axis_at))
    return factor_of


def length_profile(count, total, bound, slope):
    loads = [(1 << 20) // math.isqrt(standing ** slope) + 1 for standing in range(2, count + 1)]
    surplus, given = total - bound - (count - 1), [1] * (count - 1)
    while surplus > 0:
        free = [i for i in range(count - 1) if given[i] < bound]
        pool, left = sum([loads[i] for i in free]), surplus
        for i in free:
            more = min(bound - given[i], max(1, left * loads[i] // pool), surplus)
            given[i] = given[i] + more
            surplus = surplus - more
    return np.array([bound] + given)


def uneven(key, number_of, total, bound, lean):
    if number_of == 2:
        one = jax.random.randint(key, (), max(1, total - bound), min(bound, total - 1) + 1)
        return jnp.stack([one, total - one])
    tallies = jnp.asarray(length_profile(number_of, total, bound, lean), jnp.int32)
    pairs = (number_of - 1) // 2
    donor, receiver = tallies[1:1 + 2 * pairs:2], tallies[2:2 + 2 * pairs:2]
    room = jnp.minimum(donor - 1, bound - receiver)
    shifted = jax.random.randint(jax.random.fold_in(key, 1), (pairs,), 0, 1 << 20) % (room + 1)
    tallies = tallies.at[1:1 + 2 * pairs:2].set(donor - shifted).at[2:2 + 2 * pairs:2].set(receiver + shifted)
    return tallies[jax.random.permutation(jax.random.fold_in(key, 2), number_of)]


def normal_values(own_key, shape, scale, reach, pieces=(), kind=jnp.bfloat16):
    drawn = scale * jax.random.normal(own_key, shape, jnp.float32)
    if pieces:
        drawn = drawn * shard_levels(own_key, shape, pieces, -0.22, 0.18)
    return jnp.clip(drawn, -reach, reach).astype(kind)


def setup_inputs(seed: int = 0) -> dict:
    key_list = jax.random.split(jax.random.key(seed), 18)
    return {
        "tokens": normal_values(key_list[0], (TOKENS, D), 1.0, 6.0, ((0, 8),)),
        "image_ids": jnp.searchsorted(jnp.cumsum(uneven(key_list[1], IMAGES, TOKENS, MAXLEN, 0)), jnp.arange(TOKENS), side="right").astype(jnp.int32),
        "cotangent": normal_values(key_list[2], (TOKENS, D), 1.0, 6.0, ((0, 8),)),
        "ln1_gain": jnp.clip(1.0 + 0.15 * jax.random.normal(key_list[3], (LAYERS, D), jnp.float32), 0.25, 1.75),
        "ln1_bias": normal_values(key_list[4], (LAYERS, D), 0.5, 3.0, (), jnp.float32),
        "qkv_weight": normal_values(key_list[5], (LAYERS, D, 3, D), D ** -0.5, 0.1875, ((3, 4),)),
        "qv_bias": normal_values(key_list[6], (LAYERS, 2, D), 0.5, 3.0, ((2, 4),), jnp.float32),
        "proj_weight": normal_values(key_list[7], (LAYERS, D, D), (max(D // 256, 1)) ** -0.5, 3.0, ((1, 4),)),
        "proj_bias": normal_values(key_list[8], (LAYERS, D), 1.0, 5.0, (), jnp.float32),
        "scale_attn": jnp.clip(jnp.exp(jax.random.uniform(key_list[9], (LAYERS, D), jnp.float32, math.log(0.3), math.log(1.5))), 0.3, 1.5),
        "ln2_gain": jnp.clip(1.0 + 0.15 * jax.random.normal(key_list[10], (LAYERS, D), jnp.float32), 0.25, 1.75),
        "ln2_bias": normal_values(key_list[11], (LAYERS, D), 0.3, 2.0, (), jnp.float32),
        "fc1_weight": normal_values(key_list[12], (LAYERS, D, FF), D ** -0.5, 0.1875, ((2, 4),)),
        "fc1_bias": normal_values(key_list[13], (LAYERS, FF), 0.5, 3.0, ((1, 4),), jnp.float32),
        "fc2_weight": normal_values(key_list[14], (LAYERS, FF, D), FF ** -0.5, 0.09375, ((1, 4),)),
        "fc2_bias": normal_values(key_list[15], (LAYERS, D), 0.3, 2.0, (), jnp.float32),
        "scale_mlp": jnp.clip(jnp.exp(jax.random.uniform(key_list[16], (LAYERS, D), jnp.float32, math.log(0.3), math.log(1.5))), 0.3, 1.5),
    }


eps = 1e-06
masked_score = -1e+30
half_root = 0.7071067811865476
density_scale = 0.3989422804014327

def norm_forward(stream, gain_row, offset):
    centre = lax.optimization_barrier(jnp.mean(stream, axis=-1, keepdims=True))
    centred = stream - centre
    spread = lax.rsqrt(lax.optimization_barrier(jnp.mean(centred * centred, axis=-1, keepdims=True)) + eps)
    normed = centred * spread
    return (normed * gain_row + offset, normed, spread)

def norm_backward(upstream, normed, spread, gain_row):
    scaled = upstream * gain_row
    centred_grad = scaled - lax.optimization_barrier(jnp.mean(scaled, axis=-1, keepdims=True)) - normed * lax.optimization_barrier(jnp.mean(scaled * normed, axis=-1, keepdims=True))
    return (centred_grad * spread, lax.optimization_barrier(jnp.sum(upstream * normed, axis=0)), lax.optimization_barrier(jnp.sum(upstream, axis=0)))

def gelu_pair(before):
    cumulative = 0.5 * (1.0 + lax.erf(before * half_root))
    density = jnp.exp(-0.5 * before * before) * density_scale
    return (before * cumulative, cumulative + before * density)

def padded(array, fill):
    widths = [(TOK_DEV, TOK_DEV)] + [(0, 0)] * (array.ndim - 1)
    return jnp.pad(array, widths, constant_values=fill)

def slice_window(array, start, length):
    return lax.dynamic_slice_in_dim(array, start, length, 0)

def head_scores(query_head, key_head, allowed):
    scores = jnp.dot(query_head, key_head.T, preferred_element_type=jnp.float32) * HD ** (-0.5)
    return jnp.where(allowed, scores, masked_score)

def attention_forward(queries, keys, values, image_ids):
    slice_count = queries.shape[0] // TOK_DEV
    keys_wide = padded(keys, 0.0)
    values_wide = padded(values, 0.0)
    ids_wide = padded(image_ids, -1)

    def per_slice(slice_index):
        start = slice_index * TOK_DEV
        allowed = slice_window(image_ids, start, TOK_DEV)[:, None] == slice_window(ids_wide, start, 3 * TOK_DEV)[None, :]
        query_slice = jnp.transpose(slice_window(queries, start, TOK_DEV), (1, 0, 2))
        key_slice = jnp.transpose(slice_window(keys_wide, start, 3 * TOK_DEV), (1, 0, 2))
        value_slice = jnp.transpose(slice_window(values_wide, start, 3 * TOK_DEV), (1, 0, 2))

        def per_head(triple):
            query_head, key_head, value_head = triple
            scores = head_scores(query_head, key_head, allowed)
            row_peak = lax.optimization_barrier(jnp.max(scores, axis=-1, keepdims=True))
            weights = jnp.exp(scores - row_peak)
            row_total = lax.optimization_barrier(jnp.sum(weights, axis=-1, keepdims=True))
            mixture = jnp.dot(weights.astype(jnp.bfloat16), value_head, preferred_element_type=jnp.float32)
            return ((mixture / row_total).astype(jnp.bfloat16), (row_peak + jnp.log(row_total))[:, 0])
        results, logsums = lax.map(per_head, (query_slice, key_slice, value_slice))
        return (jnp.transpose(results, (1, 0, 2)), jnp.transpose(logsums))
    results, logsums = lax.map(per_slice, jnp.arange(slice_count, dtype=jnp.int32))
    return (results.reshape(queries.shape), logsums.reshape(queries.shape[0], queries.shape[1]))

def attention_backward(queries, keys, values, image_ids, attended, upstream, logsums):
    row_count, head_count, head_width = queries.shape
    slice_count = row_count // TOK_DEV
    score_scale = head_width ** (-0.5)
    keys_wide = padded(keys, 0.0)
    values_wide = padded(values, 0.0)
    ids_wide = padded(image_ids, -1)

    def per_slice(running, slice_index):
        start = slice_index * TOK_DEV
        allowed = slice_window(image_ids, start, TOK_DEV)[:, None] == slice_window(ids_wide, start, 3 * TOK_DEV)[None, :]
        query_slice = jnp.transpose(slice_window(queries, start, TOK_DEV), (1, 0, 2))
        key_slice = jnp.transpose(slice_window(keys_wide, start, 3 * TOK_DEV), (1, 0, 2))
        value_slice = jnp.transpose(slice_window(values_wide, start, 3 * TOK_DEV), (1, 0, 2))
        out_slice = jnp.transpose(slice_window(attended, start, TOK_DEV), (1, 0, 2))
        grad_slice = jnp.transpose(slice_window(upstream, start, TOK_DEV), (1, 0, 2))
        lse_slice = jnp.transpose(slice_window(logsums, start, TOK_DEV))

        def per_head(bundle):
            query_head, key_head, value_head, out_head, grad_head, lse_head = bundle
            scores = head_scores(query_head, key_head, allowed)
            probabilities = jnp.exp(scores - lse_head[:, None])
            row_delta = lax.optimization_barrier(jnp.sum(grad_head.astype(jnp.float32) * out_head.astype(jnp.float32), axis=-1))
            grad_prob = jnp.dot(grad_head, value_head.T, preferred_element_type=jnp.float32)
            grad_score = (probabilities * (grad_prob - row_delta[:, None])).astype(jnp.bfloat16)
            grad_query = jnp.dot(grad_score, key_head, preferred_element_type=jnp.float32) * score_scale
            grad_key = jnp.dot(grad_score.T, query_head, preferred_element_type=jnp.float32) * score_scale
            grad_value = jnp.dot(probabilities.astype(jnp.bfloat16).T, grad_head, preferred_element_type=jnp.float32)
            return (grad_query, grad_key, grad_value)
        grad_query, grad_key, grad_value = lax.map(per_head, (query_slice, key_slice, value_slice, out_slice, grad_slice, lse_slice))
        key_sum = lax.dynamic_update_slice_in_dim(running[0], slice_window(running[0], start, 3 * TOK_DEV) + jnp.transpose(grad_key, (1, 0, 2)), start, 0)
        value_sum = lax.dynamic_update_slice_in_dim(running[1], slice_window(running[1], start, 3 * TOK_DEV) + jnp.transpose(grad_value, (1, 0, 2)), start, 0)
        return ((key_sum, value_sum), jnp.transpose(grad_query, (1, 0, 2)))
    zeros_wide = jnp.zeros((row_count + 2 * TOK_DEV, head_count, head_width), jnp.float32)
    sums, grad_queries = lax.scan(per_slice, (zeros_wide, zeros_wide), jnp.arange(slice_count, dtype=jnp.int32))
    return (grad_queries.reshape(row_count, head_count, head_width), sums[0][TOK_DEV:TOK_DEV + row_count], sums[1][TOK_DEV:TOK_DEV + row_count])

def reference(tokens, image_ids, cotangent, ln1_gain, ln1_bias, qkv_weight, qv_bias, proj_weight, proj_bias, scale_attn, ln2_gain, ln2_bias, fc1_weight, fc1_bias, fc2_weight, fc2_bias, scale_mlp):
    row_count = tokens.shape[0]
    stream = tokens.astype(jnp.float32)
    records = []
    for level_index in range(LAYERS):
        normed1, hat1, spread1 = norm_forward(stream, ln1_gain[level_index], ln1_bias[level_index])
        first_in = normed1.astype(jnp.bfloat16)
        projected = jnp.dot(first_in, qkv_weight[level_index].reshape(D, 3 * D), preferred_element_type=jnp.float32).reshape(row_count, 3, D)
        queries = (projected[:, 0] + qv_bias[level_index, 0]).astype(jnp.bfloat16).reshape(row_count, HEADS, HD)
        keys = projected[:, 1].astype(jnp.bfloat16).reshape(row_count, HEADS, HD)
        values = (projected[:, 2] + qv_bias[level_index, 1]).astype(jnp.bfloat16).reshape(row_count, HEADS, HD)
        attended, logsums = attention_forward(queries, keys, values, image_ids)
        attended_flat = attended.reshape(row_count, D)
        mixed1 = jnp.dot(attended_flat, proj_weight[level_index], preferred_element_type=jnp.float32)
        middle = stream + scale_attn[level_index] * (mixed1 + proj_bias[level_index])
        normed2, hat2, spread2 = norm_forward(middle, ln2_gain[level_index], ln2_bias[level_index])
        second_in = normed2.astype(jnp.bfloat16)
        before = jnp.dot(second_in, fc1_weight[level_index], preferred_element_type=jnp.float32) + fc1_bias[level_index]
        activated, slopes = gelu_pair(before)
        activated = activated.astype(jnp.bfloat16)
        mixed2 = jnp.dot(activated, fc2_weight[level_index], preferred_element_type=jnp.float32)
        records.append((hat1, spread1, first_in, queries, keys, values, attended, logsums, mixed1, hat2, spread2, second_in, activated, slopes, mixed2))
        stream = middle + scale_mlp[level_index] * (mixed2 + fc2_bias[level_index])
    output = stream
    upstream = cotangent.astype(jnp.float32)
    gradients = [None] * LAYERS
    for level_index in reversed(range(LAYERS)):
        hat1, spread1, first_in, queries, keys, values, attended, logsums, mixed1, hat2, spread2, second_in, activated, slopes, mixed2 = records[level_index]
        grad_scale_mlp = lax.optimization_barrier(jnp.sum(upstream * (mixed2 + fc2_bias[level_index]), axis=0))
        grad_fc2_bias = lax.optimization_barrier(jnp.sum(upstream * scale_mlp[level_index], axis=0))
        grad_branch2 = (upstream * scale_mlp[level_index]).astype(jnp.bfloat16)
        grad_fc2 = jnp.dot(activated.T, grad_branch2, preferred_element_type=jnp.float32)
        grad_activated = jnp.dot(grad_branch2, fc2_weight[level_index].T, preferred_element_type=jnp.float32)
        grad_before = grad_activated * slopes
        grad_fc1_bias = lax.optimization_barrier(jnp.sum(grad_before, axis=0))
        grad_before_narrow = grad_before.astype(jnp.bfloat16)
        grad_fc1 = jnp.dot(second_in.T, grad_before_narrow, preferred_element_type=jnp.float32)
        grad_normed2 = jnp.dot(grad_before_narrow, fc1_weight[level_index].T, preferred_element_type=jnp.float32)
        back2, grad_ln2_gain, grad_ln2_bias = norm_backward(grad_normed2, hat2, spread2, ln2_gain[level_index])
        grad_middle = upstream + back2
        grad_scale_attn = lax.optimization_barrier(jnp.sum(grad_middle * (mixed1 + proj_bias[level_index]), axis=0))
        grad_proj_bias = lax.optimization_barrier(jnp.sum(grad_middle * scale_attn[level_index], axis=0))
        grad_branch1 = (grad_middle * scale_attn[level_index]).astype(jnp.bfloat16)
        attended_flat = attended.reshape(row_count, D)
        grad_proj = jnp.dot(attended_flat.T, grad_branch1, preferred_element_type=jnp.float32)
        grad_heads = jnp.dot(grad_branch1, proj_weight[level_index].T, preferred_element_type=jnp.float32).astype(jnp.bfloat16)
        grad_queries, grad_keys, grad_values = attention_backward(queries, keys, values, image_ids, attended, grad_heads.reshape(row_count, HEADS, HD), logsums)
        grad_queries = grad_queries.reshape(row_count, D)
        grad_keys = grad_keys.reshape(row_count, D)
        grad_values = grad_values.reshape(row_count, D)
        grad_qv = jnp.stack([lax.optimization_barrier(jnp.sum(grad_queries, axis=0)), lax.optimization_barrier(jnp.sum(grad_values, axis=0))])
        grad_all = jnp.stack([grad_queries, grad_keys, grad_values], axis=1).astype(jnp.bfloat16)
        grad_qkv = jnp.dot(first_in.T, grad_all.reshape(row_count, 3 * D), preferred_element_type=jnp.float32).reshape(D, 3, D)
        grad_normed1 = jnp.dot(grad_all.reshape(row_count, 3 * D), qkv_weight[level_index].reshape(D, 3 * D).T, preferred_element_type=jnp.float32)
        back1, grad_ln1_gain, grad_ln1_bias = norm_backward(grad_normed1, hat1, spread1, ln1_gain[level_index])
        upstream = grad_middle + back1
        gradients[level_index] = (grad_ln1_gain, grad_ln1_bias, grad_qkv, grad_qv, grad_proj, grad_proj_bias, grad_scale_attn, grad_ln2_gain, grad_ln2_bias, grad_fc1, grad_fc1_bias, grad_fc2, grad_fc2_bias, grad_scale_mlp)
    stacks = [jnp.stack([gradients[level_index][member] for level_index in range(LAYERS)]) for member in range(14)]
    return (output, upstream, stacks[0], stacks[1], stacks[2], stacks[3], stacks[4], stacks[5], stacks[6], stacks[7], stacks[8], stacks[9], stacks[10], stacks[11], stacks[12], stacks[13])
```

```python
import functools
import jax
import jax.numpy as jnp
from jax import lax
from jax.experimental import pallas as pl
from jax.experimental.pallas import tpu as pltpu
from jax.sharding import PartitionSpec as P

HD = 64
LAYERS = 2
D = 1024
MESH = pl.DeviceIdType.MESH
F32 = jnp.float32
BF16 = jnp.bfloat16
eps = 1e-06
half_root = 0.7071067811865476
density_scale = 0.3989422804014327
BIG = 1e30
Q_BLOCK = 512
K_BLOCK = 512
VMEM_LIMIT = 60 * 2**20


def bit_of(index, k):
    return (index // (1 << k)) % 2


def order_bits(nbits, half):
    return tuple(range(nbits)) if half == 0 else tuple(reversed(range(nbits)))


def compose(free_bits, free_value, fixed):
    index = sum(value * (1 << k) for k, value in fixed.items())
    for place, k in enumerate(free_bits):
        index = index + ((free_value >> place) & 1) * (1 << k)
    return index


class Exchange:
    def __init__(self, n, chunks, sub):
        self.n, self.chunks, self.sub = n, chunks, sub
        self.nbits = n.bit_length() - 1
        self.half = sub // 2
        self.me = lax.axis_index("tensor")
        self.bits = [bit_of(self.me, k) for k in range(self.nbits)]
        self.pending = []

    def partner(self, k):
        return self.me + (1 - 2 * self.bits[k]) * (1 << k)

    def barrier(self):
        sem = pltpu.get_barrier_semaphore()
        for k in range(self.nbits):
            pl.semaphore_signal(
                sem, inc=1, device_id={"tensor": self.partner(k)}, device_id_type=MESH
            )
        pl.semaphore_wait(sem, self.nbits)

    def rows(self, h):
        return pl.ds(h * self.half, self.half)

    def copy(self, src, dst, sems, c, h, message, k):
        return pltpu.make_async_remote_copy(
            src_ref=src,
            dst_ref=dst,
            send_sem=sems.at[0, c, h, message],
            recv_sem=sems.at[1, c, h, message],
            device_id={"tensor": self.partner(k)},
            device_id_type=MESH,
        )

    def rs_base(self, p):
        return sum(self.n >> (q + 1) for q in range(p))

    def rs_fixed(self, order, p, flip):
        fixed = {k: self.bits[k] for k in order[:p]}
        fixed[order[p]] = 1 - self.bits[order[p]] if flip else self.bits[order[p]]
        return fixed

    def rs_places(self, order, p, f):
        places = []
        for q in range(p):
            free = order[q + 1 :]
            index = 0
            for place, k in enumerate(free):
                at = order.index(k)
                if at < p:
                    value = self.bits[k]
                elif at == p:
                    value = 1 - self.bits[k]
                else:
                    value = (f >> (at - p - 1)) & 1
                index = index + value * (1 << place)
            places.append(self.rs_base(q) + index)
        return places

    def rs_send(self, part, recv, sems, c, p):
        for h in range(2):
            order = order_bits(self.nbits, h)
            free = order[p + 1 :]
            for f in range(1 << len(free)):
                b = compose(free, f, self.rs_fixed(order, p, True))
                message = self.rs_base(p) + f
                if p > 0:
                    total = part[b, c, self.rows(h), :].astype(F32)
                    for place in self.rs_places(order, p, f):
                        total = total + recv[c, place, self.rows(h), :].astype(F32)
                    part[b, c, self.rows(h), :] = total.astype(BF16)
                cp = self.copy(
                    part.at[b, c, self.rows(h), :],
                    recv.at[c, message, self.rows(h), :],
                    sems,
                    c,
                    h,
                    message,
                    order[p],
                )
                cp.start()
                self.pending.append(cp)

    def rs_wait(self, part, recv, sems, c, p):
        for h in range(2):
            order = order_bits(self.nbits, h)
            for f in range(self.n >> (p + 1)):
                message = self.rs_base(p) + f
                self.copy(
                    part.at[0, c, self.rows(h), :],
                    recv.at[c, message, self.rows(h), :],
                    sems,
                    c,
                    h,
                    message,
                    order[p],
                ).wait_recv()

    def rs_total(self, part, recv, c):
        halves = []
        for h in range(2):
            order = order_bits(self.nbits, h)
            total = part[self.me, c, self.rows(h), :].astype(F32)
            for p in range(self.nbits):
                free = order[p + 1 :]
                place = self.rs_base(p) + sum(
                    self.bits[k] * (1 << at) for at, k in enumerate(free)
                )
                total = total + recv[c, place, self.rows(h), :].astype(F32)
            halves.append(total)
        return jnp.concatenate(halves, axis=0)

    def ag_send(self, full, sems, c, p):
        for h in range(2):
            order = order_bits(self.nbits, h)
            fixed = {k: self.bits[k] for k in order[p:]}
            for f in range(1 << p):
                b = compose(order[:p], f, fixed)
                message = (1 << p) - 1 + f
                ref = full.at[b, c, self.rows(h), :]
                cp = self.copy(ref, ref, sems, c, h, message, order[p])
                cp.start()
                self.pending.append(cp)

    def ag_wait(self, full, sems, c, p):
        for h in range(2):
            order = order_bits(self.nbits, h)
            fixed = {k: self.bits[k] for k in order[p + 1 :]}
            fixed[order[p]] = 1 - self.bits[order[p]]
            for f in range(1 << p):
                b = compose(order[:p], f, fixed)
                message = (1 << p) - 1 + f
                ref = full.at[b, c, self.rows(h), :]
                self.copy(ref, ref, sems, c, h, message, order[p]).wait_recv()

    def drain(self):
        for cp in self.pending:
            cp.wait_send()
        self.pending = []


def erf(x):
    c = jnp.clip(x, -3.832506856900711, 3.832506856900711)
    s = c * c
    top = jnp.full_like(s, 0.00022905065861350646)
    for k in (0.0034082910107109506, 0.050955695062380861, 0.18520832239976145, 1.128379143519084):
        top = top * s + k
    low = jnp.full_like(s, -1.1791602954361697e-7)
    for k in (
        0.000023547966471313185,
        0.0010179625278914885,
        0.014070470171167667,
        0.11098505178285362,
        0.49746925110067538,
        1.0,
    ):
        low = low * s + k
    return c * top / low


def gelu_pair(before):
    cumulative = 0.5 * (1.0 + erf(before * half_root))
    density = jnp.exp(-0.5 * before * before) * density_scale
    return before * cumulative, cumulative + before * density


def normalised(stream):
    centre = jnp.mean(stream, axis=-1, keepdims=True)
    centred = stream - centre
    spread = lax.rsqrt(jnp.mean(centred * centred, axis=-1, keepdims=True) + eps)
    return centred * spread, spread


def norm_back(upstream, normed, spread, gain_row):
    scaled = upstream * gain_row
    return spread * (
        scaled
        - jnp.mean(scaled, axis=-1, keepdims=True)
        - normed * jnp.mean(scaled * normed, axis=-1, keepdims=True)
    )


def chunk_of(ref, c):
    x = ref[:, c]
    return x.reshape(x.shape[0] * x.shape[1], x.shape[2])


def column_loop(width, step, fn):
    if width <= step:
        fn(pl.ds(0, width))
    else:

        def one(j, carry):
            fn(pl.ds(pl.multiple_of(j * step, step), step))
            return carry

        lax.fori_loop(0, width // step, one, 0)


def matmul_nn(x, w_ref, cols):
    return jnp.dot(x, w_ref[:, cols], preferred_element_type=F32)


def matmul_nt(x, w_ref, cols):
    return lax.dot_general(
        x, w_ref[cols, :], (((1,), (1,)), ((), ())), preferred_element_type=F32
    )


def run_stages(ex, stages):
    for stage in stages:
        for c in range(ex.chunks):
            stage(c)


def rs_stages(ex, part, recv, sems):
    stages = []
    for p in range(1, ex.nbits):

        def stage(c, p=p):
            ex.rs_wait(part, recv, sems, c, p - 1)
            ex.rs_send(part, recv, sems, c, p)

        stages.append(stage)
    return stages


def ag_stages(ex, full, sems):
    stages = []
    for p in range(1, ex.nbits):

        def stage(c, p=p):
            ex.ag_wait(full, sems, c, p - 1)
            ex.ag_send(full, sems, c, p)

        stages.append(stage)
    return stages


def own_rows(ref, c):
    return ref[c]


def forward_kernel(
    n, chunks, sub, last,
    attended, proj, fc1, fc2, fc1_bias, vec, stream, *rest,
):
    if last:
        (u1_o, hat2_o, sp2_o, u2_o, a2_o, act_o, slope_o, out_o,
         part1, recv1, part2, recv2, full2, sems) = rest
    else:
        (qkv, qv_bias, u1_o, hat2_o, sp2_o, u2_o, a2_o, act_o, slope_o, stream_o, hat1_o, sp1_o, a1_o, q_o, k_o, v_o,
         part1, recv1, part2, recv2, sems) = rest
        full2 = a1_o
    ex = Exchange(n, chunks, sub)
    ex.barrier()
    row = lambda i: vec[i : i + 1, :]

    def pre(c):
        def cols(j):
            y = matmul_nn(chunk_of(attended, c), proj, j)
            part1[:, c, :, j] = y.astype(BF16).reshape(n, sub, -1)

        column_loop(D, 256, cols)
        ex.rs_send(part1, recv1, sems.at[0], c, 0)

    def own1(c):
        ex.rs_wait(part1, recv1, sems.at[0], c, ex.nbits - 1)
        u1 = ex.rs_total(part1, recv1, c) + row(0)
        u1_o[c] = u1
        middle = stream[c] + row(1) * u1
        hat, spread = normalised(middle)
        hat2_o[c] = hat
        sp2_o[c] = spread
        a2_o[ex.me, c] = (hat * row(2) + row(3)).astype(BF16)
        ex.ag_send(a2_o, sems.at[1], c, 0)

    def mid(c):
        ex.ag_wait(a2_o, sems.at[1], c, ex.nbits - 1)

        def hidden(j):
            before = matmul_nn(chunk_of(a2_o, c), fc1, j) + fc1_bias[:, j]
            a, s = gelu_pair(before)
            act_o[:, c, :, j] = a.astype(BF16).reshape(n, sub, -1)
            slope_o[:, c, :, j] = s.astype(BF16).reshape(n, sub, -1)

        column_loop(fc1.shape[1], 256, hidden)

        def cols(j):
            y = matmul_nn(chunk_of(act_o, c), fc2, j)
            part2[:, c, :, j] = y.astype(BF16).reshape(n, sub, -1)

        column_loop(D, 256, cols)
        ex.rs_send(part2, recv2, sems.at[2], c, 0)

    def own2(c):
        ex.rs_wait(part2, recv2, sems.at[2], c, ex.nbits - 1)
        u2 = ex.rs_total(part2, recv2, c) + row(4)
        u2_o[c] = u2
        middle = stream[c] + row(1) * u1_o[c]
        after = middle + row(5) * u2
        if last:
            full2[ex.me, c] = after.astype(BF16)
        else:
            stream_o[c] = after
            hat, spread = normalised(after)
            hat1_o[c] = hat
            sp1_o[c] = spread
            full2[ex.me, c] = (hat * row(6) + row(7)).astype(BF16)
        ex.ag_send(full2, sems.at[3], c, 0)

    def post(c):
        ex.ag_wait(full2, sems.at[3], c, ex.nbits - 1)
        if last:
            for b in range(n):
                out_o[b, c] = full2[b, c].astype(F32)
            return
        x = chunk_of(full2, c)
        width = q_o.shape[3]
        for i, ref in enumerate((q_o, k_o, v_o)):
            y = matmul_nn(x, qkv, slice(i * width, (i + 1) * width))
            if i != 1:
                y = y + qv_bias[i // 2 : i // 2 + 1, :]
            ref[:, c] = y.astype(BF16).reshape(n, sub, width)

    run_stages(
        ex,
        [pre]
        + rs_stages(ex, part1, recv1, sems.at[0])
        + [own1]
        + ag_stages(ex, a2_o, sems.at[1])
        + [mid]
        + rs_stages(ex, part2, recv2, sems.at[2])
        + [own2]
        + ag_stages(ex, full2, sems.at[3])
        + [post],
    )
    ex.drain()


def sizes(rows, n):
    block = rows // n
    chunks = 3 if block % 96 == 0 else (2 if block % 64 == 0 else 1)
    return block, chunks, block // chunks


def vmem():
    return pl.BlockSpec(memory_space=pltpu.VMEM)


def call(kernel, name, collective_id, outs, scratch, args, flops):
    return pl.pallas_call(
        kernel,
        out_shape=[jax.ShapeDtypeStruct(s, d) for s, d in outs],
        in_specs=[vmem()] * len(args),
        out_specs=[vmem()] * len(outs),
        scratch_shapes=scratch,
        compiler_params=pltpu.CompilerParams(
            collective_id=collective_id, has_side_effects=True, vmem_limit_bytes=VMEM_LIMIT
        ),
        cost_estimate=pl.CostEstimate(flops=flops, bytes_accessed=10**8, transcendentals=0),
        name=name,
    )(*args)


def comm_scratch(n, chunks, sub):
    return [
        pltpu.VMEM((n, chunks, sub, D), BF16),
        pltpu.VMEM((chunks, n - 1, sub, D), BF16),
    ]


def sem_scratch(stages, n, chunks):
    return [pltpu.SemaphoreType.DMA((stages, 2, chunks, 2, n - 1))]


def forward_block(n, last, collective_id, attended, proj, fc1, fc2, fc1_bias, vec, stream, qkv=None, qv_bias=None):
    rows, width = attended.shape
    block, chunks, sub = sizes(rows, n)
    hidden = fc1.shape[1]
    split = lambda cols: (n, chunks, sub, cols)
    mine = (chunks, sub, D)
    args = [attended.reshape(split(width)), proj, fc1, fc2, fc1_bias, vec, stream.reshape(mine)]
    outs = [
        (mine, F32), (mine, F32), ((chunks, sub, 1), F32), (mine, F32),
        (split(D), BF16), (split(hidden), BF16), (split(hidden), BF16),
    ]
    scratch = comm_scratch(n, chunks, sub) + comm_scratch(n, chunks, sub)
    if last:
        outs += [(split(D), F32)]
        scratch += [pltpu.VMEM(split(D), BF16)]
    else:
        args += [qkv, qv_bias]
        outs += [(mine, F32), (mine, F32), ((chunks, sub, 1), F32), (split(D), BF16)] + [(split(width), BF16)] * 3
    return call(
        functools.partial(forward_kernel, n, chunks, sub, last),
        "forward_last" if last else "forward_block",
        collective_id,
        outs,
        scratch + sem_scratch(4, n, chunks),
        args,
        2 * rows * D * (2 * hidden + 4 * width),
    )


def add_rows(ref, i, value):
    ref[i : i + 1, :] += jnp.sum(value, axis=0, keepdims=True)


def input_norm_own(ex, part, recv, sems, c, hat, spread, gain, gm, sums, at):
    ex.rs_wait(part, recv, sems, c, ex.nbits - 1)
    da1 = ex.rs_total(part, recv, c)
    add_rows(sums, at, da1 * hat[c])
    add_rows(sums, at + 1, da1)
    return gm[c] + norm_back(da1, hat[c], spread[c], gain)


def input_grad_chunk(ex, dqkv, qkv, part, c):
    def cols(j):
        y = matmul_nt(chunk_of(dqkv, c), qkv, j)
        part[:, c, :, j] = y.astype(BF16).reshape(ex.n, ex.sub, -1)

    column_loop(D, 256, cols)


def backward_kernel(n, chunks, sub, first, *refs):
    if first:
        (cot, e2_in, fc1, fc2, proj, vec, slope, u1, hat2, sp2, u2,
         dbn_o, e1_o, datt_o, gm_o, sums_o, fc1b_o, part2, recv2, sems) = refs
        full = e2_in
    else:
        (dqkv, qkv, hat1, sp1, gm_in, fc1, fc2, proj, vec, slope, u1, hat2, sp2, u2,
         e2_o, dbn_o, e1_o, datt_o, gm_o, sums_o, fc1b_o, part1, recv1, part2, recv2, sems) = refs
        full = e2_o
    ex = Exchange(n, chunks, sub)
    ex.barrier()
    row = lambda i: vec[i : i + 1, :]
    sums_o[...] = jnp.zeros_like(sums_o)
    fc1b_o[...] = jnp.zeros_like(fc1b_o)

    def pre(c):
        input_grad_chunk(ex, dqkv, qkv, part1, c)
        ex.rs_send(part1, recv1, sems.at[0], c, 0)

    def own0(c):
        g = input_norm_own(ex, part1, recv1, sems.at[0], c, hat1, sp1, row(3), gm_in, sums_o, 6)
        add_rows(sums_o, 0, g * u2[c])
        add_rows(sums_o, 1, g * row(0))
        gm_o[c] = g
        full[ex.me, c] = (g * row(0)).astype(BF16)
        ex.ag_send(full, sems.at[1], c, 0)

    def mid(c):
        if first:
            g = cot[c].astype(F32)
            add_rows(sums_o, 0, g * u2[c])
            add_rows(sums_o, 1, g * row(0))
            gm_o[c] = g
        else:
            ex.ag_wait(full, sems.at[1], c, ex.nbits - 1)

        def hidden(j):
            y = matmul_nt(chunk_of(full, c), fc2, j)
            w = y.shape[1]
            db = y * slope[:, c, :, j].astype(F32).reshape(n * sub, w)
            fc1b_o[:, j] += jnp.sum(db, axis=0, keepdims=True)
            dbn_o[:, c, :, j] = db.astype(BF16).reshape(n, sub, w)

        column_loop(fc1.shape[1], 256, hidden)

        def cols(j):
            y = matmul_nt(chunk_of(dbn_o, c), fc1, j)
            part2[:, c, :, j] = y.astype(BF16).reshape(n, sub, -1)

        column_loop(D, 256, cols)
        ex.rs_send(part2, recv2, sems.at[2], c, 0)

    def own1(c):
        ex.rs_wait(part2, recv2, sems.at[2], c, ex.nbits - 1)
        da2 = ex.rs_total(part2, recv2, c)
        hat = hat2[c]
        add_rows(sums_o, 2, da2 * hat)
        add_rows(sums_o, 3, da2)
        gm = gm_o[c] + norm_back(da2, hat, sp2[c], row(1))
        gm_o[c] = gm
        add_rows(sums_o, 4, gm * u1[c])
        add_rows(sums_o, 5, gm * row(2))
        e1_o[ex.me, c] = (gm * row(2)).astype(BF16)
        ex.ag_send(e1_o, sems.at[3], c, 0)

    def post(c):
        ex.ag_wait(e1_o, sems.at[3], c, ex.nbits - 1)
        y = matmul_nt(chunk_of(e1_o, c), proj, slice(None))
        datt_o[:, c] = y.astype(BF16).reshape(n, sub, -1)

    head = [] if first else (
        [pre] + rs_stages(ex, part1, recv1, sems.at[0]) + [own0] + ag_stages(ex, full, sems.at[1])
    )
    run_stages(
        ex,
        head
        + [mid]
        + rs_stages(ex, part2, recv2, sems.at[2])
        + [own1]
        + ag_stages(ex, e1_o, sems.at[3])
        + [post],
    )
    ex.drain()


def backward_block(n, collective_id, source, fc1, fc2, proj, vec, slope, u1, hat2, sp2, u2):
    first = len(source) == 2
    _, chunks, sub, hidden = slope.shape
    width = proj.shape[0]
    split = lambda cols: (n, chunks, sub, cols)
    mine = (chunks, sub, D)
    outs = [] if first else [(split(D), BF16)]
    outs += [
        (split(hidden), BF16), (split(D), BF16), (split(width), BF16), (mine, F32),
        ((8, D), F32), ((1, hidden), F32),
    ]
    scratch = [] if first else comm_scratch(n, chunks, sub)
    scratch += comm_scratch(n, chunks, sub) + sem_scratch(4, n, chunks)
    return call(
        functools.partial(backward_kernel, n, chunks, sub, first),
        "backward_first" if first else "backward_block",
        collective_id,
        outs,
        scratch,
        list(source) + [fc1, fc2, proj, vec, slope, u1, hat2, sp2, u2],
        2 * n * chunks * sub * D * (2 * hidden + 4 * width),
    )


def tail_kernel(n, chunks, sub, dqkv, qkv, hat1, sp1, gm_in, vec, out_o, sums_o, part1, recv1, full, sems):
    ex = Exchange(n, chunks, sub)
    ex.barrier()
    sums_o[...] = jnp.zeros_like(sums_o)

    def pre(c):
        input_grad_chunk(ex, dqkv, qkv, part1, c)
        ex.rs_send(part1, recv1, sems.at[0], c, 0)

    def own(c):
        g = input_norm_own(ex, part1, recv1, sems.at[0], c, hat1, sp1, vec[3:4, :], gm_in, sums_o, 6)
        full[ex.me, c] = g.astype(BF16)
        ex.ag_send(full, sems.at[1], c, 0)

    def post(c):
        ex.ag_wait(full, sems.at[1], c, ex.nbits - 1)
        for b in range(n):
            out_o[b, c] = full[b, c].astype(F32)

    run_stages(
        ex,
        [pre]
        + rs_stages(ex, part1, recv1, sems.at[0])
        + [own]
        + ag_stages(ex, full, sems.at[1])
        + [post],
    )
    ex.drain()


def backward_tail(n, collective_id, dqkv, qkv, hat1, sp1, gm, vec):
    _, chunks, sub, width = dqkv.shape
    split = lambda cols: (n, chunks, sub, cols)
    return call(
        functools.partial(tail_kernel, n, chunks, sub),
        "backward_tail",
        collective_id,
        [(split(D), F32), ((8, D), F32)],
        comm_scratch(n, chunks, sub) + [pltpu.VMEM(split(D), BF16)] + sem_scratch(2, n, chunks),
        [dqkv, qkv, hat1, sp1, gm, vec],
        2 * n * chunks * sub * D * width,
    )


def id_features(ids_col, query_side):
    lane = lax.broadcasted_iota(jnp.int32, (ids_col.shape[0], HD), 1)
    bit = (ids_col >> (lane & 15)) & 1
    first = lane < 16
    second = (lane >= 16) & (lane < 32)
    inv = 1 - bit
    if query_side:
        v = jnp.where(first, bit, jnp.where(second, inv, 0)).astype(F32) * (-BIG)
    else:
        v = jnp.where(first, inv, jnp.where(second, bit, 0)).astype(F32)
    return v

def fwd_kernel(QB, KB, nq, lo_ref, hi_ref, q_ref, k_ref, v_ref, idq_ref, idk_ref, o_ref, lse_ref, kaug, vt, qaug):
    nk = k_ref.shape[0] // KB
    t_lo = lo_ref[0]
    t_hi = hi_ref[nq - 1]
    def prep(t, _):
        r = pl.ds(pl.multiple_of(t * KB, KB), KB)
        feat = id_features(idk_ref[r, :], False).astype(BF16)
        kk = k_ref[r, :]
        kaug[0, r, :] = jnp.concatenate([kk[:, :HD], feat], axis=1)
        kaug[1, r, :] = jnp.concatenate([kk[:, HD:], feat], axis=1)
        vt[:, r] = v_ref[r, :].T
        return 0
    lax.fori_loop(t_lo, t_hi, prep, 0)
    def qprep(t, _):
        r = pl.ds(pl.multiple_of(t * QB, QB), QB)
        feat = id_features(idq_ref[r, :], True).astype(BF16)
        qq = (q_ref[r, :] * BF16(0.125))
        qaug[0, :, r] = jnp.concatenate([qq[:, :HD], feat], axis=1).T
        qaug[1, :, r] = jnp.concatenate([qq[:, HD:], feat], axis=1).T
        return 0
    lax.fori_loop(0, nq, qprep, 0)
    def qloop(qb, _):
        rq = pl.ds(pl.multiple_of(qb * QB, QB), QB)
        outs = []
        qts = [qaug[h, :, rq] for h in range(2)]
        def kloop(t, c):
            r = pl.ds(pl.multiple_of(t * KB, KB), KB)
            new = []
            for h in range(2):
                m, l, acc = c[h]
                s = jnp.dot(kaug[h, r, :], qts[h], preferred_element_type=F32)
                mn = jnp.maximum(m, jnp.max(s, axis=0, keepdims=True))
                p = jnp.exp(s - mn)
                al = jnp.exp(m - mn)
                l = l * al + jnp.sum(p, axis=0, keepdims=True)
                acc = acc * al + jnp.dot(vt[h * HD:(h + 1) * HD, r], p.astype(BF16), preferred_element_type=F32)
                new.append((mn, l, acc))
            return tuple(new)
        z = (jnp.full((1, QB), -3e38, F32), jnp.zeros((1, QB), F32), jnp.zeros((HD, QB), F32))
        c = lax.fori_loop(lo_ref[qb], hi_ref[qb], kloop, (z, z))
        both = jnp.concatenate([c[h][2] / c[h][1] for h in range(2)], axis=0)
        o_ref[rq, :] = both.T.astype(BF16)
        for h in range(2):
            lse_ref[0, h:h + 1, rq] = c[h][0] + jnp.log(c[h][1])
        return 0
    lax.fori_loop(0, nq, qloop, 0)

def attend_fwd(q, kwin, vwin, idq, idk, lo, hi, QB, KB):
    n, cols = q.shape
    w = kwin.shape[0]
    pairs = cols // 128
    nq = n // QB
    return pl.pallas_call(
        functools.partial(fwd_kernel, QB, KB, nq),
        grid_spec=pltpu.PrefetchScalarGridSpec(
            num_scalar_prefetch=2, grid=(pairs,),
            in_specs=[pl.BlockSpec((n, 128), lambda g, *_: (0, g)), pl.BlockSpec((w, 128), lambda g, *_: (0, g)), pl.BlockSpec((w, 128), lambda g, *_: (0, g)),
                      pl.BlockSpec((n, 1), lambda g, *_: (0, 0)), pl.BlockSpec((w, 1), lambda g, *_: (0, 0))],
            out_specs=[pl.BlockSpec((n, 128), lambda g, *_: (0, g)), pl.BlockSpec((1, 2, n), lambda g, *_: (g, 0, 0))],
            scratch_shapes=[pltpu.VMEM((2, w, 128), BF16), pltpu.VMEM((128, w), BF16), pltpu.VMEM((2, 128, n), BF16)]),
        out_shape=[jax.ShapeDtypeStruct((n, cols), BF16), jax.ShapeDtypeStruct((pairs, 2, n), F32)],
        compiler_params=pltpu.CompilerParams(vmem_limit_bytes=VMEM_LIMIT),
        name="attend_fwd",
    )(lo, hi, q, kwin, vwin, idq, idk)

def bwd_kernel(QB, KB, nq, lo_ref, hi_ref, q_ref, k_ref, v_ref, idq_ref, idk_ref, o_ref, g_ref, lse_ref, dq_ref, dk_ref, dv_ref, kaug, vaug, kt, qaug, gaug, acc):
    w = k_ref.shape[0]
    t_lo = lo_ref[0]
    t_hi = hi_ref[nq - 1]
    lane = lax.broadcasted_iota(jnp.int32, (KB, HD), 1)
    three = ((lane >= 32) & (lane < 35))
    def zero(t, _):
        r = pl.ds(pl.multiple_of(t * KB, KB), KB)
        dk_ref[r, :] = jnp.zeros((KB, 128), BF16)
        dv_ref[r, :] = jnp.zeros((KB, 128), BF16)
        return 0
    lax.fori_loop(0, w // KB, zero, 0)
    def prep(t, _):
        r = pl.ds(pl.multiple_of(t * KB, KB), KB)
        feat = jnp.where(three, 1.0, id_features(idk_ref[r, :], False)).astype(BF16)
        ones = jnp.where(three, 1.0, 0.0).astype(BF16)
        kk = k_ref[r, :]
        vv = v_ref[r, :]
        for h in range(2):
            kaug[h, r, :] = jnp.concatenate([kk[:, h * HD:(h + 1) * HD], feat], axis=1)
            vaug[h, r, :] = jnp.concatenate([vv[:, h * HD:(h + 1) * HD], ones], axis=1)
            acc[h, r, :] = jnp.zeros((KB, 128), F32)
        kt[:, r] = kk.T
        return 0
    lax.fori_loop(t_lo, t_hi, prep, 0)
    def pieces(x):
        a = x.astype(BF16).astype(F32)
        b = (x - a).astype(BF16).astype(F32)
        return a, b, x - a - b
    def qprep(t, _):
        r = pl.ds(pl.multiple_of(t * QB, QB), QB)
        fid = id_features(idq_ref[r, :], True).T
        row = lax.broadcasted_iota(jnp.int32, (HD, QB), 0)
        qt = (q_ref[r, :] * BF16(0.125)).T
        gg = g_ref[r, :]
        gt = gg.T
        prod = (gg.astype(F32) * o_ref[r, :].astype(F32)).T
        for h in range(2):
            a, b, c = pieces(-lse_ref[0, h:h + 1, r])
            f = jnp.where(row == 32, a, jnp.where(row == 33, b, jnp.where(row == 34, c, fid)))
            qaug[h, :, r] = jnp.concatenate([qt[h * HD:(h + 1) * HD, :], f.astype(BF16)], axis=0)
            d = -jnp.sum(prod[h * HD:(h + 1) * HD, :], axis=0, keepdims=True)
            a, b, c = pieces(d)
            f = jnp.where(row == 32, a, jnp.where(row == 33, b, jnp.where(row == 34, c, 0.0)))
            gaug[h, :, r] = jnp.concatenate([gt[h * HD:(h + 1) * HD, :], f.astype(BF16)], axis=0)
        return 0
    lax.fori_loop(0, nq, qprep, 0)
    def qloop(qb, _):
        rq = pl.ds(pl.multiple_of(qb * QB, QB), QB)
        qq = q_ref[rq, :] * BF16(0.125)
        gg = g_ref[rq, :]
        zz = jnp.zeros((QB, HD), BF16)
        qts = [qaug[h, :, rq] for h in range(2)]
        gts = [gaug[h, :, rq] for h in range(2)]
        rhs = [jnp.concatenate([jnp.concatenate([qq[:, h * HD:(h + 1) * HD], zz], axis=1), jnp.concatenate([zz, gg[:, h * HD:(h + 1) * HD]], axis=1)], axis=0) for h in range(2)]
        def kloop(t, c):
            r = pl.ds(pl.multiple_of(t * KB, KB), KB)
            new = []
            for h in range(2):
                s = jnp.dot(kaug[h, r, :], qts[h], preferred_element_type=F32)
                dp = jnp.dot(vaug[h, r, :], gts[h], preferred_element_type=F32)
                p = jnp.exp(s)
                ds = (p * dp).astype(BF16)
                both = jnp.concatenate([ds, p.astype(BF16)], axis=1)
                acc[h, r, :] += jnp.dot(both, rhs[h], preferred_element_type=F32)
                new.append(c[h] + jnp.dot(kt[h * HD:(h + 1) * HD, r], ds, preferred_element_type=F32))
            return tuple(new)
        z = jnp.zeros((HD, QB), F32)
        c = lax.fori_loop(lo_ref[qb], hi_ref[qb], kloop, (z, z))
        dq_ref[rq, :] = (jnp.concatenate([c[0], c[1]], axis=0) * 0.125).T
        return 0
    lax.fori_loop(0, nq, qloop, 0)
    def fin(t, _):
        r = pl.ds(pl.multiple_of(t * KB, KB), KB)
        a0 = acc[0, r, :]
        a1 = acc[1, r, :]
        dk_ref[r, :] = jnp.concatenate([a0[:, :HD], a1[:, :HD]], axis=1).astype(dk_ref.dtype)
        dv_ref[r, :] = jnp.concatenate([a0[:, HD:], a1[:, HD:]], axis=1).astype(dv_ref.dtype)
        return 0
    lax.fori_loop(t_lo, t_hi, fin, 0)

def attend_bwd(q, kwin, vwin, idq, idk, lo, hi, out, grad, lse, QB, KB):
    n, cols = q.shape
    w = kwin.shape[0]
    pairs = cols // 128
    nq = n // QB
    rows = lambda m: pl.BlockSpec((m, 128), lambda g, *_: (0, g))
    return pl.pallas_call(
        functools.partial(bwd_kernel, QB, KB, nq),
        grid_spec=pltpu.PrefetchScalarGridSpec(
            num_scalar_prefetch=2, grid=(pairs,),
            in_specs=[rows(n), rows(w), rows(w), pl.BlockSpec((n, 1), lambda g, *_: (0, 0)), pl.BlockSpec((w, 1), lambda g, *_: (0, 0)), rows(n), rows(n), pl.BlockSpec((1, 2, n), lambda g, *_: (g, 0, 0))],
            out_specs=[rows(n), rows(w), rows(w)],
            scratch_shapes=[pltpu.VMEM((2, w, 128), BF16), pltpu.VMEM((2, w, 128), BF16), pltpu.VMEM((128, w), BF16), pltpu.VMEM((2, 128, n), BF16), pltpu.VMEM((2, 128, n), BF16), pltpu.VMEM((2, w, 128), F32)]),
        out_shape=[jax.ShapeDtypeStruct((n, cols), F32), jax.ShapeDtypeStruct((w, cols), BF16), jax.ShapeDtypeStruct((w, cols), BF16)],
        compiler_params=pltpu.CompilerParams(vmem_limit_bytes=VMEM_LIMIT),
        name="attend_bwd",
    )(lo, hi, q, kwin, vwin, idq, idk, out, grad, lse)

def reach(ids_win, n, QB, KB):
    w = ids_win.shape[0]
    own = ids_win[n:2 * n].reshape(n // QB, QB)
    lo = jnp.argmax(ids_win[None, :] == own[:, :1], axis=1)
    hi = w - jnp.argmax(ids_win[::-1][None, :] == own[:, -1:], axis=1)
    return (lo // KB).astype(jnp.int32), ((hi + KB - 1) // KB).astype(jnp.int32)

def neighbours(axis):
    peers = lax.axis_size(axis)
    up = [(i, i + 1) for i in range(peers - 1)]
    return up, [(j, i) for i, j in up]


def with_halo(array):
    up, down = neighbours("dp")
    return jnp.concatenate(
        [lax.ppermute(array, "dp", up), array, lax.ppermute(array, "dp", down)], axis=0
    )


def own_part(array, n):
    block, chunks, sub = sizes(array.shape[0], n)
    first = lax.axis_index("tensor") * block
    return lax.dynamic_slice_in_dim(array, first, block, 0).reshape(chunks, sub, array.shape[1])


def weight_grad(left, right):
    rows = left.shape[0] * left.shape[1] * left.shape[2]
    return lax.dot_general(
        left.reshape(rows, -1),
        right.reshape(rows, -1),
        (((0,), (0,)), ((), ())),
        preferred_element_type=F32,
    ).astype(BF16)


def body(
    tokens, image_ids, cotangent, ln1_gain, ln1_bias, qkv_weight, qv_bias, proj_weight, proj_bias, scale_attn,
    ln2_gain, ln2_bias, fc1_weight, fc1_bias, fc2_weight, fc2_bias, scale_mlp,
):
    n = lax.axis_size("tensor")
    rows = tokens.shape[0]
    width = qkv_weight.shape[3]
    _, chunks, sub = sizes(rows, n)
    split = (n, chunks, sub)
    qkv2 = qkv_weight.reshape(LAYERS, D, 3 * width)
    ids_win = with_halo(image_ids + 1)
    lo, hi = reach(ids_win, rows, Q_BLOCK, K_BLOCK)
    idq, idk = ids_win[rows : 2 * rows, None], ids_win[:, None]

    stream = tokens.astype(F32)
    hat, _ = normalised(stream)
    a1 = (hat * ln1_gain[0] + ln1_bias[0]).astype(BF16)
    first = jnp.dot(a1, qkv2[0], preferred_element_type=F32)
    q = (first[:, :width] + qv_bias[0, 0]).astype(BF16)
    k = first[:, width : 2 * width].astype(BF16)
    v = (first[:, 2 * width :] + qv_bias[0, 1]).astype(BF16)
    a1 = a1.reshape(split + (D,))
    own = own_part(tokens, n).astype(F32)
    hat1, sp1 = normalised(own)

    saved = []
    for level in range(LAYERS):
        kwin, vwin = with_halo(k), with_halo(v)
        attended, lse = attend_fwd(q, kwin, vwin, idq, idk, lo, hi, Q_BLOCK, K_BLOCK)
        last = level == LAYERS - 1
        after = 0 if last else level + 1
        vec = jnp.stack(
            [
                proj_bias[level], scale_attn[level], ln2_gain[level], ln2_bias[level], fc2_bias[level],
                scale_mlp[level], ln1_gain[after], ln1_bias[after],
            ]
        )
        extra = () if last else (qkv2[level + 1], qv_bias[level + 1])
        outs = forward_block(
            n, last, level, attended, proj_weight[level], fc1_weight[level], fc2_weight[level], fc1_bias[level][None],
            vec, own, *extra,
        )
        u1, hat2, sp2, u2, a2, act, slope = outs[:7]
        saved.append((q, kwin, vwin, attended, lse, a1, hat1, sp1, u1, hat2, sp2, u2, a2, act, slope))
        if last:
            output = outs[7].reshape(rows, D)
        else:
            own, hat1, sp1, a1, q, k, v = outs[7:]
            q, k, v = (x.reshape(rows, width) for x in (q, k, v))

    cot = cotangent.astype(F32)
    source = (own_part(cotangent, n), (cot * scale_mlp[LAYERS - 1]).astype(BF16).reshape(split + (D,)))
    weights = [None] * LAYERS
    sums = [None] * (LAYERS + 1)
    narrow = [None] * LAYERS
    up, down = neighbours("dp")
    for level in reversed(range(LAYERS)):
        q, kwin, vwin, attended, lse, a1, hat1, sp1, u1, hat2, sp2, u2, a2, act, slope = saved[level]
        above = min(level + 1, LAYERS - 1)
        vec = jnp.stack([scale_mlp[level], ln2_gain[level], scale_attn[level], ln1_gain[above]])
        outs = backward_block(
            n, LAYERS + level, source, fc1_weight[level], fc2_weight[level], proj_weight[level], vec, slope, u1, hat2,
            sp2, u2,
        )
        e2 = source[1] if level == LAYERS - 1 else outs[0]
        dbn, e1, datt, gm, vec_sums, fc1b = outs[-6:]
        sums[level + 1] = vec_sums
        datt = datt.reshape(rows, width)
        dq, dkwin, dvwin = attend_bwd(q, kwin, vwin, idq, idk, lo, hi, attended, datt, lse, Q_BLOCK, K_BLOCK)

        def home(win):
            back = lax.ppermute(win[:rows], "dp", down).astype(F32)
            on = lax.ppermute(win[2 * rows :], "dp", up).astype(F32)
            return win[rows : 2 * rows].astype(F32) + back + on

        dk, dv = home(dkwin), home(dvwin)
        qv = jnp.stack([jnp.sum(dq, axis=0), jnp.sum(dv, axis=0)])
        dqkv = jnp.concatenate([dq, dk, dv], axis=1).astype(BF16).reshape(split + (3 * width,))
        narrow[level] = (qv, fc1b[0])
        weights[level] = lax.psum(
            (
                weight_grad(a1, dqkv),
                weight_grad(attended.reshape(split + (width,)), e1),
                weight_grad(a2, dbn),
                weight_grad(act, e2),
            ),
            "dp",
        )
        source = (dqkv, qkv2[level], hat1, sp1, gm)
    vec = jnp.stack([ln1_gain[0]] * 4)
    grad_tokens, sums[0] = backward_tail(n, 2 * LAYERS, *source, vec)
    total = lax.psum(jnp.stack(sums), ("dp", "tensor"))
    qv_total, fc1b_total = lax.psum(
        (jnp.stack([narrow[i][0] for i in range(LAYERS)]), jnp.stack([narrow[i][1] for i in range(LAYERS)])), "dp"
    )
    big = [jnp.stack([weights[i][j].astype(F32) for i in range(LAYERS)]) for j in range(4)]
    upper, lower = total[1:], total[:-1]
    return (
        output,
        grad_tokens.reshape(rows, D),
        lower[:, 6],
        lower[:, 7],
        big[0].reshape(LAYERS, D, 3, width),
        qv_total,
        big[1],
        upper[:, 5],
        upper[:, 4],
        upper[:, 2],
        upper[:, 3],
        big[2],
        fc1b_total,
        big[3],
        upper[:, 1],
        upper[:, 0],
    )


def solution(mesh):
    cols, stack_rows = P(None, None, "tensor"), P(None, "tensor", None)
    qkv = P(None, None, None, "tensor")
    return jax.shard_map(
        body,
        mesh=mesh,
        in_specs=(
            P("dp", None), P("dp"), P("dp", None), P(), P(), qkv, cols, stack_rows, P(), P(), P(), P(), cols,
            P(None, "tensor"), stack_rows, P(), P(),
        ),
        out_specs=(
            P("dp", None), P("dp", None), P(), P(), qkv, cols, stack_rows, P(), P(), P(), P(), cols,
            P(None, "tensor"), stack_rows, P(), P(),
        ),
        check_vma=False,
    )
```

```python
import functools
import jax
import jax.numpy as jnp
from jax import lax
from jax.experimental import pallas as pl
from jax.experimental.pallas import tpu as pltpu
from jax.sharding import PartitionSpec as P

HD = 64
LAYERS = 2
D = 1024
MESH = pl.DeviceIdType.MESH
F32 = jnp.float32
BF16 = jnp.bfloat16
eps = 1e-06
half_root = 0.7071067811865476
density_scale = 0.3989422804014327
BIG = 1e30
TILES = (4, 512, 512, 256)
VMEM_LIMIT = 62 * 2**20


def bit_of(index, k):
    return (index // (1 << k)) % 2


def order_bits(nbits, half):
    return tuple(range(nbits)) if half == 0 else tuple(reversed(range(nbits)))


def compose(free_bits, free_value, fixed):
    index = sum(value * (1 << k) for k, value in fixed.items())
    for place, k in enumerate(free_bits):
        index = index + ((free_value >> place) & 1) * (1 << k)
    return index


class Names:
    def __getattr__(self, key):
        return key


N = Names()


class Exchange:
    def __init__(self, n, chunks, sub):
        self.n, self.chunks, self.sub = n, chunks, sub
        self.nbits = n.bit_length() - 1
        self.half = sub // 2
        self.me = lax.axis_index(N.tensor)
        self.bits = [bit_of(self.me, k) for k in range(self.nbits)]
        self.pending = []

    def partner(self, k):
        return self.me + (1 - 2 * self.bits[k]) * (1 << k)

    def partners(self):
        return [{N.tensor: self.partner(k)} for k in range(self.nbits)]

    def rows(self, h):
        return pl.ds(h * self.half, self.half)

    def copy(self, src, dst, sems, c, h, message, k):
        return pltpu.make_async_remote_copy(
            src_ref=src,
            dst_ref=dst,
            send_sem=sems.at[0, c, h, message],
            recv_sem=sems.at[1, c, h, message],
            device_id={N.tensor: self.partner(k)},
            device_id_type=MESH,
        )

    def rs_base(self, p):
        return sum(self.n >> (q + 1) for q in range(p))

    def rs_fixed(self, order, p, flip):
        fixed = {k: self.bits[k] for k in order[:p]}
        fixed[order[p]] = 1 - self.bits[order[p]] if flip else self.bits[order[p]]
        return fixed

    def rs_places(self, order, p, f):
        places = []
        for q in range(p):
            free = order[q + 1 :]
            index = 0
            for place, k in enumerate(free):
                at = order.index(k)
                if at < p:
                    value = self.bits[k]
                elif at == p:
                    value = 1 - self.bits[k]
                else:
                    value = (f >> (at - p - 1)) & 1
                index = index + value * (1 << place)
            places.append(self.rs_base(q) + index)
        return places

    def rs_send(self, part, recv, sems, c, p):
        for h in range(2):
            order = order_bits(self.nbits, h)
            free = order[p + 1 :]
            for f in range(1 << len(free)):
                b = compose(free, f, self.rs_fixed(order, p, True))
                message = self.rs_base(p) + f
                if p > 0:
                    total = part[b, c, self.rows(h), :].astype(F32)
                    for place in self.rs_places(order, p, f):
                        total = total + recv[c, place, self.rows(h), :].astype(F32)
                    part[b, c, self.rows(h), :] = total.astype(BF16)
                cp = self.copy(
                    part.at[b, c, self.rows(h), :],
                    recv.at[c, message, self.rows(h), :],
                    sems,
                    c,
                    h,
                    message,
                    order[p],
                )
                cp.start()
                self.pending.append(cp)

    def rs_wait(self, part, recv, sems, c, p):
        for h in range(2):
            order = order_bits(self.nbits, h)
            for f in range(self.n >> (p + 1)):
                message = self.rs_base(p) + f
                self.copy(
                    part.at[0, c, self.rows(h), :],
                    recv.at[c, message, self.rows(h), :],
                    sems,
                    c,
                    h,
                    message,
                    order[p],
                ).wait_recv()

    def rs_total(self, part, recv, c):
        halves = []
        for h in range(2):
            order = order_bits(self.nbits, h)
            total = part[self.me, c, self.rows(h), :].astype(F32)
            for p in range(self.nbits):
                free = order[p + 1 :]
                place = self.rs_base(p) + sum(
                    self.bits[k] * (1 << at) for at, k in enumerate(free)
                )
                total = total + recv[c, place, self.rows(h), :].astype(F32)
            halves.append(total)
        return jnp.concatenate(halves, axis=0)

    def ag_send(self, full, sems, c, p):
        for h in range(2):
            order = order_bits(self.nbits, h)
            fixed = {k: self.bits[k] for k in order[p:]}
            for f in range(1 << p):
                b = compose(order[:p], f, fixed)
                message = (1 << p) - 1 + f
                ref = full.at[b, c, self.rows(h), :]
                cp = self.copy(ref, ref, sems, c, h, message, order[p])
                cp.start()
                self.pending.append(cp)

    def ag_wait(self, full, sems, c, p):
        for h in range(2):
            order = order_bits(self.nbits, h)
            fixed = {k: self.bits[k] for k in order[p + 1 :]}
            fixed[order[p]] = 1 - self.bits[order[p]]
            for f in range(1 << p):
                b = compose(order[:p], f, fixed)
                message = (1 << p) - 1 + f
                ref = full.at[b, c, self.rows(h), :]
                self.copy(ref, ref, sems, c, h, message, order[p]).wait_recv()

    def drain(self):
        for cp in self.pending:
            cp.wait_send()
        self.pending = []


def erf(x):
    c = jnp.clip(x, -3.832506856900711, 3.832506856900711)
    s = c * c
    top = jnp.full_like(s, 0.00022905065861350646)
    for k in (0.0034082910107109506, 0.050955695062380861, 0.18520832239976145, 1.128379143519084):
        top = top * s + k
    low = jnp.full_like(s, -1.1791602954361697e-7)
    for k in (
        0.000023547966471313185,
        0.0010179625278914885,
        0.014070470171167667,
        0.11098505178285362,
        0.49746925110067538,
        1.0,
    ):
        low = low * s + k
    return c * top / low


def gelu_pair(before):
    cumulative = 0.5 * (1.0 + erf(before * half_root))
    density = jnp.exp(-0.5 * before * before) * density_scale
    return before * cumulative, cumulative + before * density


def normalised(stream):
    centre = jnp.mean(stream, axis=-1, keepdims=True)
    centred = stream - centre
    spread = lax.rsqrt(jnp.mean(centred * centred, axis=-1, keepdims=True) + eps)
    return centred * spread, spread


def norm_back(upstream, normed, spread, gain_row):
    scaled = upstream * gain_row
    return spread * (
        scaled
        - jnp.mean(scaled, axis=-1, keepdims=True)
        - normed * jnp.mean(scaled * normed, axis=-1, keepdims=True)
    )


def chunk_of(ref, c):
    x = ref[:, c]
    return x.reshape(x.shape[0] * x.shape[1], x.shape[2])


def column_loop(width, step, fn):
    if width <= step:
        fn(pl.ds(0, width))
    else:

        def one(j, carry):
            fn(pl.ds(pl.multiple_of(j * step, step), step))
            return carry

        lax.fori_loop(0, width // step, one, 0)


def matmul_nn(x, w_ref, cols):
    return jnp.dot(x, w_ref[:, cols], preferred_element_type=F32)


def matmul_nt(x, w_ref, cols):
    return lax.dot_general(
        x, w_ref[cols, :], (((1,), (1,)), ((), ())), preferred_element_type=F32
    )


def tall(ref, cols=slice(None)):
    x = ref[..., cols]
    return x.reshape(x.shape[0] * x.shape[1] * x.shape[2], x.shape[3])


def grad_items(left, right, out, first, step=256):
    width = left.shape[3]
    step = min(step, width)

    def item(at):
        y = lax.dot_general(
            tall(left, slice(at, at + step)), tall(right), (((0,), (0,)), ((), ())), preferred_element_type=F32
        )
        out[first + at : first + at + step, :] = y.astype(BF16)

    return [functools.partial(item, at) for at in range(0, width, step)]


def with_items(ex, stage, items):
    share = -(-len(items) // ex.chunks)

    def both(c):
        for item in items[c * share : (c + 1) * share]:
            item()
        stage(c)

    return both


def rs_stages(ex, part, recv, sems):
    stages = []
    for p in range(1, ex.nbits):

        def stage(c, p=p):
            ex.rs_wait(part, recv, sems, c, p - 1)
            ex.rs_send(part, recv, sems, c, p)

        stages.append(stage)
    return stages


def ag_stages(ex, full, sems):
    stages = []
    for p in range(1, ex.nbits):

        def stage(c, p=p):
            ex.ag_wait(full, sems, c, p - 1)
            ex.ag_send(full, sems, c, p)

        stages.append(stage)
    return stages


def sizes(rows, n):
    block = rows // n
    chunks = 3 if block % 96 == 0 else (2 if block % 64 == 0 else 1)
    return block, chunks, block // chunks


class Total:
    def __init__(self, bufs, recv, sems, dp_size, n, wide):
        self.bufs, self.recv, self.sems, self.wide = bufs, recv, sems, wide
        self.axes = [(N.dp, k) for k in range(dp_size.bit_length() - 1)]
        self.axes += [(N.tensor, k) for k in range(n.bit_length() - 1)]
        self.copies = []

    def target(self, i):
        axis, k = self.axes[i]
        me = lax.axis_index(axis)
        return {axis: me + (1 - 2 * bit_of(me, k)) * (1 << k)}

    def partners(self):
        return [self.target(i) for i, (axis, _) in enumerate(self.axes) if axis == N.dp]

    def start(self, i):
        cp = pltpu.make_async_remote_copy(
            src_ref=self.bufs.at[i],
            dst_ref=self.recv.at[i],
            send_sem=self.sems.at[0, i],
            recv_sem=self.sems.at[1, i],
            device_id=self.target(i),
            device_id_type=MESH,
        )
        cp.start()
        self.copies.append(cp)

    def step(self, i):
        self.copies[i].wait_recv()
        axis, _ = self.axes[i]
        total = self.bufs[i] + self.recv[i]
        if axis == N.tensor:
            row = lax.broadcasted_iota(jnp.int32, total.shape, 0)
            total = jnp.where(row < self.wide, total, self.bufs[i])
        self.bufs[i + 1] = total
        if i + 1 < len(self.axes):
            self.start(i + 1)

    def drain(self):
        for cp in self.copies:
            cp.wait_send()


def run_stages(ex, stages, extra=()):
    extra = sorted(extra, key=lambda pair: pair[0])
    slot = 0
    for stage in stages:
        for c in range(ex.chunks):
            while extra and extra[0][0] <= slot:
                extra.pop(0)[1]()
            stage(c)
            slot += 1
    for _, thunk in extra:
        thunk()


def meet(partners):
    sem = pltpu.get_barrier_semaphore()
    for partner in partners:
        pl.semaphore_signal(sem, inc=1, device_id=partner, device_id_type=MESH)
    pl.semaphore_wait(sem, len(partners))


class Refs:
    def __init__(self):
        self.loads, self.targets, self.stores = {}, {}, []

    def need(self, *names):
        for name in names:
            if name in self.loads:
                self.loads.pop(name).wait()

    def store(self, name, index=()):
        cp = pltpu.make_async_copy(
            getattr(self, name).at[index] if index else getattr(self, name),
            self.targets[name].at[index] if index else self.targets[name],
            self.store_sems.at[len(self.stores)],
        )
        cp.start()
        self.stores.append(cp)

    def finish(self):
        self.need(*list(self.loads))
        for cp in self.stores:
            cp.wait()


def call(kernel, name, collective_id, ins, outs, scratch, flops):
    late_in = [(k, a) for k, a, late in ins if late is True]
    late_out = [(k, shape, dtype) for k, shape, dtype, late in outs if late is True]

    def entry(*refs):
        refs = list(refs)
        take = lambda count: [refs.pop(0) for _ in range(count)]
        r = Refs()
        r.sources = {}
        in_refs, out_refs = take(len(ins)), take(len(outs))
        in_bufs, out_bufs = take(len(late_in)), take(len(late_out))
        load_sems, r.store_sems = take(2)
        bufs = {k: b for (k, _), b in zip(late_in, in_bufs)}
        for (k, _, late), ref in zip(ins, in_refs):
            if late == N.far:
                r.sources[k] = ref
                continue
            setattr(r, k, bufs[k] if late else ref)
            if late:
                cp = pltpu.make_async_copy(ref, bufs[k], load_sems.at[len(r.loads)])
                cp.start()
                r.loads[k] = cp
        bufs = {k: b for (k, _, _), b in zip(late_out, out_bufs)}
        for (k, _), ref in zip(scratch, take(len(scratch))):
            setattr(r, k, ref)
        for (k, _, _, late), ref in zip(outs, out_refs):
            if late == N.far:
                r.targets[k] = ref
                continue
            setattr(r, k, getattr(r, late) if isinstance(late, str) else bufs[k] if late else ref)
            if late:
                r.targets[k] = ref
        kernel(r)
        r.finish()

    space = lambda late: pl.BlockSpec(memory_space=pl.ANY if late else pltpu.VMEM)
    result = pl.pallas_call(
        entry,
        out_shape=[jax.ShapeDtypeStruct(shape, dtype) for _, shape, dtype, _ in outs],
        in_specs=[space(late) for _, _, late in ins],
        out_specs=[space(late) for _, _, _, late in outs],
        scratch_shapes=[pltpu.VMEM(a.shape, a.dtype) for _, a in late_in]
        + [pltpu.VMEM(shape, dtype) for _, shape, dtype in late_out]
        + [pltpu.SemaphoreType.DMA((max(len(late_in), 1),)), pltpu.SemaphoreType.DMA((64,))]
        + [spec for _, spec in scratch],
        compiler_params=pltpu.CompilerParams(
            collective_id=collective_id, has_side_effects=True, vmem_limit_bytes=VMEM_LIMIT
        ),
        cost_estimate=pl.CostEstimate(flops=flops, bytes_accessed=10**8, transcendentals=0),
        name=name,
    )(*[a for _, a, _ in ins])
    return dict(zip([k for k, _, _, _ in outs], result))


def comm_scratch(n, chunks, sub, tag):
    return [
        (N.part + tag, pltpu.VMEM((n, chunks, sub, D), BF16)),
        (N.recv + tag, pltpu.VMEM((chunks, n - 1, sub, D), BF16)),
    ]


def sem_scratch(stages, n, chunks):
    return [(N.sems, pltpu.SemaphoreType.DMA((stages, 2, chunks, 2, n - 1)))]


class Halo:
    def __init__(self, sems, dp_size):
        self.sems, self.size = sems, dp_size
        self.me = lax.axis_index(N.dp)
        self.has = (self.me < dp_size - 1, self.me > 0)
        self.pending = []

    def partners(self):
        return [{N.dp: (self.me + step) % self.size} for step in (1, self.size - 1)]

    def copy(self, src, dst, way, message):
        step = 1 if way == 0 else -1
        return pltpu.make_async_remote_copy(
            src_ref=src,
            dst_ref=dst,
            send_sem=self.sems.at[0, way, message],
            recv_sem=self.sems.at[1, way, message],
            device_id={N.dp: self.me + step},
            device_id_type=MESH,
        )

    def send(self, src, dst, way, message):
        cp = self.copy(src, dst, way, message)

        @pl.when(self.has[way])
        def _():
            cp.start()

        self.pending.append((cp, way))

    def wait(self, dst, way, message):
        @pl.when(self.has[1 - way])
        def _():
            self.copy(dst, dst, way, message).wait_recv()

    def drain(self):
        for cp, way in self.pending:

            @pl.when(self.has[way])
            def _(cp=cp):
                cp.wait_send()


class GradSum:
    def __init__(self, arrays, sems, dp_size):
        self.arrays, self.sems = arrays, sems
        self.local = {}
        self.k = dp_size.bit_length() - 1
        self.me = lax.axis_index(N.dp)
        self.bits = [bit_of(self.me, k) for k in range(self.k)]
        self.pending = []

    def partner(self, k):
        return {N.dp: self.me + (1 - 2 * self.bits[k]) * (1 << k)}

    def partners(self):
        return [self.partner(k) for k in range(self.k)]

    def offset(self, rows, k):
        return sum(self.bits[i] * (rows >> (i + 1)) for i in range(k))

    def copy(self, src, dst, a, message, k):
        return pltpu.make_async_remote_copy(
            src_ref=src,
            dst_ref=dst,
            send_sem=self.sems.at[0, a, message],
            recv_sem=self.sems.at[1, a, message],
            device_id=self.partner(k),
            device_id_type=MESH,
        )

    def recv_rows(self, a, k):
        rows, _, _, _, start, _ = self.arrays[a]
        return (rows >> start) - (rows >> k)

    def here(self, a, at, size):
        rows, _, _, _, start, _ = self.arrays[a]
        return pl.ds(pl.multiple_of(at - self.offset(rows, start), 16), size)

    def add(self, a, base, size, k):
        rows, grad, recv, _, start, _ = self.arrays[a]
        step = 32 if size % 32 == 0 else 16

        def block(i, carry):
            at = base + i * step
            here = self.here(a, at, step)
            total = grad[here, :].astype(F32)
            for j in range(start, k):
                there = at - self.offset(rows, j + 1) + self.recv_rows(a, j)
                total = total + recv[pl.ds(pl.multiple_of(there, 16), step), :].astype(F32)
            grad[here, :] = total.astype(BF16)
            return carry

        lax.fori_loop(0, size // step, block, 0)

    def merge(self, a):
        rows, grad, _, _, start, pieces = self.arrays[a]
        size = rows >> start
        step = 32 if size % 32 == 0 else 16

        def block(i, carry):
            here = pl.ds(pl.multiple_of(i * step, 16), step)
            grad[here, :] = sum(x[here, :].astype(F32) for x in pieces).astype(BF16)
            return carry

        lax.fori_loop(0, size // step, block, 0)

    def send(self, a, k):
        rows, grad, recv, _, start, _ = self.arrays[a]
        size = rows >> (k + 1)
        base = self.offset(rows, k) + (1 - self.bits[k]) * size
        if k > start:
            self.add(a, base, size, k)
        cp = self.copy(
            grad.at[self.here(a, base, size), :], recv.at[pl.ds(self.recv_rows(a, k), size), :], a, k, k
        )
        cp.start()
        self.pending.append(cp)

    def wait(self, a, k):
        rows, _, recv, _, _, _ = self.arrays[a]
        ref = recv.at[pl.ds(self.recv_rows(a, k), rows >> (k + 1)), :]
        self.copy(ref, ref, a, k, k).wait_recv()

    def split(self, a, keep, send):
        rows, grad, recv, _, _, _ = self.arrays[a]
        size = rows >> 2
        step = 32 if size % 32 == 0 else 16
        for out, bit in ((keep, self.bits[1]), (send, 1 - self.bits[1])):

            def block(i, carry, out=out, bit=bit):
                at = bit * size + i * step
                mine = grad[pl.ds(pl.multiple_of(self.bits[0] * 2 * size + at, 16), step), :].astype(F32)
                total = mine + recv[pl.ds(pl.multiple_of(at, 16), step), :].astype(F32)
                out[pl.ds(pl.multiple_of(i * step, 16), step), :] = total.astype(BF16)
                return carry

            lax.fori_loop(0, size // step, block, 0)

    def own(self, a, k, mine):
        rows, _, _, out, _, _ = self.arrays[a]
        size = rows >> (k + 1)
        base = self.offset(rows, k + 1) if mine else self.offset(rows, k) + (1 - self.bits[k]) * size
        return out.at[pl.ds(pl.multiple_of(base, 16), size), :]

    def gather_send(self, a, k):
        ref = self.own(a, k, True)
        src = ref
        if k == self.k - 1:
            rows, grad = self.arrays[a][:2]
            src = grad.at[self.here(a, self.offset(rows, self.k), rows >> self.k), :]
            self.local[a] = pltpu.make_async_copy(src, ref, self.sems.at[0, a, 2 * self.k])
            self.local[a].start()
        elif k == self.k - 2:
            self.local[a].wait()
        cp = self.copy(src, ref, a, self.k + k, k)
        cp.start()
        self.pending.append(cp)

    def gather_wait(self, a, k):
        ref = self.own(a, k, False)
        self.copy(ref, ref, a, self.k + k, k).wait_recv()

    def steps(self, a):
        last, start = self.k - 1, self.arrays[a][4]

        def first():
            if start:
                self.merge(a)
            self.send(a, start)

        def halve(k):
            self.wait(a, k - 1)
            self.send(a, k)

        def turn():
            rows = self.arrays[a][0]
            self.wait(a, last)
            self.add(a, self.offset(rows, self.k), rows >> self.k, self.k)
            self.gather_send(a, last)

        def double(k):
            self.gather_wait(a, k + 1)
            self.gather_send(a, k)

        out = [first] + [functools.partial(halve, k) for k in range(start + 1, self.k)] + [turn]
        out += [functools.partial(double, k) for k in reversed(range(last))]
        return out + [functools.partial(self.gather_wait, a, 0)]

    def drain(self):
        for cp in self.pending:
            cp.wait_send()


def grad_scratch(shapes, dp_size):
    steps = 2 * (dp_size.bit_length() - 1) + 1
    out = [
        ("grad_recv%d" % i, pltpu.VMEM(((rows >> start) - rows // dp_size, cols), BF16))
        for i, (rows, cols, start) in enumerate(shapes)
    ]
    return out + [(N.grad_sems, pltpu.SemaphoreType.DMA((2, len(shapes), steps)))]


def grad_rows(rows, dp_size):
    unit = 16 * dp_size
    return -(-rows // unit) * unit


def placed(steps, slots):
    slots = list(slots)
    while len(slots) < len(steps):
        slots.append(slots[-1] + 2)
    return list(zip(slots, steps))


def forward_kernel(n, dp_size, chunks, sub, last, r):
    ex = Exchange(n, chunks, sub)
    if last:
        meet(ex.partners())
    else:
        halo = Halo(r.halo_sems, dp_size)
        meet(ex.partners() + halo.partners())
    sems = r.sems
    row = lambda i: r.vec[i : i + 1, :]
    full2 = None if last else r.a1

    def pre(c):
        def cols(j):
            y = matmul_nn(chunk_of(r.attended, c), r.proj, j)
            r.part1[:, c, :, j] = y.astype(BF16).reshape(n, sub, -1)

        column_loop(D, 256, cols)
        ex.rs_send(r.part1, r.recv1, sems.at[0], c, 0)

    def own1(c):
        r.need(N.stream)
        ex.rs_wait(r.part1, r.recv1, sems.at[0], c, ex.nbits - 1)
        u1 = ex.rs_total(r.part1, r.recv1, c) + row(0)
        r.u1[c] = u1
        middle = r.stream[c] + row(1) * u1
        r.stream[c] = middle
        hat, spread = normalised(middle)
        r.hat2[c] = hat
        r.sp2[c] = spread
        r.a2[ex.me, c] = (hat * row(2) + row(3)).astype(BF16)
        ex.ag_send(r.a2, sems.at[1], c, 0)
        r.store(N.u1, (c,))
        r.store(N.hat2, (c,))

    def mid(c):
        r.need(N.fc1, N.fc2)
        ex.ag_wait(r.a2, sems.at[1], c, ex.nbits - 1)

        def hidden(j):
            before = matmul_nn(chunk_of(r.a2, c), r.fc1, j) + r.fc1_bias[:, j]
            a, s = gelu_pair(before)
            r.act[:, c, :, j] = a.astype(BF16).reshape(n, sub, -1)
            r.slope[:, c, :, j] = s.astype(BF16).reshape(n, sub, -1)

        column_loop(r.fc1.shape[1], 256, hidden)

        def cols(j):
            y = matmul_nn(chunk_of(r.act, c), r.fc2, j)
            r.part2[:, c, :, j] = y.astype(BF16).reshape(n, sub, -1)

        column_loop(D, 256, cols)
        ex.rs_send(r.part2, r.recv2, sems.at[2], c, 0)
        for name in (N.a2, N.act, N.slope):
            r.store(name, (slice(None), c))

    def own2(c):
        ex.rs_wait(r.part2, r.recv2, sems.at[2], c, ex.nbits - 1)
        u2 = ex.rs_total(r.part2, r.recv2, c) + row(4)
        r.u2[c] = u2
        after = r.stream[c] + row(5) * u2
        r.after[c] = after.astype(r.after.dtype)
        r.store(N.after, (c,))
        r.store(N.u2, (c,))
        if not last:
            hat, spread = normalised(after)
            r.hat1[c] = hat
            r.sp1[c] = spread
            full2[ex.me, c] = (hat * row(6) + row(7)).astype(BF16)
            r.store(N.hat1, (c,))
            ex.ag_send(full2, sems.at[3], c, 0)

    def post(c):
        ex.ag_wait(full2, sems.at[3], c, ex.nbits - 1)
        r.need(N.qkv)
        x = chunk_of(full2, c)
        width = r.q.shape[3]
        for i, name in enumerate((N.q, N.k, N.v)):
            y = matmul_nn(x, r.qkv, slice(i * width, (i + 1) * width))
            if i != 1:
                y = y + r.qv_bias[i // 2 : i // 2 + 1, :]
            getattr(r, name)[:, c] = y.astype(BF16).reshape(n, sub, width)
            r.store(name, (slice(None), c))
            if i:
                for way in range(2):
                    halo.send(
                        getattr(r, name).at[:, c], r.targets[name + N._near].at[way, :, c], way, (i - 1) * chunks + c
                    )
        r.store(N.a1, (slice(None), c))

    run_stages(
        ex,
        [pre]
        + rs_stages(ex, r.part1, r.recv1, sems.at[0])
        + [own1]
        + ag_stages(ex, r.a2, sems.at[1])
        + [mid]
        + rs_stages(ex, r.part2, r.recv2, sems.at[2])
        + [own2]
        + ([] if last else ag_stages(ex, full2, sems.at[3]) + [post]),
    )
    if not last:
        for i, name in enumerate((N.k_near, N.v_near)):
            for c in range(chunks):
                for way in range(2):
                    halo.wait(r.targets[name].at[way, :, c], way, i * chunks + c)
        halo.drain()
    ex.drain()


def forward_block(n, dp_size, last, collective_id, attended, proj, fc1, fc2, fc1_bias, vec, stream, qkv=None, qv_bias=None):
    rows, width = attended.shape
    block, chunks, sub = sizes(rows, n)
    hidden = fc1.shape[1]
    split = lambda cols: (n, chunks, sub, cols)
    mine = (chunks, sub, D)
    ins = [
        (N.attended, attended.reshape(split(width)), False), (N.proj, proj, False), (N.stream, stream.reshape(mine), True),
        (N.fc1, fc1, True), (N.fc2, fc2, True), (N.fc1_bias, fc1_bias, False), (N.vec, vec, False),
    ]
    outs = [
        (N.u1, mine, F32, True), (N.hat2, mine, F32, True), (N.sp2, (chunks, sub, 1), F32, False),
        (N.u2, mine, F32, True), (N.a2, split(D), BF16, True), (N.act, split(hidden), BF16, True),
        (N.slope, split(hidden), BF16, True),
    ]
    scratch = comm_scratch(n, chunks, sub, "1") + comm_scratch(n, chunks, sub, "2")
    if last:
        outs += [(N.after, mine, BF16, True)]
    else:
        ins += [(N.qkv, qkv, True), (N.qv_bias, qv_bias, False)]
        outs += [(N.after, mine, F32, True), (N.hat1, mine, F32, True), (N.sp1, (chunks, sub, 1), F32, False)]
        outs += [(N.a1, split(D), BF16, True)] + [(k, split(width), BF16, True) for k in N.qkv]
        outs += [(k, (2,) + split(width), BF16, N.far) for k in (N.k_near, N.v_near)]
        scratch += [(N.halo_sems, pltpu.SemaphoreType.DMA((2, 2, 2 * chunks)))]
    return call(
        functools.partial(forward_kernel, n, dp_size, chunks, sub, last),
        N.forward_last if last else N.forward_block,
        collective_id,
        ins,
        outs,
        scratch + sem_scratch(4, n, chunks),
        2 * rows * D * (2 * hidden + 4 * width),
    )


def add_rows(ref, i, value):
    ref[i : i + 1, :] += jnp.sum(value, axis=0, keepdims=True)


def input_norm_own(ex, r, c, gain, sums):
    r.need(N.hat1, N.gm)
    ex.rs_wait(r.part, r.recv, r.sems.at[0], c, ex.nbits - 1)
    da1 = ex.rs_total(r.part, r.recv, c)
    add_rows(sums, 6, da1 * r.hat1[c])
    add_rows(sums, 7, da1)
    return r.gm[c] + norm_back(da1, r.hat1[c], r.sp1[c], gain)


def send_home(halo, r, chunks):
    cp = pltpu.make_async_copy(r.sources[N.dkv_in].at[:, 1], r.dkv, r.dkv_sem)
    cp.start()
    r.loads[N.dkv] = cp
    for c in range(chunks):
        for way in range(2):
            for i in range(2):
                src = r.sources[N.dkv_in].at[i, 2 - 2 * way, :, c]
                halo.send(src, near_part(r, way, i, c), way, 2 * c + i)


def near_part(r, way, i, c):
    width = r.dq.shape[3]
    return r.near.at[:, c, :, pl.ds((2 * way + i) * width, width)]


def input_grad_chunk(ex, halo, r, c):
    r.need(N.dq, N.dkv, N.qkv)
    width = r.dq.shape[3]
    for way in range(2):
        for i in range(2):
            halo.wait(near_part(r, way, i, c), way, 2 * c + i)
    r.dqkv[:, c, :, :width] = r.dq[:, c]
    for i in range(2):
        cols = slice((i + 1) * width, (i + 2) * width)

        for b in range(ex.n):
            r.total_kv[...] = r.dkv[i, b, c].astype(F32)
            for way in range(2):

                @pl.when(halo.has[1 - way])
                def _():
                    first = (2 * way + i) * width
                    r.total_kv[...] += r.near[b, c, :, first : first + width].astype(F32)

            total = r.total_kv[...]
            if i:
                r.dv_sum[...] += jnp.sum(total, axis=0, keepdims=True)
            r.dqkv[b, c, :, cols] = total.astype(BF16)

    def cols(j):
        y = matmul_nt(chunk_of(r.dqkv, c), r.qkv, j)
        r.part[:, c, :, j] = y.astype(BF16).reshape(ex.n, ex.sub, -1)

    column_loop(D, 256, cols)
    ex.rs_send(r.part, r.recv, r.sems.at[0], c, 0)


def backward_kernel(n, dp_size, chunks, sub, first, r):
    ex = Exchange(n, chunks, sub)
    sems, part, recv = r.sems, r.part, r.recv
    row = lambda i: r.vec[i : i + 1, :]
    if first:
        meet(ex.partners() + [{N.dp: core_partner()}])
    else:
        halo = Halo(r.halo_sems, dp_size)
        gs = GradSum(upper_arrays(r), r.grad_sems, dp_size)
        meet(ex.partners() + gs.partners() + halo.partners())
        r.near = r.e1
        send_home(halo, r, chunks)
        r.dv_sum[...] = jnp.zeros_like(r.dv_sum)
    first_arrays = [(x.shape[0], x, recv, None, 0, ()) for x, recv in ((r.g1, r.core_recv0), (r.g2, r.core_recv1))]
    first_sum = GradSum(first_arrays, r.core_sems, dp_size)
    r.sums[...] = jnp.zeros_like(r.sums)
    r.fc1b[...] = jnp.zeros_like(r.fc1b)
    width, hidden_size = r.proj.shape[0], r.fc1.shape[1]
    if r.g4.shape[0] > width:
        r.g4[width:, :] = jnp.zeros((r.g4.shape[0] - width, D), BF16)

    def pre(c):
        input_grad_chunk(ex, halo, r, c)

    def own0(c):
        r.need(N.u2)
        g = input_norm_own(ex, r, c, row(3), r.sums)
        add_rows(r.sums, 0, g * r.u2[c])
        add_rows(r.sums, 1, g * row(0))
        r.gm[c] = g
        r.full[ex.me, c] = (g * row(0)).astype(BF16)
        ex.ag_send(r.full, sems.at[1], c, 0)

    def mid(c):
        r.need(N.fc1, N.fc2, N.slope, N.full, N.u2, N.gm)
        if not first and c == 0:
            ex.drain()
        if first:
            g = r.gm[c]
            add_rows(r.sums, 0, g * r.u2[c])
            add_rows(r.sums, 1, g * row(0))
        else:
            ex.ag_wait(r.full, sems.at[1], c, ex.nbits - 1)

        def hidden(j):
            y = matmul_nt(chunk_of(r.full, c), r.fc2, j)
            w = y.shape[1]
            db = y * r.slope[:, c, :, j].astype(F32).reshape(n * sub, w)
            r.fc1b[:, j] += jnp.sum(db, axis=0, keepdims=True)
            r.slope[:, c, :, j] = db.astype(BF16).reshape(n, sub, w)

        column_loop(hidden_size, 256, hidden)

        def cols(j):
            y = matmul_nt(chunk_of(r.slope, c), r.fc1, j)
            part[:, c, :, j] = y.astype(BF16).reshape(n, sub, -1)

        column_loop(D, 256, cols)
        ex.rs_send(part, recv, sems.at[2], c, 0)

    def own1(c):
        r.need(N.hat2, N.u1)
        ex.rs_wait(part, recv, sems.at[2], c, ex.nbits - 1)
        da2 = ex.rs_total(part, recv, c)
        hat = r.hat2[c]
        add_rows(r.sums, 2, da2 * hat)
        add_rows(r.sums, 3, da2)
        gm = r.gm[c] + norm_back(da2, hat, r.sp2[c], row(1))
        r.gm[c] = gm
        add_rows(r.sums, 4, gm * r.u1[c])
        add_rows(r.sums, 5, gm * row(2))
        r.e1[ex.me, c] = (gm * row(2)).astype(BF16)
        ex.ag_send(r.e1, sems.at[3], c, 0)
        r.store(N.gm_out, (c,))

    def post(c):
        r.need(N.proj)
        ex.ag_wait(r.e1, sems.at[3], c, ex.nbits - 1)
        y = matmul_nt(chunk_of(r.e1, c), r.proj, slice(None))
        r.datt[:, c] = y.astype(BF16).reshape(n, sub, -1)
        r.store(N.datt, (slice(None), c))

    stages, extra = [], []
    if not first:
        made = [lambda: r.need(N.a1)] + grad_items(r.a1, r.dqkv, r.up3, 0)
        stages = [pre] + rs_stages(ex, part, recv, sems.at[0]) + [own0] + ag_stages(ex, r.full, sems.at[1])
        stages[1] = with_items(ex, stages[1], made)
        r.act = r.a1.at[:, :, :, pl.ds(0, hidden_size)]

        def fetch_act():
            cp = pltpu.make_async_copy(r.sources[N.act], r.act, r.act_sem)
            cp.start()
            r.loads[N.act] = cp

        extra += [(2 * chunks, fetch_act)]
        extra += [(3, lambda: r.need(N.keep1, N.got1, N.keep2, N.got2, N.up4))]
        extra += placed_sums(gs)
    gathers = ag_stages(ex, r.e1, sems.at[3])
    sums2 = rs_stages(ex, part, recv, sems.at[2])
    sums2[0] = with_items(ex, sums2[0], [lambda: r.need(N.act)] + grad_items(r.act, r.full, r.g1, 0))
    made = [lambda: r.need(N.a2)] + grad_items(r.a2, r.slope, r.g2, 0)
    stages += [mid] + sums2 + [with_items(ex, own1, made)] + gathers + [post]
    end = len(stages) * chunks
    behind = end - chunks * (1 + len(gathers))

    def part_of(a):
        first_sum.wait(a, 0)
        names = ((N.keep1, N.send1), (N.keep2, N.send2))[a]
        first_sum.split(a, getattr(r, names[0] + N._out), getattr(r, names[1] + N._out))
        for name in names:
            r.store(name + N._out)

    extra += [(behind - chunks, lambda: first_sum.send(0, 0)), (behind + 1, lambda: part_of(0))]
    extra += [(behind + 1, lambda: first_sum.send(1, 0)), (behind + 3, lambda: part_of(1))]
    run_stages(ex, stages, extra)
    r.need(N.attended)
    for item in grad_items(r.attended, r.e1, r.g4, 0):
        item()
    if not first:
        gs.drain()
        halo.drain()
    first_sum.drain()
    ex.drain()


def core_partner():
    me = lax.axis_index(N.dp)
    return me + 1 - 2 * bit_of(me, 0)


def tail_sums(gs):
    return (
        placed(gs.steps(0), (3, 6, 10, 13, 16))
        + placed(gs.steps(1), (4, 9, 13, 15.5, 17))
        + placed(gs.steps(2), (6, 7, 9, 12, 15, 16, 18))
        + placed(gs.steps(3), (3, 5, 7, 10, 12, 14, 17))
    )


def placed_sums(gs):
    return (
        placed(gs.steps(0), (3, 9, 15, 21, 25))
        + placed(gs.steps(1), (4, 10, 16, 22, 26))
        + placed(gs.steps(2), (6, 7, 11, 17, 20, 24, 27))
        + placed(gs.steps(3), (3, 5, 8, 12, 14, 18, 23))
    )


def upper_arrays(r):
    pieces = ((r.keep1, r.got1), (r.keep2, r.got2), (), ())
    return [
        (
            r.targets["up%d_out" % (i + 1)].shape[0],
            getattr(r, "up%d" % (i + 1)),
            getattr(r, "grad_recv%d" % i),
            r.targets["up%d_out" % (i + 1)],
            2 if x else 0,
            x,
        )
        for i, x in enumerate(pieces)
    ]


def upper_buffers(above, width, dp_size):
    shapes = [(4 * x.shape[0], x.shape[1]) for x in (above[N.keep1], above[N.keep2])]
    shapes += [(D, 3 * width), above[N.up4].shape]
    scratch = [(N.up1, pltpu.VMEM(above[N.keep1].shape, BF16)), (N.up2, pltpu.VMEM(above[N.keep2].shape, BF16))]
    scratch += [(N.up3, pltpu.VMEM(shapes[2], BF16))]
    scratch += grad_scratch([x + (start,) for x, start in zip(shapes, (2, 2, 0, 0))], dp_size)
    return scratch, [("up%d_out" % (i + 1), x, BF16, N.far) for i, x in enumerate(shapes)]


def home_buffers(n, chunks, sub, width):
    split = (n, chunks, sub)
    return [
        (N.dqkv, pltpu.VMEM(split + (3 * width,), BF16)),
        (N.total_kv, pltpu.VMEM((sub, width), F32)),
        (N.dkv, pltpu.VMEM((2,) + split + (width,), BF16)),
        (N.dkv_sem, pltpu.SemaphoreType.DMA),
        (N.halo_sems, pltpu.SemaphoreType.DMA((2, 2, 2 * chunks))),
    ]


def backward_block(n, dp_size, collective_id, source, above, fc1, fc2, proj, vec, saved):
    first = not above
    _, chunks, sub, hidden = saved[N.slope].shape
    width = proj.shape[0]
    split = lambda cols: (n, chunks, sub, cols)
    mine = (chunks, sub, D)
    ins = list(source.items()) + list(above.items()) + [(N.fc2, fc2), (N.slope, saved[N.slope]), (N.fc1, fc1)]
    ins += [(k, saved[k]) for k in (N.u2, N.act, N.a2, N.hat2, N.u1, N.sp2, N.attended)] + [(N.proj, proj), (N.vec, vec)]
    outs = [
        (N.datt, split(width), BF16, True), (N.gm_out, mine, F32, N.gm), (N.sums, (8, D), F32, False),
        (N.fc1b, (1, hidden), F32, False), (N.g4, (grad_rows(width, dp_size), D), BF16, False),
    ]
    for i, (rows, cols) in enumerate(((hidden, D), (D, hidden))):
        outs += [(k % (i + 1), (rows // 4, cols), BF16, True) for k in ("keep%d_out", "send%d_out")]
    scratch = comm_scratch(n, chunks, sub, "") + [(N.e1, pltpu.VMEM(split(D), BF16))] + sem_scratch(4, n, chunks)
    scratch += [(N.g1, pltpu.VMEM((hidden, D), BF16)), (N.g2, pltpu.VMEM((D, hidden), BF16))]
    scratch += [(N.core_recv0, pltpu.VMEM((hidden // 2, D), BF16)), (N.core_recv1, pltpu.VMEM((D // 2, hidden), BF16))]
    scratch += [(N.core_sems, pltpu.SemaphoreType.DMA((2, 2, 2 * (dp_size.bit_length() - 1))))]
    if not first:
        scratch += [(N.act_sem, pltpu.SemaphoreType.DMA)]
        scratch += [(N.full, pltpu.VMEM(split(D), BF16))] + home_buffers(n, chunks, sub, width)
        more, results = upper_buffers(above, width, dp_size)
        scratch += more
        outs += results + [(N.dv_sum, (1, width), F32, False)]
    return call(
        functools.partial(backward_kernel, n, dp_size, chunks, sub, first),
        N.backward_first if first else N.backward_block,
        collective_id,
        [(k, a, N.far if k == N.act and not first else lateness(k)) for k, a in ins],
        outs,
        scratch,
        2 * n * chunks * sub * D * (2 * hidden + 4 * width),
    )


def lateness(name):
    if name == N.dkv_in:
        return N.far
    return name not in (N.sp1, N.sp2, N.vec, N.base)


def tail_kernel(n, dp_size, chunks, sub, wide, r):
    ex = Exchange(n, chunks, sub)
    small = Total(r.bufs, r.small_recv, r.small_sems, dp_size, n, wide)
    gs = GradSum(upper_arrays(r), r.grad_sems, dp_size)
    halo = Halo(r.halo_sems, dp_size)
    meet(ex.partners() + gs.partners() + halo.partners())
    r.near = r.full
    send_home(halo, r, chunks)
    sems = r.sems
    r.dv_sum[...] = jnp.zeros_like(r.dv_sum)
    r.sums[...] = jnp.zeros_like(r.sums)

    def pre(c):
        input_grad_chunk(ex, halo, r, c)

    def own(c):
        g = input_norm_own(ex, r, c, r.vec[0:1, :], r.sums)
        r.full[ex.me, c] = g.astype(BF16)
        ex.ag_send(r.full, sems.at[1], c, 0)
        if c == chunks - 1:
            r.bufs[0] = r.base[...]
            r.bufs[0, 0:8, :] = r.sums[...]
            r.bufs[0, wide : wide + 1, : r.dv_sum.shape[1]] = r.dv_sum[...]
            small.start(0)

    def post(c):
        ex.ag_wait(r.full, sems.at[1], c, ex.nbits - 1)
        for b in range(n):
            r.out[b, c] = r.full[b, c].astype(F32)
        r.store(N.out, (slice(None), c))

    made = [lambda: r.need(N.a1)] + grad_items(r.a1, r.dqkv, r.up3, 0)
    stages = [pre] + rs_stages(ex, r.part, r.recv, sems.at[0]) + [own] + ag_stages(ex, r.full, sems.at[1]) + [post]
    stages[1] = with_items(ex, stages[1], made)
    after_own = chunks * (2 + ex.nbits - 1)
    extra = [(3, lambda: r.need(N.keep1, N.got1, N.keep2, N.got2, N.up4))]
    extra += tail_sums(gs)

    def spread(c, p):
        if p == 0:
            r.need(N.result)
            r.full3[ex.me, c] = r.result[c]
        else:
            ex.ag_wait(r.full3, sems.at[2], c, p - 1)
        if p < ex.nbits:
            ex.ag_send(r.full3, sems.at[2], c, p)
        else:
            for b in range(n):
                r.out2[b, c] = r.full3[b, c].astype(F32)
            r.store(N.out2, (slice(None), c))

    for p in range(ex.nbits + 1):
        slot = after_own + chunks * ex.nbits if p == ex.nbits else chunks * (1 + 2 * p)
        extra += [(slot + c, functools.partial(spread, c, p)) for c in range(chunks)]
    extra += [(after_own + 1 + i, functools.partial(small.step, i)) for i in range(len(small.axes))]
    run_stages(ex, stages, extra)
    halo.drain()
    r.total[...] = r.bufs[len(small.axes)]
    ex.drain()
    small.drain()
    gs.drain()


def backward_tail(n, dp_size, collective_id, wide, source, above, vec, base, result):
    _, chunks, sub, width = source[N.dq].shape
    split = lambda cols: (n, chunks, sub, cols)
    steps = (n * dp_size).bit_length() - 1
    ins = list(source.items()) + list(above.items()) + [(N.vec, vec), (N.base, base), (N.result, result)]
    more, results = upper_buffers(above, width, dp_size)
    outs = [(N.out, split(D), F32, True), (N.out2, split(D), F32, True), (N.total, base.shape, F32, False)] + results
    scratch = comm_scratch(n, chunks, sub, "") + sem_scratch(3, n, chunks) + home_buffers(n, chunks, sub, width)
    scratch += [(N.full3, pltpu.VMEM(split(D), BF16))]
    scratch += [(N.full, pltpu.VMEM(split(D), BF16)), (N.sums, pltpu.VMEM((8, D), F32)), (N.dv_sum, pltpu.VMEM((1, width), F32))]
    scratch += [(N.bufs, pltpu.VMEM((steps + 1,) + base.shape, F32)), (N.small_recv, pltpu.VMEM((steps,) + base.shape, F32))]
    scratch += [(N.small_sems, pltpu.SemaphoreType.DMA((2, steps)))] + more
    return call(
        functools.partial(tail_kernel, n, dp_size, chunks, sub, wide),
        N.backward_tail,
        collective_id,
        [(k, a, lateness(k)) for k, a in ins],
        outs,
        scratch,
        2 * n * chunks * sub * D * 3 * width,
    )


def id_features(ids_col, query_side):
    lane = lax.broadcasted_iota(jnp.int32, (ids_col.shape[0], HD), 1)
    bit = (ids_col >> (lane & 15)) & 1
    first = lane < 16
    second = (lane >= 16) & (lane < 32)
    inv = 1 - bit
    if query_side:
        v = jnp.where(first, bit, jnp.where(second, inv, 0)).astype(F32) * (-BIG)
    else:
        v = jnp.where(first, inv, jnp.where(second, bit, 0)).astype(F32)
    return v

def each_tile(KB, t_lo, t_hi, kn_ref, vn_ref, k_ref, v_ref, fn):
    per = k_ref.shape[0] // KB
    for segment in range(3):
        def one(t, carry, segment=segment):
            here = pl.ds(pl.multiple_of((t - segment * per) * KB, KB), KB)
            if segment == 1:
                fn(t, here, k_ref[here, :], v_ref[here, :])
            else:
                fn(t, here, kn_ref[segment // 2, here, :], vn_ref[segment // 2, here, :])
            return carry
        lax.fori_loop(jnp.maximum(t_lo, segment * per), jnp.minimum(t_hi, (segment + 1) * per), one, 0)

def fwd_kernel(HH, QB, KB, KT, nq, lo_ref, hi_ref, q_ref, kn_ref, vn_ref, k_ref, v_ref, idq_ref, idk_ref, o_ref, lse_ref, kaug, vt, qaug):
    t_lo = lo_ref[nq]
    t_hi = hi_ref[nq]
    def prep(t, here, kk, vv):
        r = pl.ds(pl.multiple_of(t * KT, KT), KT)
        feat = id_features(idk_ref[r, :], False).astype(BF16)
        for h in range(HH):
            kaug[h, r, :] = jnp.concatenate([kk[:, h * HD:(h + 1) * HD], feat], axis=1)
        vt[:, r] = vv.T
    each_tile(KT, t_lo, t_hi, kn_ref, vn_ref, k_ref, v_ref, prep)
    def qprep(t, _):
        r = pl.ds(pl.multiple_of(t * QB, QB), QB)
        feat = id_features(idq_ref[r, :], True).astype(BF16)
        qq = (q_ref[r, :] * BF16(0.125))
        for h in range(HH):
            qaug[h, :, r] = jnp.concatenate([qq[:, h * HD:(h + 1) * HD], feat], axis=1).T
        return 0
    lax.fori_loop(0, nq, qprep, 0)
    def qloop(qb, _):
        rq = pl.ds(pl.multiple_of(qb * QB, QB), QB)
        lo = lo_ref[qb]
        qts = [qaug[h, :, rq] for h in range(HH)]
        def kloop(t, c):
            r = pl.ds(pl.multiple_of(lo * KT + t * KB, KT), KB)
            new = []
            for h in range(HH):
                m, l, acc = c[h]
                s = jnp.dot(kaug[h, r, :], qts[h], preferred_element_type=F32)
                mn = jnp.maximum(m, jnp.max(s, axis=0, keepdims=True))
                p = jnp.exp(s - mn)
                al = jnp.exp(m - mn)
                l = l * al + jnp.sum(p, axis=0, keepdims=True)
                acc = acc * al + jnp.dot(vt[h * HD:(h + 1) * HD, r], p.astype(BF16), preferred_element_type=F32)
                new.append((mn, l, acc))
            return tuple(new)
        z = (jnp.full((1, QB), -3e38, F32), jnp.zeros((1, QB), F32), jnp.zeros((HD, QB), F32))
        c = lax.fori_loop(0, (hi_ref[qb] - lo) // (KB // KT), kloop, (z,) * HH)
        both = jnp.concatenate([c[h][2] / c[h][1] for h in range(HH)], axis=0)
        o_ref[rq, :] = both.T.astype(BF16)
        for h in range(HH):
            lse_ref[0, h:h + 1, rq] = c[h][0] + jnp.log(c[h][1])
        return 0
    lax.fori_loop(0, nq, qloop, 0)

def attend_fwd(q, kn, vn, k, v, idq, idk, lo, hi, HH, QB, KB, KT):
    n, cols = q.shape
    w = 3 * n
    HH = min(HH, cols // HD)
    wide = HH * HD
    near = pl.BlockSpec((2, n, wide), lambda g, *_: (0, 0, g))
    pairs = cols // wide
    nq = n // QB
    return pl.pallas_call(
        functools.partial(fwd_kernel, HH, QB, KB, KT, nq),
        grid_spec=pltpu.PrefetchScalarGridSpec(
            num_scalar_prefetch=2, grid=(pairs,),
            in_specs=[pl.BlockSpec((n, wide), lambda g, *_: (0, g)), near, near, pl.BlockSpec((n, wide), lambda g, *_: (0, g)), pl.BlockSpec((n, wide), lambda g, *_: (0, g)),
                      pl.BlockSpec((n, 1), lambda g, *_: (0, 0)), pl.BlockSpec((w, 1), lambda g, *_: (0, 0))],
            out_specs=[pl.BlockSpec((n, wide), lambda g, *_: (0, g)), pl.BlockSpec((1, HH, n), lambda g, *_: (g, 0, 0))],
            scratch_shapes=[pltpu.VMEM((HH, w, 128), BF16), pltpu.VMEM((wide, w), BF16), pltpu.VMEM((HH, 128, n), BF16)]),
        out_shape=[jax.ShapeDtypeStruct((n, cols), BF16), jax.ShapeDtypeStruct((pairs, HH, n), F32)],
        compiler_params=pltpu.CompilerParams(vmem_limit_bytes=VMEM_LIMIT),
        cost_estimate=pl.CostEstimate(flops=5 * 10**10, bytes_accessed=10**8, transcendentals=0),
        name=N.attend_fwd,
    )(lo, hi, q, kn, vn, k, v, idq, idk)

def bwd_kernel(HH, QB, KB, KT, nq, lo_ref, hi_ref, q_ref, kn_ref, vn_ref, k_ref, v_ref, idq_ref, idk_ref, o_ref, g_ref, lse_ref, dq_ref, dkv_ref, qsum_ref, kaug, vaug, kt, qaug, gaug, acc):
    w = 3 * k_ref.shape[0]
    t_lo = lo_ref[nq]
    t_hi = hi_ref[nq]
    wide = HH * HD
    lane = lax.broadcasted_iota(jnp.int32, (KT, HD), 1)
    three = ((lane >= 32) & (lane < 35))
    def zero(t, _):
        r = pl.ds(pl.multiple_of(t * KT, KT), KT)
        for i in range(2):
            dkv_ref[i, r, :] = jnp.zeros((KT, wide), BF16)
        return 0
    lax.fori_loop(0, w // KT, zero, 0)
    def prep(t, here, kk, vv):
        r = pl.ds(pl.multiple_of(t * KT, KT), KT)
        feat = jnp.where(three, 1.0, id_features(idk_ref[r, :], False)).astype(BF16)
        ones = jnp.where(three, 1.0, 0.0).astype(BF16)
        for h in range(HH):
            kaug[h, r, :] = jnp.concatenate([kk[:, h * HD:(h + 1) * HD], feat], axis=1)
            vaug[h, r, :] = jnp.concatenate([vv[:, h * HD:(h + 1) * HD], ones], axis=1)
            acc[h, r, :] = jnp.zeros((KT, 128), F32)
        kt[:, r] = kk.T
    each_tile(KT, t_lo, t_hi, kn_ref, vn_ref, k_ref, v_ref, prep)
    qsum_ref[...] = jnp.zeros((1, wide), F32)
    def pieces(x):
        a = x.astype(BF16).astype(F32)
        b = (x - a).astype(BF16).astype(F32)
        return a, b, x - a - b
    def qprep(t, _):
        r = pl.ds(pl.multiple_of(t * QB, QB), QB)
        fid = id_features(idq_ref[r, :], True).T
        row = lax.broadcasted_iota(jnp.int32, (HD, QB), 0)
        qt = (q_ref[r, :] * BF16(0.125)).T
        gg = g_ref[r, :]
        gt = gg.T
        prod = (gg.astype(F32) * o_ref[r, :].astype(F32)).T
        for h in range(HH):
            a, b, c = pieces(-lse_ref[0, h:h + 1, r])
            f = jnp.where(row == 32, a, jnp.where(row == 33, b, jnp.where(row == 34, c, fid)))
            qaug[h, :, r] = jnp.concatenate([qt[h * HD:(h + 1) * HD, :], f.astype(BF16)], axis=0)
            d = -jnp.sum(prod[h * HD:(h + 1) * HD, :], axis=0, keepdims=True)
            a, b, c = pieces(d)
            f = jnp.where(row == 32, a, jnp.where(row == 33, b, jnp.where(row == 34, c, 0.0)))
            gaug[h, :, r] = jnp.concatenate([gt[h * HD:(h + 1) * HD, :], f.astype(BF16)], axis=0)
        return 0
    lax.fori_loop(0, nq, qprep, 0)
    def qloop(qb, _):
        rq = pl.ds(pl.multiple_of(qb * QB, QB), QB)
        qq = q_ref[rq, :] * BF16(0.125)
        gg = g_ref[rq, :]
        zz = jnp.zeros((QB, HD), BF16)
        lo = lo_ref[qb]
        qts = [qaug[h, :, rq] for h in range(HH)]
        gts = [gaug[h, :, rq] for h in range(HH)]
        rhs = [jnp.concatenate([jnp.concatenate([qq[:, h * HD:(h + 1) * HD], zz], axis=1), jnp.concatenate([zz, gg[:, h * HD:(h + 1) * HD]], axis=1)], axis=0) for h in range(HH)]
        def kloop(t, c):
            r = pl.ds(pl.multiple_of(lo * KT + t * KB, KT), KB)
            new = []
            for h in range(HH):
                s = jnp.dot(kaug[h, r, :], qts[h], preferred_element_type=F32)
                dp = jnp.dot(vaug[h, r, :], gts[h], preferred_element_type=F32)
                p = jnp.exp(s)
                ds = (p * dp).astype(BF16)
                both = jnp.concatenate([ds, p.astype(BF16)], axis=1)
                acc[h, r, :] += jnp.dot(both, rhs[h], preferred_element_type=F32)
                new.append(c[h] + jnp.dot(kt[h * HD:(h + 1) * HD, r], ds, preferred_element_type=F32))
            return tuple(new)
        z = jnp.zeros((HD, QB), F32)
        c = lax.fori_loop(0, (hi_ref[qb] - lo) // (KB // KT), kloop, (z,) * HH)
        dq = (jnp.concatenate(c, axis=0) * 0.125).T
        qsum_ref[...] += jnp.sum(dq, axis=0, keepdims=True)
        dq_ref[rq, :] = dq.astype(BF16)
        return 0
    lax.fori_loop(0, nq, qloop, 0)
    def fin(t, _):
        r = pl.ds(pl.multiple_of(t * KT, KT), KT)
        sums = [acc[h, r, :] for h in range(HH)]
        for i in range(2):
            dkv_ref[i, r, :] = jnp.concatenate([x[:, i * HD:(i + 1) * HD] for x in sums], axis=1).astype(BF16)
        return 0
    lax.fori_loop(t_lo, t_hi, fin, 0)

def attend_bwd(q, kn, vn, k, v, idq, idk, lo, hi, out, grad, lse, HH, QB, KB, KT):
    n, cols = q.shape
    w = 3 * n
    HH = min(HH, cols // HD)
    wide = HH * HD
    near = pl.BlockSpec((2, n, wide), lambda g, *_: (0, 0, g))
    pairs = cols // wide
    nq = n // QB
    rows = lambda m: pl.BlockSpec((m, wide), lambda g, *_: (0, g))
    return pl.pallas_call(
        functools.partial(bwd_kernel, HH, QB, KB, KT, nq),
        grid_spec=pltpu.PrefetchScalarGridSpec(
            num_scalar_prefetch=2, grid=(pairs,),
            in_specs=[rows(n), near, near, rows(n), rows(n), pl.BlockSpec((n, 1), lambda g, *_: (0, 0)), pl.BlockSpec((w, 1), lambda g, *_: (0, 0)), rows(n), rows(n), pl.BlockSpec((1, HH, n), lambda g, *_: (g, 0, 0))],
            out_specs=[rows(n), pl.BlockSpec((2, w, wide), lambda g, *_: (0, 0, g)), pl.BlockSpec((1, wide), lambda g, *_: (0, g))],
            scratch_shapes=[pltpu.VMEM((HH, w, 128), BF16), pltpu.VMEM((HH, w, 128), BF16), pltpu.VMEM((wide, w), BF16), pltpu.VMEM((HH, 128, n), BF16), pltpu.VMEM((HH, 128, n), BF16), pltpu.VMEM((HH, w, 128), F32)]),
        out_shape=[jax.ShapeDtypeStruct((n, cols), BF16), jax.ShapeDtypeStruct((2, w, cols), BF16), jax.ShapeDtypeStruct((1, cols), F32)],
        compiler_params=pltpu.CompilerParams(vmem_limit_bytes=VMEM_LIMIT),
        cost_estimate=pl.CostEstimate(flops=5 * 10**10, bytes_accessed=10**8, transcendentals=0),
        name=N.attend_bwd,
    )(lo, hi, q, kn, vn, k, v, idq, idk, out, grad, lse)

def reach(ids_win, n, QB, KB, KT, least, most):
    w = ids_win.shape[0]
    own = ids_win[n:2 * n].reshape(n // QB, QB)
    lo = (jnp.argmax(ids_win[None, :] == own[:, :1], axis=1) // KT).astype(jnp.int32)
    hi = ((w - jnp.argmax(ids_win[::-1][None, :] == own[:, -1:], axis=1) + KT - 1) // KT).astype(jnp.int32)
    need = -(lo - hi) % (KB // KT)
    need = jnp.where(need > 0, KB // KT - need, 0)
    up = jnp.minimum(most - hi, need)
    lo, hi = lo - (need - up), hi + up
    return jnp.append(lo, jnp.min(lo)), jnp.append(hi, jnp.max(hi))


def neighbours(axis):
    peers = lax.axis_size(axis)
    up = [(i, i + 1) for i in range(peers - 1)]
    return up, [(j, i) for i, j in up]


def with_halo(array):
    up, down = neighbours(N.dp)
    return jnp.concatenate(
        [lax.ppermute(array, N.dp, up), array, lax.ppermute(array, N.dp, down)], axis=0
    )


def near(array):
    up, down = neighbours(N.dp)
    return jnp.stack([lax.ppermute(array, N.dp, up), lax.ppermute(array, N.dp, down)])


def own_part(array, n):
    block, chunks, sub = sizes(array.shape[0], n)
    first = lax.axis_index(N.tensor) * block
    return lax.dynamic_slice_in_dim(array, first, block, 0).reshape(chunks, sub, array.shape[1])


def body(
    tokens, image_ids, cotangent, ln1_gain, ln1_bias, qkv_weight, qv_bias, proj_weight, proj_bias, scale_attn,
    ln2_gain, ln2_bias, fc1_weight, fc1_bias, fc2_weight, fc2_bias, scale_mlp,
):
    n = lax.axis_size(N.tensor)
    rows = tokens.shape[0]
    width, hidden = qkv_weight.shape[3], fc1_weight.shape[2]
    _, chunks, sub = sizes(rows, n)
    split = (n, chunks, sub)
    qkv2 = qkv_weight.reshape(LAYERS, D, 3 * width)
    ids_win = with_halo(image_ids + 1)
    per = rows // TILES[3]
    place, places = lax.axis_index(N.dp), lax.axis_size(N.dp)
    least, most = jnp.where(place == 0, per, 0), jnp.where(place == places - 1, 2 * per, 3 * per)
    lo, hi = reach(ids_win, rows, *TILES[1:], least, most)
    idq, idk = ids_win[rows : 2 * rows, None], ids_win[:, None]

    stream = tokens.astype(F32)
    hat, _ = normalised(stream)
    a1 = (hat * ln1_gain[0] + ln1_bias[0]).astype(BF16)
    first = jnp.dot(a1, qkv2[0], preferred_element_type=F32)
    q = (first[:, :width] + qv_bias[0, 0]).astype(BF16)
    k = first[:, width : 2 * width].astype(BF16)
    v = (first[:, 2 * width :] + qv_bias[0, 1]).astype(BF16)
    a1 = a1.reshape(split + (D,))
    own = own_part(tokens, n).astype(F32)
    hat1, sp1 = normalised(own)

    saved = []
    dp_size = lax.axis_size(N.dp)
    kn, vn = near(k), near(v)
    for level in range(LAYERS):
        kv = (kn, vn, k, v)
        attended, lse = attend_fwd(q, *kv, idq, idk, lo, hi, *TILES)
        last = level == LAYERS - 1
        after = 0 if last else level + 1
        vec = jnp.stack(
            [
                proj_bias[level], scale_attn[level], ln2_gain[level], ln2_bias[level], fc2_bias[level],
                scale_mlp[level], ln1_gain[after], ln1_bias[after],
            ]
        )
        extra = () if last else (qkv2[level + 1], qv_bias[level + 1])
        made = forward_block(
            n, dp_size, last, level, attended, proj_weight[level], fc1_weight[level], fc2_weight[level], fc1_bias[level][None],
            vec, own, *extra,
        )
        keep = {name: made[name] for name in (N.u1, N.hat2, N.sp2, N.u2, N.a2, N.act, N.slope)}
        keep[N.attended] = attended.reshape(split + (width,))
        saved.append((q, kv, attended, lse, a1, hat1, sp1, keep))
        if last:
            result = made[N.after]
        else:
            own, hat1, sp1, a1 = (made[name] for name in (N.after, N.hat1, N.sp1, N.a1))
            q, k, v = (made[name].reshape(rows, width) for name in N.qkv)
            kn, vn = (made[name].reshape(2, rows, width) for name in (N.k_near, N.v_near))

    cot = cotangent.astype(F32)
    source = {
        N.full: (cot * scale_mlp[LAYERS - 1]).astype(BF16).reshape(split + (D,)),
        N.gm: own_part(cotangent, n).astype(F32),
    }
    above, grads = {}, [None] * LAYERS
    sums, narrow, dv_sums = [None] * (LAYERS + 1), [None] * LAYERS, [None] * LAYERS
    up, down = neighbours(N.dp)
    for level in reversed(range(LAYERS)):
        q, kv, attended, lse, a1, hat1, sp1, keep = saved[level]
        upper = min(level + 1, LAYERS - 1)
        vec = jnp.stack([scale_mlp[level], ln2_gain[level], scale_attn[level], ln1_gain[upper]])
        outs = backward_block(
            n, dp_size, LAYERS + level, source, above, fc1_weight[level], fc2_weight[level], proj_weight[level], vec, keep,
        )
        datt, fc1b, sums[level + 1] = outs[N.datt], outs[N.fc1b], outs[N.sums]
        if above:
            grads[level + 1] = [outs["up%d_out" % (i + 1)] for i in range(4)]
            dv_sums[level + 1] = outs[N.dv_sum][0]
        flip = [(i, i ^ 2) for i in range(dp_size)]
        above = {N.up4: outs[N.g4]}
        for name in "12":
            above[N.keep + name] = outs[N.keep + name + N._out]
            above[N.got + name] = lax.ppermute(outs[N.send + name + N._out], N.dp, flip)
        dq, dkv, q_sum = attend_bwd(
            q, *kv, idq, idk, lo, hi, attended, datt.reshape(rows, width), lse, *TILES
        )
        narrow[level] = (fc1b[0], q_sum[0])
        dkv = dkv.reshape((2, 3) + split + (width,))
        source = {
            N.dkv_in: dkv, N.dq: dq.reshape(split + (width,)), N.qkv: qkv2[level], N.hat1: hat1,
            N.gm: outs[N.gm_out], N.a1: a1, N.sp1: sp1,
        }
    pad = jnp.zeros((D - width,), F32)
    flat = jnp.concatenate(
        [jnp.zeros((D,), F32)]
        + [x for i in range(1, LAYERS) for x in (dv_sums[i], pad)]
        + [x for i in range(LAYERS) for x in narrow[i]]
    )
    own_rows = -(-flat.shape[0] // (8 * D)) * 8
    flat = jnp.pad(flat, (0, own_rows * D - flat.shape[0])).reshape(own_rows, D)
    wide = 8 * (LAYERS + 1)
    base = jnp.concatenate([jnp.zeros((8, D), F32)] + sums[1:] + [flat])
    tail = backward_tail(n, dp_size, 2 * LAYERS, wide, source, above, ln1_gain[:1], base, result)
    grads[0] = [tail["up%d_out" % (i + 1)] for i in range(4)]
    grad_tokens, total = tail[N.out], tail[N.total]
    dv_total = total[wide : wide + LAYERS, :width]
    flat = total[wide + LAYERS :].reshape(-1)[: LAYERS * (hidden + width)].reshape(LAYERS, hidden + width)
    fc1b_total, qv_total = flat[:, :hidden], jnp.stack([flat[:, hidden:], dv_total], axis=1)
    stacked = lambda parts: jnp.stack([x.astype(F32) for x in parts])
    big = [
        stacked([x[2] for x in grads]),
        stacked([x[3][:width] for x in grads]),
        stacked([x[1] for x in grads]),
        stacked([x[0] for x in grads]),
    ]
    total = total[:wide].reshape(LAYERS + 1, 8, D)
    upper, lower = total[1:], total[:-1]
    return (
        tail[N.out2].reshape(rows, D),
        grad_tokens.reshape(rows, D),
        lower[:, 6],
        lower[:, 7],
        big[0].reshape(LAYERS, D, 3, width),
        qv_total,
        big[1],
        upper[:, 5],
        upper[:, 4],
        upper[:, 2],
        upper[:, 3],
        big[2],
        fc1b_total,
        big[3],
        upper[:, 1],
        upper[:, 0],
    )


def solution(mesh):
    cols, stack_rows = P(None, None, N.tensor), P(None, N.tensor, None)
    qkv = P(None, None, None, N.tensor)
    return jax.shard_map(
        body,
        mesh=mesh,
        in_specs=(
            P(N.dp, None), P(N.dp), P(N.dp, None), P(), P(), qkv, cols, stack_rows, P(), P(), P(), P(), cols,
            P(None, N.tensor), stack_rows, P(), P(),
        ),
        out_specs=(
            P(N.dp, None), P(N.dp, None), P(), P(), qkv, cols, stack_rows, P(), P(), P(), P(), cols,
            P(None, N.tensor), stack_rows, P(), P(),
        ),
        check_vma=False,
    )
```

```python
import functools
import jax
import jax.numpy as jnp
from jax import lax
from jax.experimental import pallas as pl
from jax.experimental.pallas import tpu as pltpu
from jax.sharding import PartitionSpec as P

HD = 64
LAYERS = 2
D = 1024
MESH = pl.DeviceIdType.MESH
F32 = jnp.float32
BF16 = jnp.bfloat16
eps = 1e-06
half_root = 0.7071067811865476
density_scale = 0.3989422804014327
BIG = 1e30
TILES = (4, 512, 512, 256)
VMEM_LIMIT = 62 * 2**20


def bit_of(index, k):
    return (index // (1 << k)) % 2


def order_bits(nbits, half):
    return tuple(range(nbits)) if half == 0 else tuple(reversed(range(nbits)))


def compose(free_bits, free_value, fixed):
    index = sum(value * (1 << k) for k, value in fixed.items())
    for place, k in enumerate(free_bits):
        index = index + ((free_value >> place) & 1) * (1 << k)
    return index


class Names:
    def __getattr__(self, key):
        return key


N = Names()


class Exchange:
    def __init__(self, n, chunks, sub):
        self.n, self.chunks, self.sub = n, chunks, sub
        self.nbits = n.bit_length() - 1
        self.half = sub // 2
        self.me = lax.axis_index(N.tensor)
        self.bits = [bit_of(self.me, k) for k in range(self.nbits)]
        self.pending = []

    def partner(self, k):
        return self.me + (1 - 2 * self.bits[k]) * (1 << k)

    def partners(self):
        return [{N.tensor: self.partner(k)} for k in range(self.nbits)]

    def rows(self, h):
        return pl.ds(h * self.half, self.half)

    def copy(self, src, dst, sems, c, h, message, k):
        return pltpu.make_async_remote_copy(
            src_ref=src,
            dst_ref=dst,
            send_sem=sems.at[0, c, h, message],
            recv_sem=sems.at[1, c, h, message],
            device_id={N.tensor: self.partner(k)},
            device_id_type=MESH,
        )

    def rs_base(self, p):
        return sum(self.n >> (q + 1) for q in range(p))

    def rs_fixed(self, order, p, flip):
        fixed = {k: self.bits[k] for k in order[:p]}
        fixed[order[p]] = 1 - self.bits[order[p]] if flip else self.bits[order[p]]
        return fixed

    def rs_places(self, order, p, f):
        places = []
        for q in range(p):
            free = order[q + 1 :]
            index = 0
            for place, k in enumerate(free):
                at = order.index(k)
                if at < p:
                    value = self.bits[k]
                elif at == p:
                    value = 1 - self.bits[k]
                else:
                    value = (f >> (at - p - 1)) & 1
                index = index + value * (1 << place)
            places.append(self.rs_base(q) + index)
        return places

    def rs_send(self, part, recv, sems, c, p):
        for h in range(2):
            order = order_bits(self.nbits, h)
            free = order[p + 1 :]
            for f in range(1 << len(free)):
                b = compose(free, f, self.rs_fixed(order, p, True))
                message = self.rs_base(p) + f
                if p > 0:
                    total = part[b, c, self.rows(h), :].astype(F32)
                    for place in self.rs_places(order, p, f):
                        total = total + recv[c, place, self.rows(h), :].astype(F32)
                    part[b, c, self.rows(h), :] = total.astype(BF16)
                cp = self.copy(
                    part.at[b, c, self.rows(h), :],
                    recv.at[c, message, self.rows(h), :],
                    sems,
                    c,
                    h,
                    message,
                    order[p],
                )
                cp.start()
                self.pending.append(cp)

    def rs_wait(self, part, recv, sems, c, p):
        for h in range(2):
            order = order_bits(self.nbits, h)
            for f in range(self.n >> (p + 1)):
                message = self.rs_base(p) + f
                self.copy(
                    part.at[0, c, self.rows(h), :],
                    recv.at[c, message, self.rows(h), :],
                    sems,
                    c,
                    h,
                    message,
                    order[p],
                ).wait_recv()

    def rs_total(self, part, recv, c):
        halves = []
        for h in range(2):
            order = order_bits(self.nbits, h)
            total = part[self.me, c, self.rows(h), :].astype(F32)
            for p in range(self.nbits):
                free = order[p + 1 :]
                place = self.rs_base(p) + sum(
                    self.bits[k] * (1 << at) for at, k in enumerate(free)
                )
                total = total + recv[c, place, self.rows(h), :].astype(F32)
            halves.append(total)
        return jnp.concatenate(halves, axis=0)

    def ag_send(self, full, sems, c, p):
        for h in range(2):
            order = order_bits(self.nbits, h)
            fixed = {k: self.bits[k] for k in order[p:]}
            for f in range(1 << p):
                b = compose(order[:p], f, fixed)
                message = (1 << p) - 1 + f
                ref = full.at[b, c, self.rows(h), :]
                cp = self.copy(ref, ref, sems, c, h, message, order[p])
                cp.start()
                self.pending.append(cp)

    def ag_wait(self, full, sems, c, p):
        for h in range(2):
            order = order_bits(self.nbits, h)
            fixed = {k: self.bits[k] for k in order[p + 1 :]}
            fixed[order[p]] = 1 - self.bits[order[p]]
            for f in range(1 << p):
                b = compose(order[:p], f, fixed)
                message = (1 << p) - 1 + f
                ref = full.at[b, c, self.rows(h), :]
                self.copy(ref, ref, sems, c, h, message, order[p]).wait_recv()

    def drain(self):
        for cp in self.pending:
            cp.wait_send()
        self.pending = []


def erf(x):
    c = jnp.clip(x, -3.832506856900711, 3.832506856900711)
    s = c * c
    top = jnp.full_like(s, 0.00022905065861350646)
    for k in (0.0034082910107109506, 0.050955695062380861, 0.18520832239976145, 1.128379143519084):
        top = top * s + k
    low = jnp.full_like(s, -1.1791602954361697e-7)
    for k in (
        0.000023547966471313185,
        0.0010179625278914885,
        0.014070470171167667,
        0.11098505178285362,
        0.49746925110067538,
        1.0,
    ):
        low = low * s + k
    return c * top / low


def gelu_pair(before):
    cumulative = 0.5 * (1.0 + erf(before * half_root))
    density = jnp.exp(-0.5 * before * before) * density_scale
    return before * cumulative, cumulative + before * density


def normalised(stream):
    centre = jnp.mean(stream, axis=-1, keepdims=True)
    centred = stream - centre
    spread = lax.rsqrt(jnp.mean(centred * centred, axis=-1, keepdims=True) + eps)
    return centred * spread, spread


def norm_back(upstream, normed, spread, gain_row):
    scaled = upstream * gain_row
    return spread * (
        scaled
        - jnp.mean(scaled, axis=-1, keepdims=True)
        - normed * jnp.mean(scaled * normed, axis=-1, keepdims=True)
    )


def chunk_of(ref, c):
    x = ref[:, c]
    return x.reshape(x.shape[0] * x.shape[1], x.shape[2])


def column_loop(width, step, fn):
    if width <= step:
        fn(pl.ds(0, width))
    else:

        def one(j, carry):
            fn(pl.ds(pl.multiple_of(j * step, step), step))
            return carry

        lax.fori_loop(0, width // step, one, 0)


def matmul_nn(x, w_ref, cols):
    return jnp.dot(x, w_ref[:, cols], preferred_element_type=F32)


def matmul_nt(x, w_ref, cols):
    return lax.dot_general(
        x, w_ref[cols, :], (((1,), (1,)), ((), ())), preferred_element_type=F32
    )


def tall(ref, cols=slice(None)):
    x = ref[..., cols]
    return x.reshape(x.shape[0] * x.shape[1] * x.shape[2], x.shape[3])


def grad_items(left, right, out, first, step=256):
    width = left.shape[3]
    step = min(step, width)

    def item(at):
        y = lax.dot_general(
            tall(left, slice(at, at + step)), tall(right), (((0,), (0,)), ((), ())), preferred_element_type=F32
        )
        out[first + at : first + at + step, :] = y.astype(BF16)

    return [functools.partial(item, at) for at in range(0, width, step)]


def with_items(ex, stage, items):
    share = -(-len(items) // ex.chunks)

    def both(c):
        for item in items[c * share : (c + 1) * share]:
            item()
        stage(c)

    return both


def rs_stages(ex, part, recv, sems):
    stages = []
    for p in range(1, ex.nbits):

        def stage(c, p=p):
            ex.rs_wait(part, recv, sems, c, p - 1)
            ex.rs_send(part, recv, sems, c, p)

        stages.append(stage)
    return stages


def ag_stages(ex, full, sems):
    stages = []
    for p in range(1, ex.nbits):

        def stage(c, p=p):
            ex.ag_wait(full, sems, c, p - 1)
            ex.ag_send(full, sems, c, p)

        stages.append(stage)
    return stages


def sizes(rows, n):
    block = rows // n
    chunks = 3 if block % 96 == 0 else (2 if block % 64 == 0 else 1)
    return block, chunks, block // chunks


class Total:
    def __init__(self, bufs, recv, sems, dp_size, n, wide):
        self.bufs, self.recv, self.sems, self.wide = bufs, recv, sems, wide
        self.axes = [(N.dp, k) for k in range(dp_size.bit_length() - 1)]
        self.axes += [(N.tensor, k) for k in range(n.bit_length() - 1)]
        self.copies = []

    def target(self, i):
        axis, k = self.axes[i]
        me = lax.axis_index(axis)
        return {axis: me + (1 - 2 * bit_of(me, k)) * (1 << k)}

    def partners(self):
        return [self.target(i) for i, (axis, _) in enumerate(self.axes) if axis == N.dp]

    def start(self, i):
        cp = pltpu.make_async_remote_copy(
            src_ref=self.bufs.at[i],
            dst_ref=self.recv.at[i],
            send_sem=self.sems.at[0, i],
            recv_sem=self.sems.at[1, i],
            device_id=self.target(i),
            device_id_type=MESH,
        )
        cp.start()
        self.copies.append(cp)

    def step(self, i):
        self.copies[i].wait_recv()
        axis, _ = self.axes[i]
        total = self.bufs[i] + self.recv[i]
        if axis == N.tensor:
            row = lax.broadcasted_iota(jnp.int32, total.shape, 0)
            total = jnp.where(row < self.wide, total, self.bufs[i])
        self.bufs[i + 1] = total
        if i + 1 < len(self.axes):
            self.start(i + 1)

    def drain(self):
        for cp in self.copies:
            cp.wait_send()


def run_stages(ex, stages, extra=()):
    extra = sorted(extra, key=lambda pair: pair[0])
    slot = 0
    for stage in stages:
        for c in range(ex.chunks):
            while extra and extra[0][0] <= slot:
                extra.pop(0)[1]()
            stage(c)
            slot += 1
    for _, thunk in extra:
        thunk()


def meet(partners):
    sem = pltpu.get_barrier_semaphore()
    for partner in partners:
        pl.semaphore_signal(sem, inc=1, device_id=partner, device_id_type=MESH)
    pl.semaphore_wait(sem, len(partners))


class Refs:
    def __init__(self):
        self.loads, self.targets, self.stores = {}, {}, []

    def need(self, *names):
        for name in names:
            if name in self.loads:
                self.loads.pop(name).wait()

    def store(self, name, index=()):
        cp = pltpu.make_async_copy(
            getattr(self, name).at[index] if index else getattr(self, name),
            self.targets[name].at[index] if index else self.targets[name],
            self.store_sems.at[len(self.stores)],
        )
        cp.start()
        self.stores.append(cp)

    def finish(self):
        self.need(*list(self.loads))
        for cp in self.stores:
            cp.wait()


def call(kernel, name, collective_id, ins, outs, scratch, flops):
    late_in = [
        (k, jax.ShapeDtypeStruct(a.shape[1:] if type(late) is int else a.shape, a.dtype))
        for k, a, late in ins
        if late is True or type(late) is int
    ]
    late_out = [(k, shape, dtype) for k, shape, dtype, late in outs if late is True]

    def entry(*refs):
        refs = list(refs)
        take = lambda count: [refs.pop(0) for _ in range(count)]
        r = Refs()
        r.sources = {}
        in_refs, out_refs = take(len(ins)), take(len(outs))
        in_bufs, out_bufs = take(len(late_in)), take(len(late_out))
        load_sems, r.store_sems = take(2)
        bufs = {k: b for (k, _), b in zip(late_in, in_bufs)}
        for (k, _, late), ref in zip(ins, in_refs):
            if late == N.far:
                r.sources[k] = ref
                continue
            fetched = late is True or type(late) is int
            setattr(r, k, bufs[k] if fetched else ref)
            if fetched:
                cp = pltpu.make_async_copy(ref.at[late] if type(late) is int else ref, bufs[k], load_sems.at[len(r.loads)])
                cp.start()
                r.loads[k] = cp
        bufs = {k: b for (k, _, _), b in zip(late_out, out_bufs)}
        for (k, _), ref in zip(scratch, take(len(scratch))):
            setattr(r, k, ref)
        for (k, _, _, late), ref in zip(outs, out_refs):
            if late == N.far:
                r.targets[k] = ref
                continue
            setattr(r, k, getattr(r, late) if isinstance(late, str) else bufs[k] if late else ref)
            if late:
                r.targets[k] = ref
        kernel(r)
        r.finish()

    space = lambda late: pl.BlockSpec(memory_space=pltpu.VMEM if late is False else pl.ANY)
    result = pl.pallas_call(
        entry,
        out_shape=[jax.ShapeDtypeStruct(shape, dtype) for _, shape, dtype, _ in outs],
        in_specs=[space(late) for _, _, late in ins],
        out_specs=[space(late) for _, _, _, late in outs],
        scratch_shapes=[pltpu.VMEM(a.shape, a.dtype) for _, a in late_in]
        + [pltpu.VMEM(shape, dtype) for _, shape, dtype in late_out]
        + [pltpu.SemaphoreType.DMA((max(len(late_in), 1),)), pltpu.SemaphoreType.DMA((64,))]
        + [spec for _, spec in scratch],
        compiler_params=pltpu.CompilerParams(
            collective_id=collective_id, has_side_effects=True, vmem_limit_bytes=VMEM_LIMIT
        ),
        cost_estimate=pl.CostEstimate(flops=flops, bytes_accessed=10**8, transcendentals=0),
        name=name,
    )(*[a for _, a, _ in ins])
    return dict(zip([k for k, _, _, _ in outs], result))


def comm_scratch(n, chunks, sub, tag):
    return [
        (N.part + tag, pltpu.VMEM((n, chunks, sub, D), BF16)),
        (N.recv + tag, pltpu.VMEM((chunks, n - 1, sub, D), BF16)),
    ]


def sem_scratch(stages, n, chunks):
    return [(N.sems, pltpu.SemaphoreType.DMA((stages, 2, chunks, 2, n - 1)))]


class Halo:
    def __init__(self, sems, dp_size):
        self.sems, self.size = sems, dp_size
        self.me = lax.axis_index(N.dp)
        self.has = (self.me < dp_size - 1, self.me > 0)
        self.pending = []

    def partners(self):
        return [{N.dp: (self.me + step) % self.size} for step in (1, self.size - 1)]

    def copy(self, src, dst, way, message):
        step = 1 if way == 0 else -1
        return pltpu.make_async_remote_copy(
            src_ref=src,
            dst_ref=dst,
            send_sem=self.sems.at[0, way, message],
            recv_sem=self.sems.at[1, way, message],
            device_id={N.dp: self.me + step},
            device_id_type=MESH,
        )

    def send(self, src, dst, way, message):
        cp = self.copy(src, dst, way, message)

        @pl.when(self.has[way])
        def _():
            cp.start()

        self.pending.append((cp, way))

    def wait(self, dst, way, message):
        @pl.when(self.has[1 - way])
        def _():
            self.copy(dst, dst, way, message).wait_recv()

    def drain(self):
        for cp, way in self.pending:

            @pl.when(self.has[way])
            def _(cp=cp):
                cp.wait_send()


class GradSum:
    def __init__(self, arrays, sems, dp_size):
        self.arrays, self.sems = arrays, sems
        self.local = {}
        self.k = dp_size.bit_length() - 1
        self.me = lax.axis_index(N.dp)
        self.bits = [bit_of(self.me, k) for k in range(self.k)]
        self.pending = []

    def partner(self, k):
        return {N.dp: self.me + (1 - 2 * self.bits[k]) * (1 << k)}

    def partners(self):
        return [self.partner(k) for k in range(self.k)]

    def offset(self, rows, k):
        return sum(self.bits[i] * (rows >> (i + 1)) for i in range(k))

    def copy(self, src, dst, a, message, k):
        return pltpu.make_async_remote_copy(
            src_ref=src,
            dst_ref=dst,
            send_sem=self.sems.at[0, a, message],
            recv_sem=self.sems.at[1, a, message],
            device_id=self.partner(k),
            device_id_type=MESH,
        )

    def recv_rows(self, a, k):
        rows, _, _, _, start, _ = self.arrays[a]
        return (rows >> start) - (rows >> k)

    def here(self, a, at, size):
        rows, _, _, _, start, _ = self.arrays[a]
        return pl.ds(pl.multiple_of(at - self.offset(rows, start), 16), size)

    def add(self, a, base, size, k):
        rows, grad, recv, _, start, _ = self.arrays[a]
        step = 32 if size % 32 == 0 else 16

        def block(i, carry):
            at = base + i * step
            here = self.here(a, at, step)
            total = grad[here, :].astype(F32)
            for j in range(start, k):
                there = at - self.offset(rows, j + 1) + self.recv_rows(a, j)
                total = total + recv[pl.ds(pl.multiple_of(there, 16), step), :].astype(F32)
            grad[here, :] = total.astype(BF16)
            return carry

        lax.fori_loop(0, size // step, block, 0)

    def merge(self, a):
        rows, grad, _, _, start, pieces = self.arrays[a]
        size = rows >> start
        step = 32 if size % 32 == 0 else 16

        def block(i, carry):
            here = pl.ds(pl.multiple_of(i * step, 16), step)
            grad[here, :] = sum(x[here, :].astype(F32) for x in pieces).astype(BF16)
            return carry

        lax.fori_loop(0, size // step, block, 0)

    def send(self, a, k):
        rows, grad, recv, _, start, _ = self.arrays[a]
        size = rows >> (k + 1)
        base = self.offset(rows, k) + (1 - self.bits[k]) * size
        if k > start:
            self.add(a, base, size, k)
        cp = self.copy(
            grad.at[self.here(a, base, size), :], recv.at[pl.ds(self.recv_rows(a, k), size), :], a, k, k
        )
        cp.start()
        self.pending.append(cp)

    def wait(self, a, k):
        rows, _, recv, _, _, _ = self.arrays[a]
        ref = recv.at[pl.ds(self.recv_rows(a, k), rows >> (k + 1)), :]
        self.copy(ref, ref, a, k, k).wait_recv()

    def split(self, a, keep, send):
        rows, grad, recv, _, _, _ = self.arrays[a]
        size = rows >> 2
        step = 32 if size % 32 == 0 else 16
        for out, bit in ((keep, self.bits[1]), (send, 1 - self.bits[1])):

            def block(i, carry, out=out, bit=bit):
                at = bit * size + i * step
                mine = grad[pl.ds(pl.multiple_of(self.bits[0] * 2 * size + at, 16), step), :].astype(F32)
                total = mine + recv[pl.ds(pl.multiple_of(at, 16), step), :].astype(F32)
                out[pl.ds(pl.multiple_of(i * step, 16), step), :] = total.astype(BF16)
                return carry

            lax.fori_loop(0, size // step, block, 0)

    def own(self, a, k, mine):
        rows, _, _, out, _, _ = self.arrays[a]
        size = rows >> (k + 1)
        base = self.offset(rows, k + 1) if mine else self.offset(rows, k) + (1 - self.bits[k]) * size
        return out.at[pl.ds(pl.multiple_of(base, 16), size), :]

    def gather_send(self, a, k):
        ref = self.own(a, k, True)
        src = ref
        if k == self.k - 1:
            rows, grad = self.arrays[a][:2]
            src = grad.at[self.here(a, self.offset(rows, self.k), rows >> self.k), :]
            self.local[a] = pltpu.make_async_copy(src, ref, self.sems.at[0, a, 2 * self.k])
            self.local[a].start()
        elif k == self.k - 2:
            self.local[a].wait()
        cp = self.copy(src, ref, a, self.k + k, k)
        cp.start()
        self.pending.append(cp)

    def gather_wait(self, a, k):
        ref = self.own(a, k, False)
        self.copy(ref, ref, a, self.k + k, k).wait_recv()

    def steps(self, a):
        last, start = self.k - 1, self.arrays[a][4]

        def first():
            if start:
                self.merge(a)
            self.send(a, start)

        def halve(k):
            self.wait(a, k - 1)
            self.send(a, k)

        def turn():
            rows = self.arrays[a][0]
            self.wait(a, last)
            self.add(a, self.offset(rows, self.k), rows >> self.k, self.k)
            self.gather_send(a, last)

        def double(k):
            self.gather_wait(a, k + 1)
            self.gather_send(a, k)

        out = [first] + [functools.partial(halve, k) for k in range(start + 1, self.k)] + [turn]
        out += [functools.partial(double, k) for k in reversed(range(last))]
        return out + [functools.partial(self.gather_wait, a, 0)]

    def drain(self):
        for cp in self.pending:
            cp.wait_send()


def grad_scratch(shapes, dp_size):
    steps = 2 * (dp_size.bit_length() - 1) + 1
    out = [
        ("grad_recv%d" % i, pltpu.VMEM(((rows >> start) - rows // dp_size, cols), BF16))
        for i, (rows, cols, start) in enumerate(shapes)
    ]
    return out + [(N.grad_sems, pltpu.SemaphoreType.DMA((2, len(shapes), steps)))]


def grad_rows(rows, dp_size):
    unit = 16 * dp_size
    return -(-rows // unit) * unit


def placed(steps, slots):
    slots = list(slots)
    while len(slots) < len(steps):
        slots.append(slots[-1] + 2)
    return list(zip(slots, steps))


def forward_kernel(n, dp_size, chunks, sub, last, r):
    ex = Exchange(n, chunks, sub)
    if last:
        meet(ex.partners())
    else:
        halo = Halo(r.halo_sems, dp_size)
        meet(ex.partners() + halo.partners())
    sems = r.sems
    row = lambda i: r.vec[i : i + 1, :]
    full2 = None if last else r.a1

    def pre(c):
        r.need(N.proj)

        def cols(j):
            y = matmul_nn(chunk_of(r.attended, c), r.proj, j)
            r.part1[:, c, :, j] = y.astype(BF16).reshape(n, sub, -1)

        column_loop(D, 256, cols)
        ex.rs_send(r.part1, r.recv1, sems.at[0], c, 0)

    def own1(c):
        r.need(N.stream)
        ex.rs_wait(r.part1, r.recv1, sems.at[0], c, ex.nbits - 1)
        u1 = ex.rs_total(r.part1, r.recv1, c) + row(0)
        r.u1[c] = u1
        middle = r.stream[c] + row(1) * u1
        r.stream[c] = middle
        hat, spread = normalised(middle)
        r.hat2[c] = hat
        r.sp2[c] = spread
        r.a2[ex.me, c] = (hat * row(2) + row(3)).astype(BF16)
        ex.ag_send(r.a2, sems.at[1], c, 0)
        r.store(N.u1, (c,))
        r.store(N.hat2, (c,))

    def mid(c):
        r.need(N.fc1, N.fc2)
        ex.ag_wait(r.a2, sems.at[1], c, ex.nbits - 1)

        def hidden(j):
            before = matmul_nn(chunk_of(r.a2, c), r.fc1, j) + r.fc1_bias[:, j]
            a, s = gelu_pair(before)
            r.act[:, c, :, j] = a.astype(BF16).reshape(n, sub, -1)
            r.slope[:, c, :, j] = s.astype(BF16).reshape(n, sub, -1)

        column_loop(r.fc1.shape[1], 256, hidden)

        def cols(j):
            y = matmul_nn(chunk_of(r.act, c), r.fc2, j)
            r.part2[:, c, :, j] = y.astype(BF16).reshape(n, sub, -1)

        column_loop(D, 256, cols)
        ex.rs_send(r.part2, r.recv2, sems.at[2], c, 0)
        for name in (N.a2, N.act, N.slope):
            r.store(name, (slice(None), c))

    def own2(c):
        ex.rs_wait(r.part2, r.recv2, sems.at[2], c, ex.nbits - 1)
        u2 = ex.rs_total(r.part2, r.recv2, c) + row(4)
        r.u2[c] = u2
        after = r.stream[c] + row(5) * u2
        r.after[c] = after.astype(r.after.dtype)
        r.store(N.after, (c,))
        r.store(N.u2, (c,))
        if not last:
            hat, spread = normalised(after)
            r.hat1[c] = hat
            r.sp1[c] = spread
            full2[ex.me, c] = (hat * row(6) + row(7)).astype(BF16)
            r.store(N.hat1, (c,))
            ex.ag_send(full2, sems.at[3], c, 0)

    def post(c):
        ex.ag_wait(full2, sems.at[3], c, ex.nbits - 1)
        r.need(N.qkv)
        x = chunk_of(full2, c)
        width = r.q.shape[3]
        for i, name in ((1, N.k), (2, N.v), (0, N.q)):
            y = jnp.dot(x, r.qkv[i], preferred_element_type=F32)
            if i != 1:
                y = y + r.qv_bias[i // 2 : i // 2 + 1, :]
            getattr(r, name)[:, c] = y.astype(BF16).reshape(n, sub, width)
            r.store(name, (slice(None), c))
            if i:
                for way in range(2):
                    halo.send(
                        getattr(r, name).at[:, c], r.targets[name + N._near].at[way, :, c], way, (i - 1) * chunks + c
                    )
        r.store(N.a1, (slice(None), c))

    run_stages(
        ex,
        [pre]
        + rs_stages(ex, r.part1, r.recv1, sems.at[0])
        + [own1]
        + ag_stages(ex, r.a2, sems.at[1])
        + [mid]
        + rs_stages(ex, r.part2, r.recv2, sems.at[2])
        + [own2]
        + ([] if last else ag_stages(ex, full2, sems.at[3]) + [post]),
    )
    if not last:
        for i, name in enumerate((N.k_near, N.v_near)):
            for c in range(chunks):
                for way in range(2):
                    halo.wait(r.targets[name].at[way, :, c], way, i * chunks + c)
        halo.drain()
    ex.drain()


def first_kernel(n, dp_size, chunks, sub, r):
    halo = Halo(r.halo_sems, dp_size)
    meet(halo.partners())
    me = lax.axis_index(N.tensor)
    r.need(N.tokens, N.qkv)
    width = r.q.shape[3]
    for c in range(chunks):

        def norm(b, carry, c=c):
            hat, _ = normalised(r.tokens[b, c].astype(F32))
            r.a1[b, c] = (hat * r.vec[0:1, :] + r.vec[1:2, :]).astype(BF16)
            return carry

        lax.fori_loop(0, n, norm, 0)
        x = chunk_of(r.a1, c)
        for i, name in ((1, N.k), (2, N.v), (0, N.q)):
            y = jnp.dot(x, r.qkv[i], preferred_element_type=F32)
            if i != 1:
                y = y + r.qv_bias[i // 2 : i // 2 + 1, :]
            getattr(r, name)[:, c] = y.astype(BF16).reshape(n, sub, width)
            r.store(name, (slice(None), c))
            if i:
                for way in range(2):
                    halo.send(
                        getattr(r, name).at[:, c], r.targets[name + N._near].at[way, :, c], way, (i - 1) * chunks + c
                    )
        r.store(N.a1, (slice(None), c))
        own = r.tokens[me, c].astype(F32)
        r.after[c] = own
        hat, spread = normalised(own)
        r.hat1[c] = hat
        r.sp1[c] = spread
    for i, name in enumerate((N.k_near, N.v_near)):
        for c in range(chunks):
            for way in range(2):
                halo.wait(r.targets[name].at[way, :, c], way, i * chunks + c)
    halo.drain()


def first_block(n, dp_size, collective_id, tokens, qkv, qv_bias, vec):
    rows = tokens.shape[0]
    _, chunks, sub = sizes(rows, n)
    width = qv_bias.shape[1]
    split = lambda cols: (n, chunks, sub, cols)
    mine = (chunks, sub, D)
    outs = [(N.after, mine, F32, False), (N.hat1, mine, F32, False), (N.sp1, (chunks, sub, 1), F32, False)]
    outs += [(N.a1, split(D), BF16, True)] + [(k, split(width), BF16, True) for k in (N.q, N.k, N.v)]
    outs += [(k, (2,) + split(width), BF16, N.far) for k in (N.k_near, N.v_near)]
    return call(
        functools.partial(first_kernel, n, dp_size, chunks, sub),
        N.first_block,
        collective_id,
        [(N.tokens, tokens.reshape(split(D)), True), (N.qkv, qkv, 0), (N.qv_bias, qv_bias, False), (N.vec, vec, False)],
        outs,
        [(N.halo_sems, pltpu.SemaphoreType.DMA((2, 2, 2 * chunks)))],
        2 * rows * D * 3 * width,
    )


def forward_block(n, dp_size, last, level, attended, proj, fc1, fc2, fc1_bias, vec, stream, qkv=None, qv_bias=None):
    rows, width = attended.shape
    block, chunks, sub = sizes(rows, n)
    hidden = fc1.shape[2]
    split = lambda cols: (n, chunks, sub, cols)
    mine = (chunks, sub, D)
    ins = [
        (N.attended, attended.reshape(split(width)), False), (N.proj, proj, level), (N.stream, stream.reshape(mine), True),
        (N.fc1, fc1, level), (N.fc2, fc2, level), (N.fc1_bias, fc1_bias, False), (N.vec, vec, False),
    ]
    outs = [
        (N.u1, mine, F32, True), (N.hat2, mine, F32, True), (N.sp2, (chunks, sub, 1), F32, False),
        (N.u2, mine, F32, True), (N.a2, split(D), BF16, True), (N.act, split(hidden), BF16, True),
        (N.slope, split(hidden), BF16, True),
    ]
    scratch = comm_scratch(n, chunks, sub, "1") + comm_scratch(n, chunks, sub, "2")
    if last:
        outs += [(N.after, mine, BF16, True)]
    else:
        ins += [(N.qkv, qkv, level + 1), (N.qv_bias, qv_bias, False)]
        outs += [(N.after, mine, F32, True), (N.hat1, mine, F32, True), (N.sp1, (chunks, sub, 1), F32, False)]
        outs += [(N.a1, split(D), BF16, True)] + [(k, split(width), BF16, True) for k in N.qkv]
        outs += [(k, (2,) + split(width), BF16, N.far) for k in (N.k_near, N.v_near)]
        scratch += [(N.halo_sems, pltpu.SemaphoreType.DMA((2, 2, 2 * chunks)))]
    return call(
        functools.partial(forward_kernel, n, dp_size, chunks, sub, last),
        N.forward_last if last else N.forward_block,
        level,
        ins,
        outs,
        scratch + sem_scratch(4, n, chunks),
        2 * rows * D * (2 * hidden + 4 * width),
    )


def add_rows(ref, i, value):
    ref[i : i + 1, :] += jnp.sum(value, axis=0, keepdims=True)


def input_norm_own(ex, r, c, gain, sums):
    r.need(N.hat1, N.gm)
    ex.rs_wait(r.part, r.recv, r.sems.at[0], c, ex.nbits - 1)
    da1 = ex.rs_total(r.part, r.recv, c)
    add_rows(sums, 6, da1 * r.hat1[c])
    add_rows(sums, 7, da1)
    return r.gm[c] + norm_back(da1, r.hat1[c], r.sp1[c], gain)


def send_home(halo, r, chunks):
    cp = pltpu.make_async_copy(r.sources[N.dkv_in].at[:, 1], r.dkv, r.dkv_sem)
    cp.start()
    r.loads[N.dkv] = cp
    for c in range(chunks):
        for way in range(2):
            for i in range(2):
                src = r.sources[N.dkv_in].at[i, 2 - 2 * way, :, c]
                halo.send(src, near_part(r, way, i, c), way, 2 * c + i)


def near_part(r, way, i, c):
    width = r.dq.shape[3]
    return r.near.at[:, c, :, pl.ds((2 * way + i) * width, width)]


def input_grad_chunk(ex, halo, r, c):
    r.need(N.dq, N.dkv, N.qkv)
    width = r.dq.shape[3]
    for way in range(2):
        for i in range(2):
            halo.wait(near_part(r, way, i, c), way, 2 * c + i)
    r.dqkv[:, c, :, :width] = r.dq[:, c]
    for i in range(2):
        cols = slice((i + 1) * width, (i + 2) * width)

        for b in range(ex.n):
            r.total_kv[...] = r.dkv[i, b, c].astype(F32)
            for way in range(2):

                @pl.when(halo.has[1 - way])
                def _():
                    first = (2 * way + i) * width
                    r.total_kv[...] += r.near[b, c, :, first : first + width].astype(F32)

            total = r.total_kv[...]
            if i:
                r.dv_sum[...] += jnp.sum(total, axis=0, keepdims=True)
            r.dqkv[b, c, :, cols] = total.astype(BF16)

    def cols(j):
        x = chunk_of(r.dqkv, c)
        y = sum(
            lax.dot_general(
                x[:, i * width : (i + 1) * width], r.qkv[i, j, :], (((1,), (1,)), ((), ())), preferred_element_type=F32
            )
            for i in range(3)
        )
        r.part[:, c, :, j] = y.astype(BF16).reshape(ex.n, ex.sub, -1)

    column_loop(D, 256, cols)
    ex.rs_send(r.part, r.recv, r.sems.at[0], c, 0)


def backward_kernel(n, dp_size, chunks, sub, first, r):
    ex = Exchange(n, chunks, sub)
    sems, part, recv = r.sems, r.part, r.recv
    row = lambda i: r.vec[i : i + 1, :]
    if first:
        meet(ex.partners() + [{N.dp: dp_partner(0)}, {N.dp: dp_partner(1)}])
    else:
        halo = Halo(r.halo_sems, dp_size)
        gs = GradSum(upper_arrays(r), r.grad_sems, dp_size)
        meet(ex.partners() + gs.partners() + halo.partners())
        r.near = r.e1
        send_home(halo, r, chunks)
        r.dv_sum[...] = jnp.zeros_like(r.dv_sum)
    first_arrays = [(x.shape[0], x, recv, None, 0, ()) for x, recv in ((r.g1, r.core_recv0), (r.g2, r.core_recv1))]
    first_sum = GradSum(first_arrays, r.core_sems, dp_size)
    r.sums[...] = jnp.zeros_like(r.sums)
    r.fc1b[...] = jnp.zeros_like(r.fc1b)
    width, hidden_size = r.proj.shape[0], r.fc1.shape[1]
    if r.g4.shape[0] > width:
        r.g4[width:, :] = jnp.zeros((r.g4.shape[0] - width, D), BF16)

    def pre(c):
        input_grad_chunk(ex, halo, r, c)

    def own0(c):
        r.need(N.u2)
        g = input_norm_own(ex, r, c, row(3), r.sums)
        add_rows(r.sums, 0, g * r.u2[c])
        add_rows(r.sums, 1, g * row(0))
        r.gm[c] = g
        r.full[ex.me, c] = (g * row(0)).astype(BF16)
        ex.ag_send(r.full, sems.at[1], c, 0)

    def mid(c):
        r.need(N.fc1, N.fc2, N.slope, N.full, N.u2, N.gm)
        if not first and c == 0:
            ex.drain()
        if first:
            g = r.gm[c]
            add_rows(r.sums, 0, g * r.u2[c])
            add_rows(r.sums, 1, g * row(0))
        else:
            ex.ag_wait(r.full, sems.at[1], c, ex.nbits - 1)

        def hidden(j):
            y = matmul_nt(chunk_of(r.full, c), r.fc2, j)
            w = y.shape[1]
            db = y * r.slope[:, c, :, j].astype(F32).reshape(n * sub, w)
            r.fc1b[:, j] += jnp.sum(db, axis=0, keepdims=True)
            r.slope[:, c, :, j] = db.astype(BF16).reshape(n, sub, w)

        column_loop(hidden_size, 256, hidden)

        def cols(j):
            y = matmul_nt(chunk_of(r.slope, c), r.fc1, j)
            part[:, c, :, j] = y.astype(BF16).reshape(n, sub, -1)

        column_loop(D, 256, cols)
        ex.rs_send(part, recv, sems.at[2], c, 0)

    def own1(c):
        r.need(N.hat2, N.u1)
        ex.rs_wait(part, recv, sems.at[2], c, ex.nbits - 1)
        da2 = ex.rs_total(part, recv, c)
        hat = r.hat2[c]
        add_rows(r.sums, 2, da2 * hat)
        add_rows(r.sums, 3, da2)
        gm = r.gm[c] + norm_back(da2, hat, r.sp2[c], row(1))
        r.gm[c] = gm
        add_rows(r.sums, 4, gm * r.u1[c])
        add_rows(r.sums, 5, gm * row(2))
        r.e1[ex.me, c] = (gm * row(2)).astype(BF16)
        ex.ag_send(r.e1, sems.at[3], c, 0)
        r.store(N.gm_out, (c,))

    def post(c):
        r.need(N.proj)
        ex.ag_wait(r.e1, sems.at[3], c, ex.nbits - 1)
        y = matmul_nt(chunk_of(r.e1, c), r.proj, slice(None))
        r.datt[:, c] = y.astype(BF16).reshape(n, sub, -1)
        r.store(N.datt, (slice(None), c))

    stages, extra = [], []
    if not first:
        made = [lambda: r.need(N.a1)] + grad_items(r.a1, r.dqkv, r.up3, 0)
        stages = [pre] + rs_stages(ex, part, recv, sems.at[0]) + [own0] + ag_stages(ex, r.full, sems.at[1])
        stages[1] = with_items(ex, stages[1], made)
        r.act = r.a1.at[:, :, :, pl.ds(0, hidden_size)]

        def fetch_act():
            cp = pltpu.make_async_copy(r.sources[N.act], r.act, r.act_sem)
            cp.start()
            r.loads[N.act] = cp

        extra += [(2 * chunks, fetch_act)]
        extra += [(3, lambda: r.need(N.keep1, N.got1, N.keep2, N.got2, N.up4))]
        extra += placed_sums(gs)
    gathers = ag_stages(ex, r.e1, sems.at[3])
    sums2 = rs_stages(ex, part, recv, sems.at[2])
    sums2[0] = with_items(ex, sums2[0], [lambda: r.need(N.act)] + grad_items(r.act, r.full, r.g1, 0))
    made = [lambda: r.need(N.a2)] + grad_items(r.a2, r.slope, r.g2, 0)
    stages += [mid] + sums2 + [with_items(ex, own1, made)] + gathers + [post]
    end = len(stages) * chunks
    behind = end - chunks * (1 + len(gathers))

    def part_of(a):
        first_sum.wait(a, 0)
        names = ((N.keep1, N.send1), (N.keep2, N.send2))[a]
        first_sum.split(a, getattr(r, names[0] + N._out), getattr(r, names[1] + N._out))
        r.store(names[0] + N._out)
        if first:
            got = r.targets[(N.got1_out, N.got2_out)[a]]
            cp = first_sum.copy(getattr(r, names[1] + N._out), got, a, 1, 1)
            cp.start()
            first_sum.pending.append(cp)
            arrivals.append(cp)
        else:
            r.store(names[1] + N._out)

    arrivals = []
    extra += [(behind - chunks, lambda: first_sum.send(0, 0)), (behind - chunks + 1, lambda: part_of(0))]
    extra += [(behind, lambda: first_sum.send(1, 0)), (behind + 1, lambda: part_of(1))]
    run_stages(ex, stages, extra)
    r.need(N.attended)
    for item in grad_items(r.attended, r.e1, r.g4, 0):
        item()
    if not first:
        gs.drain()
        halo.drain()
    for cp in arrivals:
        cp.wait_recv()
    first_sum.drain()
    ex.drain()


def dp_partner(k):
    me = lax.axis_index(N.dp)
    return me + (1 - 2 * bit_of(me, k)) * (1 << k)


def tail_sums(gs):
    return (
        placed(gs.steps(0), (3, 6, 10, 13, 16))
        + placed(gs.steps(1), (4, 9, 13, 15.5, 17))
        + placed(gs.steps(2), (6, 7, 9, 12, 15, 16, 18))
        + placed(gs.steps(3), (3, 5, 7, 10, 12, 14, 17))
    )


def placed_sums(gs):
    return (
        placed(gs.steps(0), (3, 9, 15, 21, 25))
        + placed(gs.steps(1), (4, 10, 16, 22, 26))
        + placed(gs.steps(2), (6, 7, 11, 17, 20, 24, 27))
        + placed(gs.steps(3), (3, 5, 8, 12, 14, 18, 23))
    )


def upper_arrays(r):
    pieces = ((r.keep1, r.got1), (r.keep2, r.got2), (), ())
    return [
        (
            r.targets["up%d_out" % (i + 1)].shape[0],
            getattr(r, "up%d" % (i + 1)),
            getattr(r, "grad_recv%d" % i),
            r.targets["up%d_out" % (i + 1)],
            2 if x else 0,
            x,
        )
        for i, x in enumerate(pieces)
    ]


def upper_buffers(above, width, dp_size):
    shapes = [(4 * x.shape[0], x.shape[1]) for x in (above[N.keep1], above[N.keep2])]
    shapes += [(D, 3 * width), above[N.up4].shape]
    scratch = [(N.up1, pltpu.VMEM(above[N.keep1].shape, BF16)), (N.up2, pltpu.VMEM(above[N.keep2].shape, BF16))]
    scratch += [(N.up3, pltpu.VMEM(shapes[2], BF16))]
    scratch += grad_scratch([x + (start,) for x, start in zip(shapes, (2, 2, 0, 0))], dp_size)
    return scratch, [("up%d_out" % (i + 1), x, BF16, N.far) for i, x in enumerate(shapes)]


def home_buffers(n, chunks, sub, width):
    split = (n, chunks, sub)
    return [
        (N.dqkv, pltpu.VMEM(split + (3 * width,), BF16)),
        (N.total_kv, pltpu.VMEM((sub, width), F32)),
        (N.dkv, pltpu.VMEM((2,) + split + (width,), BF16)),
        (N.dkv_sem, pltpu.SemaphoreType.DMA),
        (N.halo_sems, pltpu.SemaphoreType.DMA((2, 2, 2 * chunks))),
    ]


def backward_block(n, dp_size, collective_id, source, above, fc1, fc2, proj, vec, saved):
    first = not above
    _, chunks, sub, hidden = saved[N.slope].shape
    width = proj[0].shape[1]
    split = lambda cols: (n, chunks, sub, cols)
    mine = (chunks, sub, D)
    ins = list(source.items()) + list(above.items()) + [(N.fc2, fc2), (N.slope, saved[N.slope]), (N.fc1, fc1)]
    ins += [(k, saved[k]) for k in (N.u2, N.act, N.a2, N.hat2, N.u1, N.sp2, N.attended)] + [(N.proj, proj), (N.vec, vec)]
    outs = [
        (N.datt, split(width), BF16, True), (N.gm_out, mine, F32, N.gm), (N.sums, (8, D), F32, False),
        (N.fc1b, (1, hidden), F32, False), (N.g4, (grad_rows(width, dp_size), D), BF16, False),
    ]
    quarters = []
    for i, (rows, cols) in enumerate(((hidden, D), (D, hidden))):
        keep, send, got = ((N.keep1_out, N.send1_out, N.got1_out), (N.keep2_out, N.send2_out, N.got2_out))[i]
        quarter = (rows // 4, cols)
        outs += [(keep, quarter, BF16, True)]
        if first:
            quarters += [(send, pltpu.VMEM(quarter, BF16))]
            outs += [(got, quarter, BF16, N.far)]
        else:
            outs += [(send, quarter, BF16, True)]
    scratch = quarters + comm_scratch(n, chunks, sub, "") + [(N.e1, pltpu.VMEM(split(D), BF16))] + sem_scratch(4, n, chunks)
    scratch += [(N.g1, pltpu.VMEM((hidden, D), BF16)), (N.g2, pltpu.VMEM((D, hidden), BF16))]
    scratch += [(N.core_recv0, pltpu.VMEM((hidden // 2, D), BF16)), (N.core_recv1, pltpu.VMEM((D // 2, hidden), BF16))]
    scratch += [(N.core_sems, pltpu.SemaphoreType.DMA((2, 2, 2 * (dp_size.bit_length() - 1))))]
    if not first:
        scratch += [(N.act_sem, pltpu.SemaphoreType.DMA)]
        scratch += [(N.full, pltpu.VMEM(split(D), BF16))] + home_buffers(n, chunks, sub, width)
        more, results = upper_buffers(above, width, dp_size)
        scratch += more
        outs += results + [(N.dv_sum, (1, width), F32, False)]
    return call(
        functools.partial(backward_kernel, n, dp_size, chunks, sub, first),
        N.backward_first if first else N.backward_block,
        collective_id,
        [placed_input(k, a) if first or k != N.act else (k, a, N.far) for k, a in ins],
        outs,
        scratch,
        2 * n * chunks * sub * D * (2 * hidden + 4 * width),
    )


def placed_input(name, array):
    return (name,) + (array if isinstance(array, tuple) else (array, lateness(name)))


def lateness(name):
    if name == N.dkv_in:
        return N.far
    return name not in (N.sp1, N.sp2, N.vec, N.base)


def tail_kernel(n, dp_size, chunks, sub, wide, r):
    ex = Exchange(n, chunks, sub)
    small = Total(r.bufs, r.small_recv, r.small_sems, dp_size, n, wide)
    gs = GradSum(upper_arrays(r), r.grad_sems, dp_size)
    halo = Halo(r.halo_sems, dp_size)
    meet(ex.partners() + gs.partners() + halo.partners())
    r.near = r.full
    send_home(halo, r, chunks)
    sems = r.sems
    r.dv_sum[...] = jnp.zeros_like(r.dv_sum)
    r.sums[...] = jnp.zeros_like(r.sums)

    def pre(c):
        input_grad_chunk(ex, halo, r, c)

    def own(c):
        g = input_norm_own(ex, r, c, r.vec[0:1, :], r.sums)
        r.full[ex.me, c] = g.astype(BF16)
        ex.ag_send(r.full, sems.at[1], c, 0)
        if c == chunks - 1:
            r.bufs[0] = r.base[...]
            r.bufs[0, 0:8, :] = r.sums[...]
            r.bufs[0, wide : wide + 1, : r.dv_sum.shape[1]] = r.dv_sum[...]
            small.start(0)

    def post(c):
        ex.ag_wait(r.full, sems.at[1], c, ex.nbits - 1)
        r.store(N.out, (slice(None), c))

    made = [lambda: r.need(N.a1)] + grad_items(r.a1, r.dqkv, r.up3, 0)
    stages = [pre] + rs_stages(ex, r.part, r.recv, sems.at[0]) + [own] + ag_stages(ex, r.full, sems.at[1]) + [post]
    stages[1] = with_items(ex, stages[1], made)
    after_own = chunks * (2 + ex.nbits - 1)
    extra = [(3, lambda: r.need(N.keep1, N.got1, N.keep2, N.got2, N.up4))]
    extra += tail_sums(gs)

    def spread(c, p):
        if p == 0:
            r.need(N.result)
            r.full3[ex.me, c] = r.result[c]
        else:
            ex.ag_wait(r.full3, sems.at[2], c, p - 1)
        if p < ex.nbits:
            ex.ag_send(r.full3, sems.at[2], c, p)
        else:
            r.store(N.out2, (slice(None), c))

    for p in range(ex.nbits + 1):
        slot = after_own + chunks * ex.nbits if p == ex.nbits else chunks * (1 + 2 * p)
        extra += [(slot + c, functools.partial(spread, c, p)) for c in range(chunks)]
    extra += [(after_own + 1 + i, functools.partial(small.step, i)) for i in range(len(small.axes))]
    run_stages(ex, stages, extra)
    halo.drain()
    r.total[...] = r.bufs[len(small.axes)]
    ex.drain()
    small.drain()
    gs.drain()


def backward_tail(n, dp_size, collective_id, wide, source, above, vec, base, result):
    _, chunks, sub, width = source[N.dq].shape
    split = lambda cols: (n, chunks, sub, cols)
    steps = (n * dp_size).bit_length() - 1
    ins = list(source.items()) + list(above.items()) + [(N.vec, vec), (N.base, base), (N.result, result)]
    more, results = upper_buffers(above, width, dp_size)
    outs = [(N.out, split(D), BF16, N.full), (N.out2, split(D), BF16, N.full3), (N.total, base.shape, F32, False)] + results
    scratch = comm_scratch(n, chunks, sub, "") + sem_scratch(3, n, chunks) + home_buffers(n, chunks, sub, width)
    scratch += [(N.full3, pltpu.VMEM(split(D), BF16))]
    scratch += [(N.full, pltpu.VMEM(split(D), BF16)), (N.sums, pltpu.VMEM((8, D), F32)), (N.dv_sum, pltpu.VMEM((1, width), F32))]
    scratch += [(N.bufs, pltpu.VMEM((steps + 1,) + base.shape, F32)), (N.small_recv, pltpu.VMEM((steps,) + base.shape, F32))]
    scratch += [(N.small_sems, pltpu.SemaphoreType.DMA((2, steps)))] + more
    return call(
        functools.partial(tail_kernel, n, dp_size, chunks, sub, wide),
        N.backward_tail,
        collective_id,
        [placed_input(k, a) for k, a in ins],
        outs,
        scratch,
        2 * n * chunks * sub * D * 3 * width,
    )


def id_features(ids_col, query_side):
    lane = lax.broadcasted_iota(jnp.int32, (ids_col.shape[0], HD), 1)
    bit = (ids_col >> (lane & 15)) & 1
    first = lane < 16
    second = (lane >= 16) & (lane < 32)
    inv = 1 - bit
    if query_side:
        v = jnp.where(first, bit, jnp.where(second, inv, 0)).astype(F32) * (-BIG)
    else:
        v = jnp.where(first, inv, jnp.where(second, bit, 0)).astype(F32)
    return v

def each_tile(KB, t_lo, t_hi, kn_ref, vn_ref, k_ref, v_ref, fn):
    per = k_ref.shape[0] // KB
    for segment in range(3):
        def one(t, carry, segment=segment):
            here = pl.ds(pl.multiple_of((t - segment * per) * KB, KB), KB)
            if segment == 1:
                fn(t, here, k_ref[here, :], v_ref[here, :])
            else:
                fn(t, here, kn_ref[segment // 2, here, :], vn_ref[segment // 2, here, :])
            return carry
        lax.fori_loop(jnp.maximum(t_lo, segment * per), jnp.minimum(t_hi, (segment + 1) * per), one, 0)

def fwd_kernel(HH, QB, KB, KT, nq, lo_ref, hi_ref, q_ref, kn_ref, vn_ref, k_ref, v_ref, idq_ref, idk_ref, o_ref, lse_ref, kaug, vt, qaug):
    t_lo = lo_ref[nq]
    t_hi = hi_ref[nq]
    def prep(t, here, kk, vv):
        r = pl.ds(pl.multiple_of(t * KT, KT), KT)
        feat = id_features(idk_ref[r, :], False).astype(BF16)
        for h in range(HH):
            kaug[h, r, :] = jnp.concatenate([kk[:, h * HD:(h + 1) * HD], feat], axis=1)
        vt[:, r] = vv.T
    each_tile(KT, t_lo, t_hi, kn_ref, vn_ref, k_ref, v_ref, prep)
    def qprep(t, _):
        r = pl.ds(pl.multiple_of(t * QB, QB), QB)
        feat = id_features(idq_ref[r, :], True).astype(BF16)
        qq = (q_ref[r, :] * BF16(0.125))
        for h in range(HH):
            qaug[h, :, r] = jnp.concatenate([qq[:, h * HD:(h + 1) * HD], feat], axis=1).T
        return 0
    lax.fori_loop(0, nq, qprep, 0)
    def qloop(qb, _):
        rq = pl.ds(pl.multiple_of(qb * QB, QB), QB)
        lo = lo_ref[qb]
        qts = [qaug[h, :, rq] for h in range(HH)]
        def kloop(t, c):
            r = pl.ds(pl.multiple_of(lo * KT + t * KB, KT), KB)
            new = []
            for h in range(HH):
                m, l, acc = c[h]
                s = jnp.dot(kaug[h, r, :], qts[h], preferred_element_type=F32)
                mn = jnp.maximum(m, jnp.max(s, axis=0, keepdims=True))
                p = jnp.exp(s - mn)
                al = jnp.exp(m - mn)
                l = l * al + jnp.sum(p, axis=0, keepdims=True)
                acc = acc * al + jnp.dot(vt[h * HD:(h + 1) * HD, r], p.astype(BF16), preferred_element_type=F32)
                new.append((mn, l, acc))
            return tuple(new)
        z = (jnp.full((1, QB), -3e38, F32), jnp.zeros((1, QB), F32), jnp.zeros((HD, QB), F32))
        c = lax.fori_loop(0, (hi_ref[qb] - lo) // (KB // KT), kloop, (z,) * HH)
        both = jnp.concatenate([c[h][2] / c[h][1] for h in range(HH)], axis=0)
        o_ref[rq, :] = both.T.astype(BF16)
        for h in range(HH):
            lse_ref[0, h:h + 1, rq] = c[h][0] + jnp.log(c[h][1])
        return 0
    lax.fori_loop(0, nq, qloop, 0)

def attend_fwd(q, kn, vn, k, v, idq, idk, lo, hi, HH, QB, KB, KT):
    n, cols = q.shape
    w = 3 * n
    HH = min(HH, cols // HD)
    wide = HH * HD
    near = pl.BlockSpec((2, n, wide), lambda g, *_: (0, 0, g))
    pairs = cols // wide
    nq = n // QB
    return pl.pallas_call(
        functools.partial(fwd_kernel, HH, QB, KB, KT, nq),
        grid_spec=pltpu.PrefetchScalarGridSpec(
            num_scalar_prefetch=2, grid=(pairs,),
            in_specs=[pl.BlockSpec((n, wide), lambda g, *_: (0, g)), near, near, pl.BlockSpec((n, wide), lambda g, *_: (0, g)), pl.BlockSpec((n, wide), lambda g, *_: (0, g)),
                      pl.BlockSpec((n, 1), lambda g, *_: (0, 0)), pl.BlockSpec((w, 1), lambda g, *_: (0, 0))],
            out_specs=[pl.BlockSpec((n, wide), lambda g, *_: (0, g)), pl.BlockSpec((1, HH, n), lambda g, *_: (g, 0, 0))],
            scratch_shapes=[pltpu.VMEM((HH, w, 128), BF16), pltpu.VMEM((wide, w), BF16), pltpu.VMEM((HH, 128, n), BF16)]),
        out_shape=[jax.ShapeDtypeStruct((n, cols), BF16), jax.ShapeDtypeStruct((pairs, HH, n), F32)],
        compiler_params=pltpu.CompilerParams(vmem_limit_bytes=VMEM_LIMIT),
        cost_estimate=pl.CostEstimate(flops=5 * 10**10, bytes_accessed=10**8, transcendentals=0),
        name=N.attend_fwd,
    )(lo, hi, q, kn, vn, k, v, idq, idk)

def bwd_kernel(HH, QB, KB, KT, nq, lo_ref, hi_ref, q_ref, kn_ref, vn_ref, k_ref, v_ref, idq_ref, idk_ref, o_ref, g_ref, lse_ref, dq_ref, dkv_ref, qsum_ref, kaug, vaug, kt, qaug, gaug, acc):
    w = 3 * k_ref.shape[0]
    t_lo = lo_ref[nq]
    t_hi = hi_ref[nq]
    wide = HH * HD
    lane = lax.broadcasted_iota(jnp.int32, (KT, HD), 1)
    three = ((lane >= 32) & (lane < 35))
    def zero(t, _):
        r = pl.ds(pl.multiple_of(t * KT, KT), KT)
        for i in range(2):
            dkv_ref[i, r, :] = jnp.zeros((KT, wide), BF16)
        return 0
    lax.fori_loop(0, w // KT, zero, 0)
    def prep(t, here, kk, vv):
        r = pl.ds(pl.multiple_of(t * KT, KT), KT)
        feat = jnp.where(three, 1.0, id_features(idk_ref[r, :], False)).astype(BF16)
        ones = jnp.where(three, 1.0, 0.0).astype(BF16)
        for h in range(HH):
            kaug[h, r, :] = jnp.concatenate([kk[:, h * HD:(h + 1) * HD], feat], axis=1)
            vaug[h, r, :] = jnp.concatenate([vv[:, h * HD:(h + 1) * HD], ones], axis=1)
            acc[h, r, :] = jnp.zeros((KT, 128), F32)
        kt[:, r] = kk.T
    each_tile(KT, t_lo, t_hi, kn_ref, vn_ref, k_ref, v_ref, prep)
    qsum_ref[...] = jnp.zeros((1, wide), F32)
    def pieces(x):
        a = x.astype(BF16).astype(F32)
        b = (x - a).astype(BF16).astype(F32)
        return a, b, x - a - b
    def qprep(t, _):
        r = pl.ds(pl.multiple_of(t * QB, QB), QB)
        fid = id_features(idq_ref[r, :], True).T
        row = lax.broadcasted_iota(jnp.int32, (HD, QB), 0)
        qt = (q_ref[r, :] * BF16(0.125)).T
        gg = g_ref[r, :]
        gt = gg.T
        prod = (gg.astype(F32) * o_ref[r, :].astype(F32)).T
        for h in range(HH):
            a, b, c = pieces(-lse_ref[0, h:h + 1, r])
            f = jnp.where(row == 32, a, jnp.where(row == 33, b, jnp.where(row == 34, c, fid)))
            qaug[h, :, r] = jnp.concatenate([qt[h * HD:(h + 1) * HD, :], f.astype(BF16)], axis=0)
            d = -jnp.sum(prod[h * HD:(h + 1) * HD, :], axis=0, keepdims=True)
            a, b, c = pieces(d)
            f = jnp.where(row == 32, a, jnp.where(row == 33, b, jnp.where(row == 34, c, 0.0)))
            gaug[h, :, r] = jnp.concatenate([gt[h * HD:(h + 1) * HD, :], f.astype(BF16)], axis=0)
        return 0
    lax.fori_loop(0, nq, qprep, 0)
    def qloop(qb, _):
        rq = pl.ds(pl.multiple_of(qb * QB, QB), QB)
        qq = q_ref[rq, :] * BF16(0.125)
        gg = g_ref[rq, :]
        zz = jnp.zeros((QB, HD), BF16)
        lo = lo_ref[qb]
        qts = [qaug[h, :, rq] for h in range(HH)]
        gts = [gaug[h, :, rq] for h in range(HH)]
        rhs = [jnp.concatenate([jnp.concatenate([qq[:, h * HD:(h + 1) * HD], zz], axis=1), jnp.concatenate([zz, gg[:, h * HD:(h + 1) * HD]], axis=1)], axis=0) for h in range(HH)]
        def kloop(t, c):
            r = pl.ds(pl.multiple_of(lo * KT + t * KB, KT), KB)
            new = []
            for h in range(HH):
                s = jnp.dot(kaug[h, r, :], qts[h], preferred_element_type=F32)
                dp = jnp.dot(vaug[h, r, :], gts[h], preferred_element_type=F32)
                p = jnp.exp(s)
                ds = (p * dp).astype(BF16)
                both = jnp.concatenate([ds, p.astype(BF16)], axis=1)
                acc[h, r, :] += jnp.dot(both, rhs[h], preferred_element_type=F32)
                new.append(c[h] + jnp.dot(kt[h * HD:(h + 1) * HD, r], ds, preferred_element_type=F32))
            return tuple(new)
        z = jnp.zeros((HD, QB), F32)
        c = lax.fori_loop(0, (hi_ref[qb] - lo) // (KB // KT), kloop, (z,) * HH)
        dq = (jnp.concatenate(c, axis=0) * 0.125).T
        qsum_ref[...] += jnp.sum(dq, axis=0, keepdims=True)
        dq_ref[rq, :] = dq.astype(BF16)
        return 0
    lax.fori_loop(0, nq, qloop, 0)
    def fin(t, _):
        r = pl.ds(pl.multiple_of(t * KT, KT), KT)
        sums = [acc[h, r, :] for h in range(HH)]
        for i in range(2):
            dkv_ref[i, r, :] = jnp.concatenate([x[:, i * HD:(i + 1) * HD] for x in sums], axis=1).astype(BF16)
        return 0
    lax.fori_loop(t_lo, t_hi, fin, 0)

def attend_bwd(q, kn, vn, k, v, idq, idk, lo, hi, out, grad, lse, HH, QB, KB, KT):
    n, cols = q.shape
    w = 3 * n
    HH = min(HH, cols // HD)
    wide = HH * HD
    near = pl.BlockSpec((2, n, wide), lambda g, *_: (0, 0, g))
    pairs = cols // wide
    nq = n // QB
    rows = lambda m: pl.BlockSpec((m, wide), lambda g, *_: (0, g))
    return pl.pallas_call(
        functools.partial(bwd_kernel, HH, QB, KB, KT, nq),
        grid_spec=pltpu.PrefetchScalarGridSpec(
            num_scalar_prefetch=2, grid=(pairs,),
            in_specs=[rows(n), near, near, rows(n), rows(n), pl.BlockSpec((n, 1), lambda g, *_: (0, 0)), pl.BlockSpec((w, 1), lambda g, *_: (0, 0)), rows(n), rows(n), pl.BlockSpec((1, HH, n), lambda g, *_: (g, 0, 0))],
            out_specs=[rows(n), pl.BlockSpec((2, w, wide), lambda g, *_: (0, 0, g)), pl.BlockSpec((1, wide), lambda g, *_: (0, g))],
            scratch_shapes=[pltpu.VMEM((HH, w, 128), BF16), pltpu.VMEM((HH, w, 128), BF16), pltpu.VMEM((wide, w), BF16), pltpu.VMEM((HH, 128, n), BF16), pltpu.VMEM((HH, 128, n), BF16), pltpu.VMEM((HH, w, 128), F32)]),
        out_shape=[jax.ShapeDtypeStruct((n, cols), BF16), jax.ShapeDtypeStruct((2, w, cols), BF16), jax.ShapeDtypeStruct((1, cols), F32)],
        compiler_params=pltpu.CompilerParams(vmem_limit_bytes=VMEM_LIMIT),
        cost_estimate=pl.CostEstimate(flops=5 * 10**10, bytes_accessed=10**8, transcendentals=0),
        name=N.attend_bwd,
    )(lo, hi, q, kn, vn, k, v, idq, idk, out, grad, lse)

def reach(ids_win, n, QB, KB, KT, least, most):
    w = ids_win.shape[0]
    own = ids_win[n:2 * n].reshape(n // QB, QB)
    lo = (jnp.argmax(ids_win[None, :] == own[:, :1], axis=1) // KT).astype(jnp.int32)
    hi = ((w - jnp.argmax(ids_win[::-1][None, :] == own[:, -1:], axis=1) + KT - 1) // KT).astype(jnp.int32)
    need = -(lo - hi) % (KB // KT)
    need = jnp.where(need > 0, KB // KT - need, 0)
    up = jnp.minimum(most - hi, need)
    lo, hi = lo - (need - up), hi + up
    return jnp.append(lo, jnp.min(lo)), jnp.append(hi, jnp.max(hi))


def neighbours(axis):
    peers = lax.axis_size(axis)
    up = [(i, i + 1) for i in range(peers - 1)]
    return up, [(j, i) for i, j in up]


def with_halo(array):
    up, down = neighbours(N.dp)
    return jnp.concatenate(
        [lax.ppermute(array, N.dp, up), array, lax.ppermute(array, N.dp, down)], axis=0
    )


def own_part(array, n):
    block, chunks, sub = sizes(array.shape[0], n)
    first = lax.axis_index(N.tensor) * block
    return lax.dynamic_slice_in_dim(array, first, block, 0).reshape(chunks, sub, array.shape[1])


def body(
    tokens, image_ids, cotangent, ln1_gain, ln1_bias, qkv_weight, qv_bias, proj_weight, proj_bias, scale_attn,
    ln2_gain, ln2_bias, fc1_weight, fc1_bias, fc2_weight, fc2_bias, scale_mlp,
):
    n = lax.axis_size(N.tensor)
    rows = tokens.shape[0]
    width, hidden = qkv_weight.shape[3], fc1_weight.shape[2]
    _, chunks, sub = sizes(rows, n)
    split = (n, chunks, sub)
    planes = jnp.transpose(qkv_weight, (0, 2, 1, 3))
    ids_win = with_halo(image_ids + 1)
    per = rows // TILES[3]
    place, places = lax.axis_index(N.dp), lax.axis_size(N.dp)
    least, most = jnp.where(place == 0, per, 0), jnp.where(place == places - 1, 2 * per, 3 * per)
    lo, hi = reach(ids_win, rows, *TILES[1:], least, most)
    idq, idk = ids_win[rows : 2 * rows, None], ids_win[:, None]

    dp_size = lax.axis_size(N.dp)
    made = first_block(n, dp_size, 2 * LAYERS + 1, tokens, planes, qv_bias[0], jnp.stack([ln1_gain[0], ln1_bias[0]]))
    own, hat1, sp1, a1 = made[N.after], made[N.hat1], made[N.sp1], made[N.a1]
    q, k, v = (made[name].reshape(rows, width) for name in (N.q, N.k, N.v))
    kn, vn = (made[name].reshape(2, rows, width) for name in (N.k_near, N.v_near))

    saved = []
    for level in range(LAYERS):
        kv = (kn, vn, k, v)
        attended, lse = attend_fwd(q, *kv, idq, idk, lo, hi, *TILES)
        last = level == LAYERS - 1
        after = 0 if last else level + 1
        vec = jnp.stack(
            [
                proj_bias[level], scale_attn[level], ln2_gain[level], ln2_bias[level], fc2_bias[level],
                scale_mlp[level], ln1_gain[after], ln1_bias[after],
            ]
        )
        extra = () if last else (planes, qv_bias[level + 1])
        made = forward_block(
            n, dp_size, last, level, attended, proj_weight, fc1_weight, fc2_weight, fc1_bias[level][None],
            vec, own, *extra,
        )
        keep = {name: made[name] for name in (N.u1, N.hat2, N.sp2, N.u2, N.a2, N.act, N.slope)}
        keep[N.attended] = attended.reshape(split + (width,))
        saved.append((q, kv, attended, lse, a1, hat1, sp1, keep))
        if last:
            result = made[N.after]
        else:
            own, hat1, sp1, a1 = (made[name] for name in (N.after, N.hat1, N.sp1, N.a1))
            q, k, v = (made[name].reshape(rows, width) for name in N.qkv)
            kn, vn = (made[name].reshape(2, rows, width) for name in (N.k_near, N.v_near))

    cot = cotangent.astype(F32)
    source = {
        N.full: (cot * scale_mlp[LAYERS - 1]).astype(BF16).reshape(split + (D,)),
        N.gm: own_part(cotangent, n).astype(F32),
    }
    above, grads = {}, [None] * LAYERS
    sums, narrow, dv_sums = [None] * (LAYERS + 1), [None] * LAYERS, [None] * LAYERS
    up, down = neighbours(N.dp)
    for level in reversed(range(LAYERS)):
        q, kv, attended, lse, a1, hat1, sp1, keep = saved[level]
        upper = min(level + 1, LAYERS - 1)
        vec = jnp.stack([scale_mlp[level], ln2_gain[level], scale_attn[level], ln1_gain[upper]])
        outs = backward_block(
            n, dp_size, LAYERS + level, source, above, (fc1_weight, level), (fc2_weight, level), (proj_weight, level), vec, keep,
        )
        datt, fc1b, sums[level + 1] = outs[N.datt], outs[N.fc1b], outs[N.sums]
        if above:
            grads[level + 1] = [outs["up%d_out" % (i + 1)] for i in range(4)]
            dv_sums[level + 1] = outs[N.dv_sum][0]
        flip = [(i, i ^ 2) for i in range(dp_size)]
        above = {N.up4: outs[N.g4]}
        for name in "12":
            above[N.keep + name] = outs[N.keep + name + N._out]
            got = N.got + name + N._out
            send = N.send + name + N._out
            above[N.got + name] = outs[got] if got in outs else lax.ppermute(outs[send], N.dp, flip)
        dq, dkv, q_sum = attend_bwd(
            q, *kv, idq, idk, lo, hi, attended, datt.reshape(rows, width), lse, *TILES
        )
        narrow[level] = (fc1b[0], q_sum[0])
        dkv = dkv.reshape((2, 3) + split + (width,))
        source = {
            N.dkv_in: dkv, N.dq: dq.reshape(split + (width,)), N.qkv: (planes, level), N.hat1: hat1,
            N.gm: outs[N.gm_out], N.a1: a1, N.sp1: sp1,
        }
    pad = jnp.zeros((D - width,), F32)
    flat = jnp.concatenate(
        [jnp.zeros((D,), F32)]
        + [x for i in range(1, LAYERS) for x in (dv_sums[i], pad)]
        + [x for i in range(LAYERS) for x in narrow[i]]
    )
    own_rows = -(-flat.shape[0] // (8 * D)) * 8
    flat = jnp.pad(flat, (0, own_rows * D - flat.shape[0])).reshape(own_rows, D)
    wide = 8 * (LAYERS + 1)
    base = jnp.concatenate([jnp.zeros((8, D), F32)] + sums[1:] + [flat])
    tail = backward_tail(n, dp_size, 2 * LAYERS, wide, source, above, ln1_gain[:1], base, result)
    grads[0] = [tail["up%d_out" % (i + 1)] for i in range(4)]
    grad_tokens, total = tail[N.out], tail[N.total]
    dv_total = total[wide : wide + LAYERS, :width]
    flat = total[wide + LAYERS :].reshape(-1)[: LAYERS * (hidden + width)].reshape(LAYERS, hidden + width)
    fc1b_total, qv_total = flat[:, :hidden], jnp.stack([flat[:, hidden:], dv_total], axis=1)
    stacked = lambda parts: jnp.stack([x.astype(F32) for x in parts])
    big = [
        jnp.transpose(
            stacked([x[2][:, i * width : (i + 1) * width] for x in grads for i in range(3)]).reshape(LAYERS, 3, D, width),
            (0, 2, 1, 3),
        ),
        stacked([x[3][:width] for x in grads]),
        stacked([x[1] for x in grads]),
        stacked([x[0] for x in grads]),
    ]
    total = total[:wide].reshape(LAYERS + 1, 8, D)
    upper, lower = total[1:], total[:-1]
    return (
        tail[N.out2].reshape(rows, D).astype(F32),
        grad_tokens.reshape(rows, D).astype(F32),
        lower[:, 6],
        lower[:, 7],
        big[0],
        qv_total,
        big[1],
        upper[:, 5],
        upper[:, 4],
        upper[:, 2],
        upper[:, 3],
        big[2],
        fc1b_total,
        big[3],
        upper[:, 1],
        upper[:, 0],
    )


def solution(mesh):
    cols, stack_rows = P(None, None, N.tensor), P(None, N.tensor, None)
    qkv = P(None, None, None, N.tensor)
    return jax.shard_map(
        body,
        mesh=mesh,
        in_specs=(
            P(N.dp, None), P(N.dp), P(N.dp, None), P(), P(), qkv, cols, stack_rows, P(), P(), P(), P(), cols,
            P(None, N.tensor), stack_rows, P(), P(),
        ),
        out_specs=(
            P(N.dp, None), P(N.dp, None), P(), P(), qkv, cols, stack_rows, P(), P(), P(), P(), cols,
            P(None, N.tensor), stack_rows, P(), P(),
        ),
        check_vma=False,
    )
```

```python
import functools
import jax
import jax.numpy as jnp
from jax import lax
from jax.experimental import pallas as pl
from jax.experimental.pallas import tpu as pltpu
from jax.sharding import PartitionSpec as P

HD = 64
LAYERS = 2
D = 1024
MESH = pl.DeviceIdType.MESH
F32 = jnp.float32
BF16 = jnp.bfloat16
eps = 1e-06
half_root = 0.7071067811865476
density_scale = 0.3989422804014327
BIG = 1e30
TILES = (4, 512, 512, 256)
VMEM_LIMIT = 62 * 2**20


def bit_of(index, k):
    return (index // (1 << k)) % 2


def order_bits(nbits, half):
    return tuple(range(nbits)) if half == 0 else tuple(reversed(range(nbits)))


def compose(free_bits, free_value, fixed):
    index = sum(value * (1 << k) for k, value in fixed.items())
    for place, k in enumerate(free_bits):
        index = index + ((free_value >> place) & 1) * (1 << k)
    return index


class Names:
    def __getattr__(self, key):
        return key


N = Names()


class Exchange:
    def __init__(self, n, chunks, sub):
        self.n, self.chunks, self.sub = n, chunks, sub
        self.nbits = n.bit_length() - 1
        self.half = sub // 2
        self.me = lax.axis_index(N.tensor)
        self.bits = [bit_of(self.me, k) for k in range(self.nbits)]
        self.pending = []

    def partner(self, k):
        return self.me + (1 - 2 * self.bits[k]) * (1 << k)

    def partners(self):
        return [{N.tensor: self.partner(k)} for k in range(self.nbits)]

    def rows(self, h):
        return pl.ds(h * self.half, self.half)

    def copy(self, src, dst, sems, c, h, message, k):
        return pltpu.make_async_remote_copy(
            src_ref=src,
            dst_ref=dst,
            send_sem=sems.at[0, c, h, message],
            recv_sem=sems.at[1, c, h, message],
            device_id={N.tensor: self.partner(k)},
            device_id_type=MESH,
        )

    def rs_base(self, p):
        return sum(self.n >> (q + 1) for q in range(p))

    def rs_fixed(self, order, p, flip):
        fixed = {k: self.bits[k] for k in order[:p]}
        fixed[order[p]] = 1 - self.bits[order[p]] if flip else self.bits[order[p]]
        return fixed

    def rs_places(self, order, p, f):
        places = []
        for q in range(p):
            free = order[q + 1 :]
            index = 0
            for place, k in enumerate(free):
                at = order.index(k)
                if at < p:
                    value = self.bits[k]
                elif at == p:
                    value = 1 - self.bits[k]
                else:
                    value = (f >> (at - p - 1)) & 1
                index = index + value * (1 << place)
            places.append(self.rs_base(q) + index)
        return places

    def rs_send(self, part, recv, sems, c, p):
        for h in range(2):
            order = order_bits(self.nbits, h)
            free = order[p + 1 :]
            for f in range(1 << len(free)):
                b = compose(free, f, self.rs_fixed(order, p, True))
                message = self.rs_base(p) + f
                if p > 0:
                    total = part[b, c, self.rows(h), :].astype(F32)
                    for place in self.rs_places(order, p, f):
                        total = total + recv[c, place, self.rows(h), :].astype(F32)
                    part[b, c, self.rows(h), :] = total.astype(BF16)
                cp = self.copy(
                    part.at[b, c, self.rows(h), :],
                    recv.at[c, message, self.rows(h), :],
                    sems,
                    c,
                    h,
                    message,
                    order[p],
                )
                cp.start()
                self.pending.append(cp)

    def rs_wait(self, part, recv, sems, c, p):
        for h in range(2):
            order = order_bits(self.nbits, h)
            for f in range(self.n >> (p + 1)):
                message = self.rs_base(p) + f
                self.copy(
                    part.at[0, c, self.rows(h), :],
                    recv.at[c, message, self.rows(h), :],
                    sems,
                    c,
                    h,
                    message,
                    order[p],
                ).wait_recv()

    def rs_total(self, part, recv, c):
        halves = []
        for h in range(2):
            order = order_bits(self.nbits, h)
            total = part[self.me, c, self.rows(h), :].astype(F32)
            for p in range(self.nbits):
                free = order[p + 1 :]
                place = self.rs_base(p) + sum(
                    self.bits[k] * (1 << at) for at, k in enumerate(free)
                )
                total = total + recv[c, place, self.rows(h), :].astype(F32)
            halves.append(total)
        return jnp.concatenate(halves, axis=0)

    def ag_send(self, full, sems, c, p):
        for h in range(2):
            order = order_bits(self.nbits, h)
            fixed = {k: self.bits[k] for k in order[p:]}
            for f in range(1 << p):
                b = compose(order[:p], f, fixed)
                message = (1 << p) - 1 + f
                ref = full.at[b, c, self.rows(h), :]
                cp = self.copy(ref, ref, sems, c, h, message, order[p])
                cp.start()
                self.pending.append(cp)

    def ag_wait(self, full, sems, c, p):
        for h in range(2):
            order = order_bits(self.nbits, h)
            fixed = {k: self.bits[k] for k in order[p + 1 :]}
            fixed[order[p]] = 1 - self.bits[order[p]]
            for f in range(1 << p):
                b = compose(order[:p], f, fixed)
                message = (1 << p) - 1 + f
                ref = full.at[b, c, self.rows(h), :]
                self.copy(ref, ref, sems, c, h, message, order[p]).wait_recv()

    def drain(self):
        for cp in self.pending:
            cp.wait_send()
        self.pending = []


def erf(x):
    c = jnp.clip(x, -3.832506856900711, 3.832506856900711)
    s = c * c
    top = jnp.full_like(s, 0.00022905065861350646)
    for k in (0.0034082910107109506, 0.050955695062380861, 0.18520832239976145, 1.128379143519084):
        top = top * s + k
    low = jnp.full_like(s, -1.1791602954361697e-7)
    for k in (
        0.000023547966471313185,
        0.0010179625278914885,
        0.014070470171167667,
        0.11098505178285362,
        0.49746925110067538,
        1.0,
    ):
        low = low * s + k
    return c * top / low


def gelu_pair(before):
    cumulative = 0.5 * (1.0 + erf(before * half_root))
    density = jnp.exp(-0.5 * before * before) * density_scale
    return before * cumulative, cumulative + before * density


def normalised(stream):
    centre = jnp.mean(stream, axis=-1, keepdims=True)
    centred = stream - centre
    spread = lax.rsqrt(jnp.mean(centred * centred, axis=-1, keepdims=True) + eps)
    return centred * spread, spread


def norm_back(upstream, normed, spread, gain_row):
    scaled = upstream * gain_row
    return spread * (
        scaled
        - jnp.mean(scaled, axis=-1, keepdims=True)
        - normed * jnp.mean(scaled * normed, axis=-1, keepdims=True)
    )


def chunk_of(ref, c):
    x = ref[:, c]
    return x.reshape(x.shape[0] * x.shape[1], x.shape[2])


def column_loop(width, step, fn):
    if width <= step:
        fn(pl.ds(0, width))
    else:

        def one(j, carry):
            fn(pl.ds(pl.multiple_of(j * step, step), step))
            return carry

        lax.fori_loop(0, width // step, one, 0)


def matmul_nn(x, w_ref, cols):
    return jnp.dot(x, w_ref[:, cols], preferred_element_type=F32)


def matmul_nt(x, w_ref, cols):
    return lax.dot_general(
        x, w_ref[cols, :], (((1,), (1,)), ((), ())), preferred_element_type=F32
    )


def tall(ref, cols=slice(None)):
    x = ref[..., cols]
    return x.reshape(x.shape[0] * x.shape[1] * x.shape[2], x.shape[3])


def grad_items(left, right, out, first, step=256):
    width = left.shape[3]
    step = min(step, width)

    def item(at):
        y = lax.dot_general(
            tall(left, slice(at, at + step)), tall(right), (((0,), (0,)), ((), ())), preferred_element_type=F32
        )
        out[first + at : first + at + step, :] = y.astype(BF16)

    return [functools.partial(item, at) for at in range(0, width, step)]


def with_items(ex, stage, items):
    share = -(-len(items) // ex.chunks)

    def both(c):
        for item in items[c * share : (c + 1) * share]:
            item()
        stage(c)

    return both


def rs_stages(ex, part, recv, sems):
    stages = []
    for p in range(1, ex.nbits):

        def stage(c, p=p):
            ex.rs_wait(part, recv, sems, c, p - 1)
            ex.rs_send(part, recv, sems, c, p)

        stages.append(stage)
    return stages


def ag_stages(ex, full, sems):
    stages = []
    for p in range(1, ex.nbits):

        def stage(c, p=p):
            ex.ag_wait(full, sems, c, p - 1)
            ex.ag_send(full, sems, c, p)

        stages.append(stage)
    return stages


def sizes(rows, n):
    block = rows // n
    chunks = 3 if block % 96 == 0 else (2 if block % 64 == 0 else 1)
    return block, chunks, block // chunks


class Total:
    def __init__(self, bufs, recv, sems, dp_size, n, wide):
        self.bufs, self.recv, self.sems, self.wide = bufs, recv, sems, wide
        self.axes = [(N.dp, k) for k in range(dp_size.bit_length() - 1)]
        self.axes += [(N.tensor, k) for k in range(n.bit_length() - 1)]
        self.copies = []

    def target(self, i):
        axis, k = self.axes[i]
        me = lax.axis_index(axis)
        return {axis: me + (1 - 2 * bit_of(me, k)) * (1 << k)}

    def partners(self):
        return [self.target(i) for i, (axis, _) in enumerate(self.axes) if axis == N.dp]

    def start(self, i):
        cp = pltpu.make_async_remote_copy(
            src_ref=self.bufs.at[i],
            dst_ref=self.recv.at[i],
            send_sem=self.sems.at[0, i],
            recv_sem=self.sems.at[1, i],
            device_id=self.target(i),
            device_id_type=MESH,
        )
        cp.start()
        self.copies.append(cp)

    def step(self, i):
        self.copies[i].wait_recv()
        axis, _ = self.axes[i]
        total = self.bufs[i] + self.recv[i]
        if axis == N.tensor:
            row = lax.broadcasted_iota(jnp.int32, total.shape, 0)
            total = jnp.where(row < self.wide, total, self.bufs[i])
        self.bufs[i + 1] = total
        if i + 1 < len(self.axes):
            self.start(i + 1)

    def drain(self):
        for cp in self.copies:
            cp.wait_send()


def run_stages(ex, stages, extra=()):
    extra = sorted(extra, key=lambda pair: pair[0])
    slot = 0
    for stage in stages:
        for c in range(ex.chunks):
            while extra and extra[0][0] <= slot:
                extra.pop(0)[1]()
            stage(c)
            slot += 1
    for _, thunk in extra:
        thunk()


def meet(partners):
    sem = pltpu.get_barrier_semaphore()
    for partner in partners:
        pl.semaphore_signal(sem, inc=1, device_id=partner, device_id_type=MESH)
    pl.semaphore_wait(sem, len(partners))


class Refs:
    def __init__(self):
        self.loads, self.targets, self.stores = {}, {}, []

    def need(self, *names):
        for name in names:
            if name in self.loads:
                self.loads.pop(name).wait()

    def store(self, name, index=()):
        cp = pltpu.make_async_copy(
            getattr(self, name).at[index] if index else getattr(self, name),
            self.targets[name].at[index] if index else self.targets[name],
            self.store_sems.at[len(self.stores)],
        )
        cp.start()
        self.stores.append(cp)

    def finish(self):
        self.need(*list(self.loads))
        for cp in self.stores:
            cp.wait()


def call(kernel, name, collective_id, ins, outs, scratch, flops):
    late_in = [
        (k, jax.ShapeDtypeStruct(a.shape[1:] if type(late) is int else a.shape, a.dtype))
        for k, a, late in ins
        if late is True or type(late) is int
    ]
    late_out = [(k, shape, dtype) for k, shape, dtype, late in outs if late is True]

    def entry(*refs):
        refs = list(refs)
        take = lambda count: [refs.pop(0) for _ in range(count)]
        r = Refs()
        r.sources = {}
        in_refs, out_refs = take(len(ins)), take(len(outs))
        in_bufs, out_bufs = take(len(late_in)), take(len(late_out))
        load_sems, r.store_sems = take(2)
        bufs = {k: b for (k, _), b in zip(late_in, in_bufs)}
        for (k, _, late), ref in zip(ins, in_refs):
            if late == N.far:
                r.sources[k] = ref
                continue
            fetched = late is True or type(late) is int
            setattr(r, k, bufs[k] if fetched else ref)
            if fetched:
                cp = pltpu.make_async_copy(ref.at[late] if type(late) is int else ref, bufs[k], load_sems.at[len(r.loads)])
                cp.start()
                r.loads[k] = cp
        bufs = {k: b for (k, _, _), b in zip(late_out, out_bufs)}
        for (k, _), ref in zip(scratch, take(len(scratch))):
            setattr(r, k, ref)
        for (k, _, _, late), ref in zip(outs, out_refs):
            if late == N.far:
                r.targets[k] = ref
                continue
            setattr(r, k, getattr(r, late) if isinstance(late, str) else bufs[k] if late else ref)
            if late:
                r.targets[k] = ref
        kernel(r)
        r.finish()

    space = lambda late: pl.BlockSpec(memory_space=pltpu.VMEM if late is False else pl.ANY)
    result = pl.pallas_call(
        entry,
        out_shape=[jax.ShapeDtypeStruct(shape, dtype) for _, shape, dtype, _ in outs],
        in_specs=[space(late) for _, _, late in ins],
        out_specs=[space(late) for _, _, _, late in outs],
        scratch_shapes=[pltpu.VMEM(a.shape, a.dtype) for _, a in late_in]
        + [pltpu.VMEM(shape, dtype) for _, shape, dtype in late_out]
        + [pltpu.SemaphoreType.DMA((max(len(late_in), 1),)), pltpu.SemaphoreType.DMA((64,))]
        + [spec for _, spec in scratch],
        compiler_params=pltpu.CompilerParams(
            collective_id=collective_id, has_side_effects=True, vmem_limit_bytes=VMEM_LIMIT
        ),
        cost_estimate=pl.CostEstimate(flops=flops, bytes_accessed=10**8, transcendentals=0),
        name=name,
    )(*[a for _, a, _ in ins])
    return dict(zip([k for k, _, _, _ in outs], result))


def comm_scratch(n, chunks, sub, tag):
    return [
        (N.part + tag, pltpu.VMEM((n, chunks, sub, D), BF16)),
        (N.recv + tag, pltpu.VMEM((chunks, n - 1, sub, D), BF16)),
    ]


def sem_scratch(stages, n, chunks):
    return [(N.sems, pltpu.SemaphoreType.DMA((stages, 2, chunks, 2, n - 1)))]


class Halo:
    def __init__(self, sems, dp_size):
        self.sems, self.size = sems, dp_size
        self.me = lax.axis_index(N.dp)
        self.has = (self.me < dp_size - 1, self.me > 0)
        self.pending = []

    def partners(self):
        return [{N.dp: (self.me + step) % self.size} for step in (1, self.size - 1)]

    def copy(self, src, dst, way, message):
        step = 1 if way == 0 else -1
        return pltpu.make_async_remote_copy(
            src_ref=src,
            dst_ref=dst,
            send_sem=self.sems.at[0, way, message],
            recv_sem=self.sems.at[1, way, message],
            device_id={N.dp: self.me + step},
            device_id_type=MESH,
        )

    def send(self, src, dst, way, message):
        cp = self.copy(src, dst, way, message)

        @pl.when(self.has[way])
        def _():
            cp.start()

        self.pending.append((cp, way))

    def wait(self, dst, way, message):
        @pl.when(self.has[1 - way])
        def _():
            self.copy(dst, dst, way, message).wait_recv()

    def drain(self):
        for cp, way in self.pending:

            @pl.when(self.has[way])
            def _(cp=cp):
                cp.wait_send()


class GradSum:
    def __init__(self, arrays, sems, dp_size):
        self.arrays, self.sems = arrays, sems
        self.local = {}
        self.k = dp_size.bit_length() - 1
        self.me = lax.axis_index(N.dp)
        self.bits = [bit_of(self.me, k) for k in range(self.k)]
        self.pending = []

    def partner(self, k):
        return {N.dp: self.me + (1 - 2 * self.bits[k]) * (1 << k)}

    def partners(self):
        return [self.partner(k) for k in range(self.k)]

    def offset(self, rows, k):
        return sum(self.bits[i] * (rows >> (i + 1)) for i in range(k))

    def copy(self, src, dst, a, message, k):
        return pltpu.make_async_remote_copy(
            src_ref=src,
            dst_ref=dst,
            send_sem=self.sems.at[0, a, message],
            recv_sem=self.sems.at[1, a, message],
            device_id=self.partner(k),
            device_id_type=MESH,
        )

    def recv_rows(self, a, k):
        rows, _, _, _, start, _ = self.arrays[a]
        return (rows >> start) - (rows >> k)

    def here(self, a, at, size):
        rows, _, _, _, start, _ = self.arrays[a]
        return pl.ds(pl.multiple_of(at - self.offset(rows, start), 16), size)

    def add(self, a, base, size, k):
        rows, grad, recv, _, start, _ = self.arrays[a]
        step = 32 if size % 32 == 0 else 16

        def block(i, carry):
            at = base + i * step
            here = self.here(a, at, step)
            total = grad[here, :].astype(F32)
            for j in range(start, k):
                there = at - self.offset(rows, j + 1) + self.recv_rows(a, j)
                total = total + recv[pl.ds(pl.multiple_of(there, 16), step), :].astype(F32)
            grad[here, :] = total.astype(BF16)
            return carry

        lax.fori_loop(0, size // step, block, 0)

    def merge(self, a):
        rows, grad, _, _, start, pieces = self.arrays[a]
        size = rows >> start
        step = 32 if size % 32 == 0 else 16

        def block(i, carry):
            here = pl.ds(pl.multiple_of(i * step, 16), step)
            grad[here, :] = sum(x[here, :].astype(F32) for x in pieces).astype(BF16)
            return carry

        lax.fori_loop(0, size // step, block, 0)

    def send(self, a, k):
        rows, grad, recv, _, start, _ = self.arrays[a]
        size = rows >> (k + 1)
        base = self.offset(rows, k) + (1 - self.bits[k]) * size
        if k > start:
            self.add(a, base, size, k)
        cp = self.copy(
            grad.at[self.here(a, base, size), :], recv.at[pl.ds(self.recv_rows(a, k), size), :], a, k, k
        )
        cp.start()
        self.pending.append(cp)

    def wait(self, a, k):
        rows, _, recv, _, _, _ = self.arrays[a]
        ref = recv.at[pl.ds(self.recv_rows(a, k), rows >> (k + 1)), :]
        self.copy(ref, ref, a, k, k).wait_recv()

    def split(self, a, keep, send):
        rows, grad, recv, _, _, _ = self.arrays[a]
        size = rows >> 2
        step = 32 if size % 32 == 0 else 16
        for out, bit in ((keep, self.bits[1]), (send, 1 - self.bits[1])):

            def block(i, carry, out=out, bit=bit):
                at = bit * size + i * step
                mine = grad[pl.ds(pl.multiple_of(self.bits[0] * 2 * size + at, 16), step), :].astype(F32)
                total = mine + recv[pl.ds(pl.multiple_of(at, 16), step), :].astype(F32)
                out[pl.ds(pl.multiple_of(i * step, 16), step), :] = total.astype(BF16)
                return carry

            lax.fori_loop(0, size // step, block, 0)

    def own(self, a, k, mine):
        rows, _, _, out, _, _ = self.arrays[a]
        size = rows >> (k + 1)
        base = self.offset(rows, k + 1) if mine else self.offset(rows, k) + (1 - self.bits[k]) * size
        return out.at[pl.ds(pl.multiple_of(base, 16), size), :]

    def gather_send(self, a, k):
        ref = self.own(a, k, True)
        src = ref
        if k == self.k - 1:
            rows, grad = self.arrays[a][:2]
            src = grad.at[self.here(a, self.offset(rows, self.k), rows >> self.k), :]
            self.local[a] = pltpu.make_async_copy(src, ref, self.sems.at[0, a, 2 * self.k])
            self.local[a].start()
        elif k == self.k - 2:
            self.local[a].wait()
        cp = self.copy(src, ref, a, self.k + k, k)
        cp.start()
        self.pending.append(cp)

    def gather_wait(self, a, k):
        ref = self.own(a, k, False)
        self.copy(ref, ref, a, self.k + k, k).wait_recv()

    def steps(self, a):
        last, start = self.k - 1, self.arrays[a][4]

        def first():
            if start:
                self.merge(a)
            self.send(a, start)

        def halve(k):
            self.wait(a, k - 1)
            self.send(a, k)

        def turn():
            rows = self.arrays[a][0]
            self.wait(a, last)
            self.add(a, self.offset(rows, self.k), rows >> self.k, self.k)
            self.gather_send(a, last)

        def double(k):
            self.gather_wait(a, k + 1)
            self.gather_send(a, k)

        out = [first] + [functools.partial(halve, k) for k in range(start + 1, self.k)] + [turn]
        out += [functools.partial(double, k) for k in reversed(range(last))]
        return out + [functools.partial(self.gather_wait, a, 0)]

    def drain(self):
        for cp in self.pending:
            cp.wait_send()


def grad_scratch(shapes, dp_size):
    steps = 2 * (dp_size.bit_length() - 1) + 1
    out = [
        ("grad_recv%d" % i, pltpu.VMEM(((rows >> start) - rows // dp_size, cols), BF16))
        for i, (rows, cols, start) in enumerate(shapes)
    ]
    return out + [(N.grad_sems, pltpu.SemaphoreType.DMA((2, len(shapes), steps)))]


def grad_rows(rows, dp_size):
    unit = 16 * dp_size
    return -(-rows // unit) * unit


def placed(steps, slots):
    slots = list(slots)
    while len(slots) < len(steps):
        slots.append(slots[-1] + 2)
    return list(zip(slots, steps))


def forward_kernel(n, dp_size, chunks, sub, last, r):
    ex = Exchange(n, chunks, sub)
    if last:
        meet(ex.partners())
    else:
        halo = Halo(r.halo_sems, dp_size)
        meet(ex.partners() + halo.partners())
    sems = r.sems
    row = lambda i: r.vec[i : i + 1, :]
    full2 = None if last else r.a1

    def pre(c):
        r.need(N.proj)

        def cols(j):
            y = matmul_nn(chunk_of(r.attended, c), r.proj, j)
            r.part1[:, c, :, j] = y.astype(BF16).reshape(n, sub, -1)

        column_loop(D, 256, cols)
        ex.rs_send(r.part1, r.recv1, sems.at[0], c, 0)

    def own1(c):
        r.need(N.stream)
        ex.rs_wait(r.part1, r.recv1, sems.at[0], c, ex.nbits - 1)
        u1 = ex.rs_total(r.part1, r.recv1, c) + row(0)
        r.u1[c] = u1
        middle = r.stream[c] + row(1) * u1
        r.stream[c] = middle
        hat, spread = normalised(middle)
        r.hat2[c] = hat
        r.sp2[c] = spread
        r.a2[ex.me, c] = (hat * row(2) + row(3)).astype(BF16)
        ex.ag_send(r.a2, sems.at[1], c, 0)
        r.store(N.u1, (c,))
        r.store(N.hat2, (c,))

    def mid(c):
        r.need(N.fc1, N.fc2)
        ex.ag_wait(r.a2, sems.at[1], c, ex.nbits - 1)

        def hidden(j):
            before = matmul_nn(chunk_of(r.a2, c), r.fc1, j) + r.fc1_bias[:, j]
            a, s = gelu_pair(before)
            r.act[:, c, :, j] = a.astype(BF16).reshape(n, sub, -1)
            r.slope[:, c, :, j] = s.astype(BF16).reshape(n, sub, -1)

        column_loop(r.fc1.shape[1], 256, hidden)

        def cols(j):
            y = matmul_nn(chunk_of(r.act, c), r.fc2, j)
            r.part2[:, c, :, j] = y.astype(BF16).reshape(n, sub, -1)

        column_loop(D, 256, cols)
        ex.rs_send(r.part2, r.recv2, sems.at[2], c, 0)
        for name in (N.a2, N.act, N.slope):
            r.store(name, (slice(None), c))

    def own2(c):
        ex.rs_wait(r.part2, r.recv2, sems.at[2], c, ex.nbits - 1)
        u2 = ex.rs_total(r.part2, r.recv2, c) + row(4)
        r.u2[c] = u2
        after = r.stream[c] + row(5) * u2
        r.after[c] = after.astype(r.after.dtype)
        r.store(N.after, (c,))
        r.store(N.u2, (c,))
        if not last:
            hat, spread = normalised(after)
            r.hat1[c] = hat
            r.sp1[c] = spread
            full2[ex.me, c] = (hat * row(6) + row(7)).astype(BF16)
            r.store(N.hat1, (c,))
            ex.ag_send(full2, sems.at[3], c, 0)

    def post(c):
        ex.ag_wait(full2, sems.at[3], c, ex.nbits - 1)
        r.need(N.qkv)
        x = chunk_of(full2, c)
        width = r.q.shape[3]
        for i, name in ((1, N.k), (2, N.v), (0, N.q)):
            y = jnp.dot(x, r.qkv[i], preferred_element_type=F32)
            if i != 1:
                y = y + r.qv_bias[i // 2 : i // 2 + 1, :]
            getattr(r, name)[:, c] = y.astype(BF16).reshape(n, sub, width)
            r.store(name, (slice(None), c))
            if i:
                for way in range(2):
                    halo.send(
                        getattr(r, name).at[:, c], r.targets[name + N._near].at[way, :, c], way, (i - 1) * chunks + c
                    )
        r.store(N.a1, (slice(None), c))

    run_stages(
        ex,
        [pre]
        + rs_stages(ex, r.part1, r.recv1, sems.at[0])
        + [own1]
        + ag_stages(ex, r.a2, sems.at[1])
        + [mid]
        + rs_stages(ex, r.part2, r.recv2, sems.at[2])
        + [own2]
        + ([] if last else ag_stages(ex, full2, sems.at[3]) + [post]),
    )
    if not last:
        for i, name in enumerate((N.k_near, N.v_near)):
            for c in range(chunks):
                for way in range(2):
                    halo.wait(r.targets[name].at[way, :, c], way, i * chunks + c)
        halo.drain()
    ex.drain()


def first_kernel(n, dp_size, chunks, sub, r):
    halo = Halo(r.halo_sems, dp_size)
    meet(halo.partners())
    me = lax.axis_index(N.tensor)
    r.need(N.tokens, N.qkv)
    width = r.q.shape[3]
    for c in range(chunks):

        def norm(b, carry, c=c):
            hat, _ = normalised(r.tokens[b, c].astype(F32))
            r.a1[b, c] = (hat * r.vec[0:1, :] + r.vec[1:2, :]).astype(BF16)
            return carry

        lax.fori_loop(0, n, norm, 0)
        x = chunk_of(r.a1, c)
        for i, name in ((1, N.k), (2, N.v), (0, N.q)):
            y = jnp.dot(x, r.qkv[i], preferred_element_type=F32)
            if i != 1:
                y = y + r.qv_bias[i // 2 : i // 2 + 1, :]
            getattr(r, name)[:, c] = y.astype(BF16).reshape(n, sub, width)
            r.store(name, (slice(None), c))
            if i:
                for way in range(2):
                    halo.send(
                        getattr(r, name).at[:, c], r.targets[name + N._near].at[way, :, c], way, (i - 1) * chunks + c
                    )
        r.store(N.a1, (slice(None), c))
        own = r.tokens[me, c].astype(F32)
        r.after[c] = own
        hat, spread = normalised(own)
        r.hat1[c] = hat
        r.sp1[c] = spread
    for i, name in enumerate((N.k_near, N.v_near)):
        for c in range(chunks):
            for way in range(2):
                halo.wait(r.targets[name].at[way, :, c], way, i * chunks + c)
    halo.drain()


def first_block(n, dp_size, collective_id, tokens, qkv, qv_bias, vec):
    rows = tokens.shape[0]
    _, chunks, sub = sizes(rows, n)
    width = qv_bias.shape[1]
    split = lambda cols: (n, chunks, sub, cols)
    mine = (chunks, sub, D)
    outs = [(N.after, mine, F32, False), (N.hat1, mine, F32, False), (N.sp1, (chunks, sub, 1), F32, False)]
    outs += [(N.a1, split(D), BF16, True)] + [(k, split(width), BF16, True) for k in (N.q, N.k, N.v)]
    outs += [(k, (2,) + split(width), BF16, N.far) for k in (N.k_near, N.v_near)]
    return call(
        functools.partial(first_kernel, n, dp_size, chunks, sub),
        N.first_block,
        collective_id,
        [(N.tokens, tokens.reshape(split(D)), True), (N.qkv, qkv, 0), (N.qv_bias, qv_bias, False), (N.vec, vec, False)],
        outs,
        [(N.halo_sems, pltpu.SemaphoreType.DMA((2, 2, 2 * chunks)))],
        2 * rows * D * 3 * width,
    )


def forward_block(n, dp_size, last, level, attended, proj, fc1, fc2, fc1_bias, vec, stream, qkv=None, qv_bias=None):
    rows, width = attended.shape
    block, chunks, sub = sizes(rows, n)
    hidden = fc1.shape[2]
    split = lambda cols: (n, chunks, sub, cols)
    mine = (chunks, sub, D)
    ins = [
        (N.attended, attended.reshape(split(width)), False), (N.proj, proj, level), (N.stream, stream.reshape(mine), True),
        (N.fc1, fc1, level), (N.fc2, fc2, level), (N.fc1_bias, fc1_bias, False), (N.vec, vec, False),
    ]
    outs = [
        (N.u1, mine, F32, True), (N.hat2, mine, F32, True), (N.sp2, (chunks, sub, 1), F32, False),
        (N.u2, mine, F32, True), (N.a2, split(D), BF16, True), (N.act, split(hidden), BF16, True),
        (N.slope, split(hidden), BF16, True),
    ]
    scratch = comm_scratch(n, chunks, sub, "1") + comm_scratch(n, chunks, sub, "2")
    if last:
        outs += [(N.after, mine, BF16, True)]
    else:
        ins += [(N.qkv, qkv, level + 1), (N.qv_bias, qv_bias, False)]
        outs += [(N.after, mine, F32, True), (N.hat1, mine, F32, True), (N.sp1, (chunks, sub, 1), F32, False)]
        outs += [(N.a1, split(D), BF16, True)] + [(k, split(width), BF16, True) for k in N.qkv]
        outs += [(k, (2,) + split(width), BF16, N.far) for k in (N.k_near, N.v_near)]
        scratch += [(N.halo_sems, pltpu.SemaphoreType.DMA((2, 2, 2 * chunks)))]
    return call(
        functools.partial(forward_kernel, n, dp_size, chunks, sub, last),
        N.forward_last if last else N.forward_block,
        level,
        ins,
        outs,
        scratch + sem_scratch(4, n, chunks),
        2 * rows * D * (2 * hidden + 4 * width),
    )


def add_rows(ref, i, value):
    ref[i : i + 1, :] += jnp.sum(value, axis=0, keepdims=True)


def input_norm_own(ex, r, c, gain, sums):
    r.need(N.hat1, N.gm)
    ex.rs_wait(r.part, r.recv, r.sems.at[0], c, ex.nbits - 1)
    da1 = ex.rs_total(r.part, r.recv, c)
    add_rows(sums, 6, da1 * r.hat1[c])
    add_rows(sums, 7, da1)
    return r.gm[c] + norm_back(da1, r.hat1[c], r.sp1[c], gain)


def send_home(halo, r, chunks):
    cp = pltpu.make_async_copy(r.sources[N.dkv_in].at[:, 1], r.dkv, r.dkv_sem)
    cp.start()
    r.loads[N.dkv] = cp
    for c in range(chunks):
        for way in range(2):
            for i in range(2):
                src = r.sources[N.dkv_in].at[i, 2 - 2 * way, :, c]
                halo.send(src, near_part(r, way, i, c), way, 2 * c + i)


def near_part(r, way, i, c):
    width = r.dq.shape[3]
    return r.near.at[:, c, :, pl.ds((2 * way + i) * width, width)]


def input_grad_chunk(ex, halo, r, c):
    r.need(N.dq, N.dkv, N.qkv)
    width = r.dq.shape[3]
    for way in range(2):
        for i in range(2):
            halo.wait(near_part(r, way, i, c), way, 2 * c + i)
    r.dqkv[:, c, :, :width] = r.dq[:, c]
    for i in range(2):
        cols = slice((i + 1) * width, (i + 2) * width)

        for b in range(ex.n):
            r.total_kv[...] = r.dkv[i, b, c].astype(F32)
            for way in range(2):

                @pl.when(halo.has[1 - way])
                def _():
                    first = (2 * way + i) * width
                    r.total_kv[...] += r.near[b, c, :, first : first + width].astype(F32)

            total = r.total_kv[...]
            if i:
                r.dv_sum[...] += jnp.sum(total, axis=0, keepdims=True)
            r.dqkv[b, c, :, cols] = total.astype(BF16)

    def cols(j):
        x = chunk_of(r.dqkv, c)
        y = sum(
            lax.dot_general(
                x[:, i * width : (i + 1) * width], r.qkv[i, j, :], (((1,), (1,)), ((), ())), preferred_element_type=F32
            )
            for i in range(3)
        )
        r.part[:, c, :, j] = y.astype(BF16).reshape(ex.n, ex.sub, -1)

    column_loop(D, 256, cols)
    ex.rs_send(r.part, r.recv, r.sems.at[0], c, 0)


def backward_kernel(n, dp_size, chunks, sub, first, r):
    ex = Exchange(n, chunks, sub)
    sems, part, recv = r.sems, r.part, r.recv
    row = lambda i: r.vec[i : i + 1, :]
    if first:
        meet(ex.partners() + [{N.dp: dp_partner(0)}, {N.dp: dp_partner(1)}])
    else:
        halo = Halo(r.halo_sems, dp_size)
        gs = GradSum(upper_arrays(r), r.grad_sems, dp_size)
        meet(ex.partners() + gs.partners() + halo.partners())
        r.near = r.e1
        send_home(halo, r, chunks)
        r.dv_sum[...] = jnp.zeros_like(r.dv_sum)
    first_arrays = [(x.shape[0], x, recv, None, 0, ()) for x, recv in ((r.g1, r.core_recv0), (r.g2, r.core_recv1))]
    first_sum = GradSum(first_arrays, r.core_sems, dp_size)
    r.sums[...] = jnp.zeros_like(r.sums)
    r.fc1b[...] = jnp.zeros_like(r.fc1b)
    width, hidden_size = r.proj.shape[0], r.fc1.shape[1]
    if r.g4.shape[0] > width:
        r.g4[width:, :] = jnp.zeros((r.g4.shape[0] - width, D), BF16)

    def pre(c):
        input_grad_chunk(ex, halo, r, c)

    def own0(c):
        r.need(N.u2)
        g = input_norm_own(ex, r, c, row(3), r.sums)
        add_rows(r.sums, 0, g * r.u2[c])
        add_rows(r.sums, 1, g * row(0))
        r.gm[c] = g
        r.full[ex.me, c] = (g * row(0)).astype(BF16)
        ex.ag_send(r.full, sems.at[1], c, 0)

    def mid(c):
        r.need(N.full, N.fc2, N.slope, N.fc1, N.u2, N.gm)
        if not first and c == 0:
            ex.drain()
        if first:
            g = r.full[ex.me, c].astype(F32)
            r.gm[c] = g

            def scaled(b, carry):
                r.full[b, c] = (r.full[b, c].astype(F32) * row(0)).astype(BF16)
                return carry

            lax.fori_loop(0, n, scaled, 0)
            add_rows(r.sums, 0, g * r.u2[c])
            add_rows(r.sums, 1, g * row(0))
        else:
            ex.ag_wait(r.full, sems.at[1], c, ex.nbits - 1)

        def hidden(j):
            y = matmul_nt(chunk_of(r.full, c), r.fc2, j)
            w = y.shape[1]
            db = y * r.slope[:, c, :, j].astype(F32).reshape(n * sub, w)
            r.fc1b[:, j] += jnp.sum(db, axis=0, keepdims=True)
            r.slope[:, c, :, j] = db.astype(BF16).reshape(n, sub, w)

        column_loop(hidden_size, 256, hidden)

        def cols(j):
            y = matmul_nt(chunk_of(r.slope, c), r.fc1, j)
            part[:, c, :, j] = y.astype(BF16).reshape(n, sub, -1)

        column_loop(D, 256, cols)
        ex.rs_send(part, recv, sems.at[2], c, 0)

    def own1(c):
        r.need(N.hat2, N.u1)
        ex.rs_wait(part, recv, sems.at[2], c, ex.nbits - 1)
        da2 = ex.rs_total(part, recv, c)
        hat = r.hat2[c]
        add_rows(r.sums, 2, da2 * hat)
        add_rows(r.sums, 3, da2)
        gm = r.gm[c] + norm_back(da2, hat, r.sp2[c], row(1))
        r.gm[c] = gm
        add_rows(r.sums, 4, gm * r.u1[c])
        add_rows(r.sums, 5, gm * row(2))
        r.e1[ex.me, c] = (gm * row(2)).astype(BF16)
        ex.ag_send(r.e1, sems.at[3], c, 0)
        r.store(N.gm_out, (c,))

    def post(c):
        r.need(N.proj)
        ex.ag_wait(r.e1, sems.at[3], c, ex.nbits - 1)
        y = matmul_nt(chunk_of(r.e1, c), r.proj, slice(None))
        r.datt[:, c] = y.astype(BF16).reshape(n, sub, -1)
        r.store(N.datt, (slice(None), c))

    stages, extra = [], []
    if not first:
        made = [lambda: r.need(N.a1)] + grad_items(r.a1, r.dqkv, r.up3, 0)
        stages = [pre] + rs_stages(ex, part, recv, sems.at[0]) + [own0] + ag_stages(ex, r.full, sems.at[1])
        stages[1] = with_items(ex, stages[1], made)
        r.act = r.a1.at[:, :, :, pl.ds(0, hidden_size)]

        def fetch_act():
            cp = pltpu.make_async_copy(r.sources[N.act], r.act, r.act_sem)
            cp.start()
            r.loads[N.act] = cp

        extra += [(2 * chunks, fetch_act)]
        extra += [(3, lambda: r.need(N.keep1, N.got1, N.keep2, N.got2, N.up4))]
        extra += placed_sums(gs)
    gathers = ag_stages(ex, r.e1, sems.at[3])
    sums2 = rs_stages(ex, part, recv, sems.at[2])
    sums2[0] = with_items(ex, sums2[0], [lambda: r.need(N.act)] + grad_items(r.act, r.full, r.g1, 0))
    made = [lambda: r.need(N.a2)] + grad_items(r.a2, r.slope, r.g2, 0)
    stages += [mid] + sums2 + [with_items(ex, own1, made)] + gathers + [post]
    end = len(stages) * chunks
    behind = end - chunks * (1 + len(gathers))

    def part_of(a):
        first_sum.wait(a, 0)
        names = ((N.keep1, N.send1), (N.keep2, N.send2))[a]
        first_sum.split(a, getattr(r, names[0] + N._out), getattr(r, names[1] + N._out))
        r.store(names[0] + N._out)
        if first:
            got = r.targets[(N.got1_out, N.got2_out)[a]]
            cp = first_sum.copy(getattr(r, names[1] + N._out), got, a, 1, 1)
            cp.start()
            first_sum.pending.append(cp)
            arrivals.append(cp)
        else:
            r.store(names[1] + N._out)

    arrivals = []
    extra += [(behind - chunks, lambda: first_sum.send(0, 0)), (behind - chunks + 1, lambda: part_of(0))]
    extra += [(behind, lambda: first_sum.send(1, 0)), (behind + 1, lambda: part_of(1))]
    run_stages(ex, stages, extra)
    r.need(N.attended)
    for item in grad_items(r.attended, r.e1, r.g4, 0):
        item()
    if not first:
        gs.drain()
        halo.drain()
    for cp in arrivals:
        cp.wait_recv()
    first_sum.drain()
    ex.drain()


def dp_partner(k):
    me = lax.axis_index(N.dp)
    return me + (1 - 2 * bit_of(me, k)) * (1 << k)


def tail_sums(gs):
    return (
        placed(gs.steps(0), (3, 6, 10, 13, 16))
        + placed(gs.steps(1), (4, 9, 13, 15.5, 17))
        + placed(gs.steps(2), (6, 7, 9, 12, 15, 16, 18))
        + placed(gs.steps(3), (3, 5, 7, 10, 12, 14, 17))
    )


def placed_sums(gs):
    return (
        placed(gs.steps(0), (3, 9, 15, 21, 25))
        + placed(gs.steps(1), (4, 10, 16, 22, 26))
        + placed(gs.steps(2), (6, 7, 11, 17, 20, 24, 27))
        + placed(gs.steps(3), (3, 5, 8, 12, 14, 18, 23))
    )


def upper_arrays(r):
    pieces = ((r.keep1, r.got1), (r.keep2, r.got2), (), ())
    return [
        (
            r.targets["up%d_out" % (i + 1)].shape[0],
            getattr(r, "up%d" % (i + 1)),
            getattr(r, "grad_recv%d" % i),
            r.targets["up%d_out" % (i + 1)],
            2 if x else 0,
            x,
        )
        for i, x in enumerate(pieces)
    ]


def upper_buffers(above, width, dp_size):
    shapes = [(4 * x.shape[0], x.shape[1]) for x in (above[N.keep1], above[N.keep2])]
    shapes += [(D, 3 * width), above[N.up4].shape]
    scratch = [(N.up1, pltpu.VMEM(above[N.keep1].shape, BF16)), (N.up2, pltpu.VMEM(above[N.keep2].shape, BF16))]
    scratch += [(N.up3, pltpu.VMEM(shapes[2], BF16))]
    scratch += grad_scratch([x + (start,) for x, start in zip(shapes, (2, 2, 0, 0))], dp_size)
    return scratch, [("up%d_out" % (i + 1), x, BF16, N.far) for i, x in enumerate(shapes)]


def home_buffers(n, chunks, sub, width):
    split = (n, chunks, sub)
    return [
        (N.dqkv, pltpu.VMEM(split + (3 * width,), BF16)),
        (N.total_kv, pltpu.VMEM((sub, width), F32)),
        (N.dkv, pltpu.VMEM((2,) + split + (width,), BF16)),
        (N.dkv_sem, pltpu.SemaphoreType.DMA),
        (N.halo_sems, pltpu.SemaphoreType.DMA((2, 2, 2 * chunks))),
    ]


def backward_block(n, dp_size, collective_id, source, above, fc1, fc2, proj, vec, saved):
    first = not above
    _, chunks, sub, hidden = saved[N.slope].shape
    width = proj[0].shape[1]
    split = lambda cols: (n, chunks, sub, cols)
    mine = (chunks, sub, D)
    ins = list(source.items()) + list(above.items()) + [(N.fc2, fc2), (N.slope, saved[N.slope]), (N.fc1, fc1)]
    ins += [(k, saved[k]) for k in (N.u2, N.act, N.a2, N.hat2, N.u1, N.sp2, N.attended)] + [(N.proj, proj), (N.vec, vec)]
    outs = [
        (N.datt, split(width), BF16, True), (N.gm_out, mine, F32, N.gm), (N.sums, (8, D), F32, False),
        (N.fc1b, (1, hidden), F32, False), (N.g4, (grad_rows(width, dp_size), D), BF16, False),
    ]
    quarters = []
    for i, (rows, cols) in enumerate(((hidden, D), (D, hidden))):
        keep, send, got = ((N.keep1_out, N.send1_out, N.got1_out), (N.keep2_out, N.send2_out, N.got2_out))[i]
        quarter = (rows // 4, cols)
        outs += [(keep, quarter, BF16, True)]
        if first:
            quarters += [(send, pltpu.VMEM(quarter, BF16))]
            outs += [(got, quarter, BF16, N.far)]
        else:
            outs += [(send, quarter, BF16, True)]
    scratch = quarters + comm_scratch(n, chunks, sub, "") + [(N.e1, pltpu.VMEM(split(D), BF16))] + sem_scratch(4, n, chunks)
    scratch += [(N.g1, pltpu.VMEM((hidden, D), BF16)), (N.g2, pltpu.VMEM((D, hidden), BF16))]
    scratch += [(N.core_recv0, pltpu.VMEM((hidden // 2, D), BF16)), (N.core_recv1, pltpu.VMEM((D // 2, hidden), BF16))]
    scratch += [(N.core_sems, pltpu.SemaphoreType.DMA((2, 2, 2 * (dp_size.bit_length() - 1))))]
    if first:
        scratch += [(N.gm, pltpu.VMEM(mine, F32))]
    else:
        scratch += [(N.act_sem, pltpu.SemaphoreType.DMA)]
        scratch += [(N.full, pltpu.VMEM(split(D), BF16))] + home_buffers(n, chunks, sub, width)
        more, results = upper_buffers(above, width, dp_size)
        scratch += more
        outs += results + [(N.dv_sum, (1, width), F32, False)]
    return call(
        functools.partial(backward_kernel, n, dp_size, chunks, sub, first),
        N.backward_first if first else N.backward_block,
        collective_id,
        [placed_input(k, a) if first or k != N.act else (k, a, N.far) for k, a in ins],
        outs,
        scratch,
        2 * n * chunks * sub * D * (2 * hidden + 4 * width),
    )


def placed_input(name, array):
    return (name,) + (array if isinstance(array, tuple) else (array, lateness(name)))


def lateness(name):
    if name == N.dkv_in:
        return N.far
    return name not in (N.sp1, N.sp2, N.vec, N.base)


def tail_kernel(n, dp_size, chunks, sub, wide, r):
    ex = Exchange(n, chunks, sub)
    small = Total(r.bufs, r.small_recv, r.small_sems, dp_size, n, wide)
    gs = GradSum(upper_arrays(r), r.grad_sems, dp_size)
    halo = Halo(r.halo_sems, dp_size)
    meet(ex.partners() + gs.partners() + halo.partners())
    r.near = r.full
    send_home(halo, r, chunks)
    sems = r.sems
    r.dv_sum[...] = jnp.zeros_like(r.dv_sum)
    r.sums[...] = jnp.zeros_like(r.sums)

    def pre(c):
        input_grad_chunk(ex, halo, r, c)

    def own(c):
        g = input_norm_own(ex, r, c, r.vec[0:1, :], r.sums)
        r.full[ex.me, c] = g.astype(BF16)
        ex.ag_send(r.full, sems.at[1], c, 0)
        if c == chunks - 1:
            r.bufs[0] = r.base[...]
            r.bufs[0, 0:8, :] = r.sums[...]
            r.bufs[0, wide : wide + 1, : r.dv_sum.shape[1]] = r.dv_sum[...]
            small.start(0)

    def post(c):
        ex.ag_wait(r.full, sems.at[1], c, ex.nbits - 1)
        r.store(N.out, (slice(None), c))

    made = [lambda: r.need(N.a1)] + grad_items(r.a1, r.dqkv, r.up3, 0)
    stages = [pre] + rs_stages(ex, r.part, r.recv, sems.at[0]) + [own] + ag_stages(ex, r.full, sems.at[1]) + [post]
    stages[1] = with_items(ex, stages[1], made)
    after_own = chunks * (2 + ex.nbits - 1)
    extra = [(3, lambda: r.need(N.keep1, N.got1, N.keep2, N.got2, N.up4))]
    extra += tail_sums(gs)

    def spread(c, p):
        if p == 0:
            r.need(N.result)
            r.full3[ex.me, c] = r.result[c]
        else:
            ex.ag_wait(r.full3, sems.at[2], c, p - 1)
        if p < ex.nbits:
            ex.ag_send(r.full3, sems.at[2], c, p)
        else:
            r.store(N.out2, (slice(None), c))

    for p in range(ex.nbits + 1):
        slot = after_own + chunks * ex.nbits if p == ex.nbits else chunks * (1 + 2 * p)
        extra += [(slot + c, functools.partial(spread, c, p)) for c in range(chunks)]
    extra += [(after_own + 1 + i, functools.partial(small.step, i)) for i in range(len(small.axes))]
    run_stages(ex, stages, extra)
    halo.drain()
    r.total[...] = r.bufs[len(small.axes)]
    ex.drain()
    small.drain()
    gs.drain()


def backward_tail(n, dp_size, collective_id, wide, source, above, vec, base, result):
    _, chunks, sub, width = source[N.dq].shape
    split = lambda cols: (n, chunks, sub, cols)
    steps = (n * dp_size).bit_length() - 1
    ins = list(source.items()) + list(above.items()) + [(N.vec, vec), (N.base, base), (N.result, result)]
    more, results = upper_buffers(above, width, dp_size)
    outs = [(N.out, split(D), BF16, N.full), (N.out2, split(D), BF16, N.full3), (N.total, base.shape, F32, False)] + results
    scratch = comm_scratch(n, chunks, sub, "") + sem_scratch(3, n, chunks) + home_buffers(n, chunks, sub, width)
    scratch += [(N.full3, pltpu.VMEM(split(D), BF16))]
    scratch += [(N.full, pltpu.VMEM(split(D), BF16)), (N.sums, pltpu.VMEM((8, D), F32)), (N.dv_sum, pltpu.VMEM((1, width), F32))]
    scratch += [(N.bufs, pltpu.VMEM((steps + 1,) + base.shape, F32)), (N.small_recv, pltpu.VMEM((steps,) + base.shape, F32))]
    scratch += [(N.small_sems, pltpu.SemaphoreType.DMA((2, steps)))] + more
    return call(
        functools.partial(tail_kernel, n, dp_size, chunks, sub, wide),
        N.backward_tail,
        collective_id,
        [placed_input(k, a) for k, a in ins],
        outs,
        scratch,
        2 * n * chunks * sub * D * 3 * width,
    )


def id_features(ids_col, query_side):
    lane = lax.broadcasted_iota(jnp.int32, (ids_col.shape[0], HD), 1)
    bit = (ids_col >> (lane & 15)) & 1
    first = lane < 16
    second = (lane >= 16) & (lane < 32)
    inv = 1 - bit
    if query_side:
        v = jnp.where(first, bit, jnp.where(second, inv, 0)).astype(F32) * (-BIG)
    else:
        v = jnp.where(first, inv, jnp.where(second, bit, 0)).astype(F32)
    return v

def each_tile(KB, t_lo, t_hi, kn_ref, vn_ref, k_ref, v_ref, fn):
    per = k_ref.shape[0] // KB
    for segment in range(3):
        def one(t, carry, segment=segment):
            here = pl.ds(pl.multiple_of((t - segment * per) * KB, KB), KB)
            if segment == 1:
                fn(t, here, k_ref[here, :], v_ref[here, :])
            else:
                fn(t, here, kn_ref[segment // 2, here, :], vn_ref[segment // 2, here, :])
            return carry
        lax.fori_loop(jnp.maximum(t_lo, segment * per), jnp.minimum(t_hi, (segment + 1) * per), one, 0)

def fwd_kernel(HH, QB, KB, KT, nq, lo_ref, hi_ref, q_ref, kn_ref, vn_ref, k_ref, v_ref, idq_ref, idk_ref, o_ref, lse_ref, kaug, vt, qaug):
    t_lo = lo_ref[nq]
    t_hi = hi_ref[nq]
    def prep(t, here, kk, vv):
        r = pl.ds(pl.multiple_of(t * KT, KT), KT)
        feat = id_features(idk_ref[r, :], False).astype(BF16)
        for h in range(HH):
            kaug[h, r, :] = jnp.concatenate([kk[:, h * HD:(h + 1) * HD], feat], axis=1)
        vt[:, r] = vv.T
    each_tile(KT, t_lo, t_hi, kn_ref, vn_ref, k_ref, v_ref, prep)
    def qprep(t, _):
        r = pl.ds(pl.multiple_of(t * QB, QB), QB)
        feat = id_features(idq_ref[r, :], True).astype(BF16)
        qq = (q_ref[r, :] * BF16(0.125))
        for h in range(HH):
            qaug[h, :, r] = jnp.concatenate([qq[:, h * HD:(h + 1) * HD], feat], axis=1).T
        return 0
    lax.fori_loop(0, nq, qprep, 0)
    def qloop(qb, _):
        rq = pl.ds(pl.multiple_of(qb * QB, QB), QB)
        lo = lo_ref[qb]
        qts = [qaug[h, :, rq] for h in range(HH)]
        def kloop(t, c):
            r = pl.ds(pl.multiple_of(lo * KT + t * KB, KT), KB)
            new = []
            for h in range(HH):
                m, l, acc = c[h]
                s = jnp.dot(kaug[h, r, :], qts[h], preferred_element_type=F32)
                mn = jnp.maximum(m, jnp.max(s, axis=0, keepdims=True))
                p = jnp.exp(s - mn)
                al = jnp.exp(m - mn)
                l = l * al + jnp.sum(p, axis=0, keepdims=True)
                acc = acc * al + jnp.dot(vt[h * HD:(h + 1) * HD, r], p.astype(BF16), preferred_element_type=F32)
                new.append((mn, l, acc))
            return tuple(new)
        z = (jnp.full((1, QB), -3e38, F32), jnp.zeros((1, QB), F32), jnp.zeros((HD, QB), F32))
        c = lax.fori_loop(0, (hi_ref[qb] - lo) // (KB // KT), kloop, (z,) * HH)
        both = jnp.concatenate([c[h][2] / c[h][1] for h in range(HH)], axis=0)
        o_ref[rq, :] = both.T.astype(BF16)
        for h in range(HH):
            lse_ref[0, h:h + 1, rq] = c[h][0] + jnp.log(c[h][1])
        return 0
    lax.fori_loop(0, nq, qloop, 0)

def attend_fwd(q, kn, vn, k, v, idq, idk, lo, hi, HH, QB, KB, KT):
    n, cols = q.shape
    w = 3 * n
    HH = min(HH, cols // HD)
    wide = HH * HD
    near = pl.BlockSpec((2, n, wide), lambda g, *_: (0, 0, g))
    pairs = cols // wide
    nq = n // QB
    return pl.pallas_call(
        functools.partial(fwd_kernel, HH, QB, KB, KT, nq),
        grid_spec=pltpu.PrefetchScalarGridSpec(
            num_scalar_prefetch=2, grid=(pairs,),
            in_specs=[pl.BlockSpec((n, wide), lambda g, *_: (0, g)), near, near, pl.BlockSpec((n, wide), lambda g, *_: (0, g)), pl.BlockSpec((n, wide), lambda g, *_: (0, g)),
                      pl.BlockSpec((n, 1), lambda g, *_: (0, 0)), pl.BlockSpec((w, 1), lambda g, *_: (0, 0))],
            out_specs=[pl.BlockSpec((n, wide), lambda g, *_: (0, g)), pl.BlockSpec((1, HH, n), lambda g, *_: (g, 0, 0))],
            scratch_shapes=[pltpu.VMEM((HH, w, 128), BF16), pltpu.VMEM((wide, w), BF16), pltpu.VMEM((HH, 128, n), BF16)]),
        out_shape=[jax.ShapeDtypeStruct((n, cols), BF16), jax.ShapeDtypeStruct((pairs, HH, n), F32)],
        compiler_params=pltpu.CompilerParams(vmem_limit_bytes=VMEM_LIMIT),
        cost_estimate=pl.CostEstimate(flops=5 * 10**10, bytes_accessed=10**8, transcendentals=0),
        name=N.attend_fwd,
    )(lo, hi, q, kn, vn, k, v, idq, idk)

def bwd_kernel(HH, QB, KB, KT, nq, lo_ref, hi_ref, q_ref, kn_ref, vn_ref, k_ref, v_ref, idq_ref, idk_ref, o_ref, g_ref, lse_ref, dq_ref, dkv_ref, qsum_ref, kaug, vaug, kt, qaug, gaug, acc):
    w = 3 * k_ref.shape[0]
    t_lo = lo_ref[nq]
    t_hi = hi_ref[nq]
    wide = HH * HD
    lane = lax.broadcasted_iota(jnp.int32, (KT, HD), 1)
    three = ((lane >= 32) & (lane < 35))
    def zero(t, _):
        r = pl.ds(pl.multiple_of(t * KT, KT), KT)
        for i in range(2):
            dkv_ref[i, r, :] = jnp.zeros((KT, wide), BF16)
        return 0
    lax.fori_loop(0, w // KT, zero, 0)
    def prep(t, here, kk, vv):
        r = pl.ds(pl.multiple_of(t * KT, KT), KT)
        feat = jnp.where(three, 1.0, id_features(idk_ref[r, :], False)).astype(BF16)
        ones = jnp.where(three, 1.0, 0.0).astype(BF16)
        for h in range(HH):
            kaug[h, r, :] = jnp.concatenate([kk[:, h * HD:(h + 1) * HD], feat], axis=1)
            vaug[h, r, :] = jnp.concatenate([vv[:, h * HD:(h + 1) * HD], ones], axis=1)
            acc[h, r, :] = jnp.zeros((KT, 128), F32)
        kt[:, r] = kk.T
    each_tile(KT, t_lo, t_hi, kn_ref, vn_ref, k_ref, v_ref, prep)
    qsum_ref[...] = jnp.zeros((1, wide), F32)
    def pieces(x):
        a = x.astype(BF16).astype(F32)
        b = (x - a).astype(BF16).astype(F32)
        return a, b, x - a - b
    def qprep(t, _):
        r = pl.ds(pl.multiple_of(t * QB, QB), QB)
        fid = id_features(idq_ref[r, :], True).T
        row = lax.broadcasted_iota(jnp.int32, (HD, QB), 0)
        qt = (q_ref[r, :] * BF16(0.125)).T
        gg = g_ref[r, :]
        gt = gg.T
        prod = (gg.astype(F32) * o_ref[r, :].astype(F32)).T
        for h in range(HH):
            a, b, c = pieces(-lse_ref[0, h:h + 1, r])
            f = jnp.where(row == 32, a, jnp.where(row == 33, b, jnp.where(row == 34, c, fid)))
            qaug[h, :, r] = jnp.concatenate([qt[h * HD:(h + 1) * HD, :], f.astype(BF16)], axis=0)
            d = -jnp.sum(prod[h * HD:(h + 1) * HD, :], axis=0, keepdims=True)
            a, b, c = pieces(d)
            f = jnp.where(row == 32, a, jnp.where(row == 33, b, jnp.where(row == 34, c, 0.0)))
            gaug[h, :, r] = jnp.concatenate([gt[h * HD:(h + 1) * HD, :], f.astype(BF16)], axis=0)
        return 0
    lax.fori_loop(0, nq, qprep, 0)
    def qloop(qb, _):
        rq = pl.ds(pl.multiple_of(qb * QB, QB), QB)
        qq = q_ref[rq, :] * BF16(0.125)
        gg = g_ref[rq, :]
        zz = jnp.zeros((QB, HD), BF16)
        lo = lo_ref[qb]
        qts = [qaug[h, :, rq] for h in range(HH)]
        gts = [gaug[h, :, rq] for h in range(HH)]
        rhs = [jnp.concatenate([jnp.concatenate([qq[:, h * HD:(h + 1) * HD], zz], axis=1), jnp.concatenate([zz, gg[:, h * HD:(h + 1) * HD]], axis=1)], axis=0) for h in range(HH)]
        def kloop(t, c):
            r = pl.ds(pl.multiple_of(lo * KT + t * KB, KT), KB)
            new = []
            for h in range(HH):
                s = jnp.dot(kaug[h, r, :], qts[h], preferred_element_type=F32)
                dp = jnp.dot(vaug[h, r, :], gts[h], preferred_element_type=F32)
                p = jnp.exp(s)
                ds = (p * dp).astype(BF16)
                both = jnp.concatenate([ds, p.astype(BF16)], axis=1)
                acc[h, r, :] += jnp.dot(both, rhs[h], preferred_element_type=F32)
                new.append(c[h] + jnp.dot(kt[h * HD:(h + 1) * HD, r], ds, preferred_element_type=F32))
            return tuple(new)
        z = jnp.zeros((HD, QB), F32)
        c = lax.fori_loop(0, (hi_ref[qb] - lo) // (KB // KT), kloop, (z,) * HH)
        dq = (jnp.concatenate(c, axis=0) * 0.125).T
        qsum_ref[...] += jnp.sum(dq, axis=0, keepdims=True)
        dq_ref[rq, :] = dq.astype(BF16)
        return 0
    lax.fori_loop(0, nq, qloop, 0)
    def fin(t, _):
        r = pl.ds(pl.multiple_of(t * KT, KT), KT)
        sums = [acc[h, r, :] for h in range(HH)]
        for i in range(2):
            dkv_ref[i, r, :] = jnp.concatenate([x[:, i * HD:(i + 1) * HD] for x in sums], axis=1).astype(BF16)
        return 0
    lax.fori_loop(t_lo, t_hi, fin, 0)

def attend_bwd(q, kn, vn, k, v, idq, idk, lo, hi, out, grad, lse, HH, QB, KB, KT):
    n, cols = q.shape
    w = 3 * n
    HH = min(HH, cols // HD)
    wide = HH * HD
    near = pl.BlockSpec((2, n, wide), lambda g, *_: (0, 0, g))
    pairs = cols // wide
    nq = n // QB
    rows = lambda m: pl.BlockSpec((m, wide), lambda g, *_: (0, g))
    return pl.pallas_call(
        functools.partial(bwd_kernel, HH, QB, KB, KT, nq),
        grid_spec=pltpu.PrefetchScalarGridSpec(
            num_scalar_prefetch=2, grid=(pairs,),
            in_specs=[rows(n), near, near, rows(n), rows(n), pl.BlockSpec((n, 1), lambda g, *_: (0, 0)), pl.BlockSpec((w, 1), lambda g, *_: (0, 0)), rows(n), rows(n), pl.BlockSpec((1, HH, n), lambda g, *_: (g, 0, 0))],
            out_specs=[rows(n), pl.BlockSpec((2, w, wide), lambda g, *_: (0, 0, g)), pl.BlockSpec((1, wide), lambda g, *_: (0, g))],
            scratch_shapes=[pltpu.VMEM((HH, w, 128), BF16), pltpu.VMEM((HH, w, 128), BF16), pltpu.VMEM((wide, w), BF16), pltpu.VMEM((HH, 128, n), BF16), pltpu.VMEM((HH, 128, n), BF16), pltpu.VMEM((HH, w, 128), F32)]),
        out_shape=[jax.ShapeDtypeStruct((n, cols), BF16), jax.ShapeDtypeStruct((2, w, cols), BF16), jax.ShapeDtypeStruct((1, cols), F32)],
        compiler_params=pltpu.CompilerParams(vmem_limit_bytes=VMEM_LIMIT),
        cost_estimate=pl.CostEstimate(flops=5 * 10**10, bytes_accessed=10**8, transcendentals=0),
        name=N.attend_bwd,
    )(lo, hi, q, kn, vn, k, v, idq, idk, out, grad, lse)

def reach(ids_win, n, QB, KB, KT, least, most):
    w = ids_win.shape[0]
    own = ids_win[n:2 * n].reshape(n // QB, QB)
    lo = (jnp.argmax(ids_win[None, :] == own[:, :1], axis=1) // KT).astype(jnp.int32)
    hi = ((w - jnp.argmax(ids_win[::-1][None, :] == own[:, -1:], axis=1) + KT - 1) // KT).astype(jnp.int32)
    need = -(lo - hi) % (KB // KT)
    need = jnp.where(need > 0, KB // KT - need, 0)
    up = jnp.minimum(most - hi, need)
    lo, hi = lo - (need - up), hi + up
    return jnp.append(lo, jnp.min(lo)), jnp.append(hi, jnp.max(hi))


def neighbours(axis):
    peers = lax.axis_size(axis)
    up = [(i, i + 1) for i in range(peers - 1)]
    return up, [(j, i) for i, j in up]


def with_halo(array):
    up, down = neighbours(N.dp)
    return jnp.concatenate(
        [lax.ppermute(array, N.dp, up), array, lax.ppermute(array, N.dp, down)], axis=0
    )


def body(
    tokens, image_ids, cotangent, ln1_gain, ln1_bias, qkv_weight, qv_bias, proj_weight, proj_bias, scale_attn,
    ln2_gain, ln2_bias, fc1_weight, fc1_bias, fc2_weight, fc2_bias, scale_mlp,
):
    n = lax.axis_size(N.tensor)
    rows = tokens.shape[0]
    width, hidden = qkv_weight.shape[3], fc1_weight.shape[2]
    _, chunks, sub = sizes(rows, n)
    split = (n, chunks, sub)
    planes = jnp.transpose(qkv_weight, (0, 2, 1, 3))
    ids_win = with_halo(image_ids + 1)
    per = rows // TILES[3]
    place, places = lax.axis_index(N.dp), lax.axis_size(N.dp)
    least, most = jnp.where(place == 0, per, 0), jnp.where(place == places - 1, 2 * per, 3 * per)
    lo, hi = reach(ids_win, rows, *TILES[1:], least, most)
    idq, idk = ids_win[rows : 2 * rows, None], ids_win[:, None]

    dp_size = lax.axis_size(N.dp)
    made = first_block(n, dp_size, 2 * LAYERS + 1, tokens, planes, qv_bias[0], jnp.stack([ln1_gain[0], ln1_bias[0]]))
    own, hat1, sp1, a1 = made[N.after], made[N.hat1], made[N.sp1], made[N.a1]
    q, k, v = (made[name].reshape(rows, width) for name in (N.q, N.k, N.v))
    kn, vn = (made[name].reshape(2, rows, width) for name in (N.k_near, N.v_near))

    saved = []
    for level in range(LAYERS):
        kv = (kn, vn, k, v)
        attended, lse = attend_fwd(q, *kv, idq, idk, lo, hi, *TILES)
        last = level == LAYERS - 1
        after = 0 if last else level + 1
        vec = jnp.stack(
            [
                proj_bias[level], scale_attn[level], ln2_gain[level], ln2_bias[level], fc2_bias[level],
                scale_mlp[level], ln1_gain[after], ln1_bias[after],
            ]
        )
        extra = () if last else (planes, qv_bias[level + 1])
        made = forward_block(
            n, dp_size, last, level, attended, proj_weight, fc1_weight, fc2_weight, fc1_bias[level][None],
            vec, own, *extra,
        )
        keep = {name: made[name] for name in (N.u1, N.hat2, N.sp2, N.u2, N.a2, N.act, N.slope)}
        keep[N.attended] = attended.reshape(split + (width,))
        saved.append((q, kv, attended, lse, a1, hat1, sp1, keep))
        if last:
            result = made[N.after]
        else:
            own, hat1, sp1, a1 = (made[name] for name in (N.after, N.hat1, N.sp1, N.a1))
            q, k, v = (made[name].reshape(rows, width) for name in N.qkv)
            kn, vn = (made[name].reshape(2, rows, width) for name in (N.k_near, N.v_near))

    source = {N.full: cotangent.reshape(split + (D,))}
    above, grads = {}, [None] * LAYERS
    sums, narrow, dv_sums = [None] * (LAYERS + 1), [None] * LAYERS, [None] * LAYERS
    up, down = neighbours(N.dp)
    for level in reversed(range(LAYERS)):
        q, kv, attended, lse, a1, hat1, sp1, keep = saved[level]
        upper = min(level + 1, LAYERS - 1)
        vec = jnp.stack([scale_mlp[level], ln2_gain[level], scale_attn[level], ln1_gain[upper]])
        outs = backward_block(
            n, dp_size, LAYERS + level, source, above, (fc1_weight, level), (fc2_weight, level), (proj_weight, level), vec, keep,
        )
        datt, fc1b, sums[level + 1] = outs[N.datt], outs[N.fc1b], outs[N.sums]
        if above:
            grads[level + 1] = [outs["up%d_out" % (i + 1)] for i in range(4)]
            dv_sums[level + 1] = outs[N.dv_sum][0]
        flip = [(i, i ^ 2) for i in range(dp_size)]
        above = {N.up4: outs[N.g4]}
        for name in "12":
            above[N.keep + name] = outs[N.keep + name + N._out]
            got = N.got + name + N._out
            send = N.send + name + N._out
            above[N.got + name] = outs[got] if got in outs else lax.ppermute(outs[send], N.dp, flip)
        dq, dkv, q_sum = attend_bwd(
            q, *kv, idq, idk, lo, hi, attended, datt.reshape(rows, width), lse, *TILES
        )
        narrow[level] = (fc1b[0], q_sum[0])
        dkv = dkv.reshape((2, 3) + split + (width,))
        source = {
            N.dkv_in: dkv, N.dq: dq.reshape(split + (width,)), N.qkv: (planes, level), N.hat1: hat1,
            N.gm: outs[N.gm_out], N.a1: a1, N.sp1: sp1,
        }
    pad = jnp.zeros((D - width,), F32)
    flat = jnp.concatenate(
        [jnp.zeros((D,), F32)]
        + [x for i in range(1, LAYERS) for x in (dv_sums[i], pad)]
        + [x for i in range(LAYERS) for x in narrow[i]]
    )
    own_rows = -(-flat.shape[0] // (8 * D)) * 8
    flat = jnp.pad(flat, (0, own_rows * D - flat.shape[0])).reshape(own_rows, D)
    wide = 8 * (LAYERS + 1)
    base = jnp.concatenate([jnp.zeros((8, D), F32)] + sums[1:] + [flat])
    tail = backward_tail(n, dp_size, 2 * LAYERS, wide, source, above, ln1_gain[:1], base, result)
    grads[0] = [tail["up%d_out" % (i + 1)] for i in range(4)]
    grad_tokens, total = tail[N.out], tail[N.total]
    dv_total = total[wide : wide + LAYERS, :width]
    flat = total[wide + LAYERS :].reshape(-1)[: LAYERS * (hidden + width)].reshape(LAYERS, hidden + width)
    fc1b_total, qv_total = flat[:, :hidden], jnp.stack([flat[:, hidden:], dv_total], axis=1)
    stacked = lambda parts: jnp.stack([x.astype(F32) for x in parts])
    big = [
        jnp.transpose(
            stacked([x[2][:, i * width : (i + 1) * width] for x in grads for i in range(3)]).reshape(LAYERS, 3, D, width),
            (0, 2, 1, 3),
        ),
        stacked([x[3][:width] for x in grads]),
        stacked([x[1] for x in grads]),
        stacked([x[0] for x in grads]),
    ]
    total = total[:wide].reshape(LAYERS + 1, 8, D)
    upper, lower = total[1:], total[:-1]
    return (
        tail[N.out2].reshape(rows, D).astype(F32),
        grad_tokens.reshape(rows, D).astype(F32),
        lower[:, 6],
        lower[:, 7],
        big[0],
        qv_total,
        big[1],
        upper[:, 5],
        upper[:, 4],
        upper[:, 2],
        upper[:, 3],
        big[2],
        fc1b_total,
        big[3],
        upper[:, 1],
        upper[:, 0],
    )


def solution(mesh):
    cols, stack_rows = P(None, None, N.tensor), P(None, N.tensor, None)
    qkv = P(None, None, None, N.tensor)
    return jax.shard_map(
        body,
        mesh=mesh,
        in_specs=(
            P(N.dp, None), P(N.dp), P(N.dp, None), P(), P(), qkv, cols, stack_rows, P(), P(), P(), P(), cols,
            P(None, N.tensor), stack_rows, P(), P(),
        ),
        out_specs=(
            P(N.dp, None), P(N.dp, None), P(), P(), qkv, cols, stack_rows, P(), P(), P(), P(), cols,
            P(None, N.tensor), stack_rows, P(), P(),
        ),
        check_vma=False,
    )
```

```python
import functools
import jax
import jax.numpy as jnp
from jax import lax
from jax.experimental import pallas as pl
from jax.experimental.pallas import tpu as pltpu
from jax.sharding import PartitionSpec as P

HD = 64
LAYERS = 2
D = 1024
MESH = pl.DeviceIdType.MESH
F32 = jnp.float32
BF16 = jnp.bfloat16
eps = 1e-06
half_root = 0.7071067811865476
density_scale = 0.3989422804014327
BIG = 1e30
TILES = (4, 512, 512, 256)
VMEM_LIMIT = 62 * 2**20


def bit_of(index, k):
    return (index // (1 << k)) % 2


def order_bits(nbits, half):
    return tuple(range(nbits)) if half == 0 else tuple(reversed(range(nbits)))


def compose(free_bits, free_value, fixed):
    index = sum(value * (1 << k) for k, value in fixed.items())
    for place, k in enumerate(free_bits):
        index = index + ((free_value >> place) & 1) * (1 << k)
    return index


class Names:
    def __getattr__(self, key):
        return key


N = Names()


class Exchange:
    def __init__(self, n, chunks, sub):
        self.n, self.chunks, self.sub = n, chunks, sub
        self.nbits = n.bit_length() - 1
        self.half = sub // 2
        self.me = lax.axis_index(N.tensor)
        self.bits = [bit_of(self.me, k) for k in range(self.nbits)]
        self.pending = []

    def partner(self, k):
        return self.me + (1 - 2 * self.bits[k]) * (1 << k)

    def partners(self):
        return [{N.tensor: self.partner(k)} for k in range(self.nbits)]

    def rows(self, h):
        return pl.ds(h * self.half, self.half)

    def copy(self, src, dst, sems, c, h, message, k):
        return pltpu.make_async_remote_copy(
            src_ref=src,
            dst_ref=dst,
            send_sem=sems.at[0, c, h, message],
            recv_sem=sems.at[1, c, h, message],
            device_id={N.tensor: self.partner(k)},
            device_id_type=MESH,
        )

    def rs_base(self, p):
        return sum(self.n >> (q + 1) for q in range(p))

    def rs_fixed(self, order, p, flip):
        fixed = {k: self.bits[k] for k in order[:p]}
        fixed[order[p]] = 1 - self.bits[order[p]] if flip else self.bits[order[p]]
        return fixed

    def rs_places(self, order, p, f):
        places = []
        for q in range(p):
            free = order[q + 1 :]
            index = 0
            for place, k in enumerate(free):
                at = order.index(k)
                if at < p:
                    value = self.bits[k]
                elif at == p:
                    value = 1 - self.bits[k]
                else:
                    value = (f >> (at - p - 1)) & 1
                index = index + value * (1 << place)
            places.append(self.rs_base(q) + index)
        return places

    def rs_send(self, part, recv, sems, c, p):
        for h in range(2):
            order = order_bits(self.nbits, h)
            free = order[p + 1 :]
            for f in range(1 << len(free)):
                b = compose(free, f, self.rs_fixed(order, p, True))
                message = self.rs_base(p) + f
                if p > 0:
                    total = part[b, c, self.rows(h), :].astype(F32)
                    for place in self.rs_places(order, p, f):
                        total = total + recv[c, place, self.rows(h), :].astype(F32)
                    part[b, c, self.rows(h), :] = total.astype(BF16)
                cp = self.copy(
                    part.at[b, c, self.rows(h), :],
                    recv.at[c, message, self.rows(h), :],
                    sems,
                    c,
                    h,
                    message,
                    order[p],
                )
                cp.start()
                self.pending.append(cp)

    def rs_wait(self, part, recv, sems, c, p):
        for h in range(2):
            order = order_bits(self.nbits, h)
            for f in range(self.n >> (p + 1)):
                message = self.rs_base(p) + f
                self.copy(
                    part.at[0, c, self.rows(h), :],
                    recv.at[c, message, self.rows(h), :],
                    sems,
                    c,
                    h,
                    message,
                    order[p],
                ).wait_recv()

    def rs_total(self, part, recv, c):
        halves = []
        for h in range(2):
            order = order_bits(self.nbits, h)
            total = part[self.me, c, self.rows(h), :].astype(F32)
            for p in range(self.nbits):
                free = order[p + 1 :]
                place = self.rs_base(p) + sum(
                    self.bits[k] * (1 << at) for at, k in enumerate(free)
                )
                total = total + recv[c, place, self.rows(h), :].astype(F32)
            halves.append(total)
        return jnp.concatenate(halves, axis=0)

    def ag_send(self, full, sems, c, p):
        for h in range(2):
            order = order_bits(self.nbits, h)
            fixed = {k: self.bits[k] for k in order[p:]}
            for f in range(1 << p):
                b = compose(order[:p], f, fixed)
                message = (1 << p) - 1 + f
                ref = full.at[b, c, self.rows(h), :]
                cp = self.copy(ref, ref, sems, c, h, message, order[p])
                cp.start()
                self.pending.append(cp)

    def ag_wait(self, full, sems, c, p):
        for h in range(2):
            order = order_bits(self.nbits, h)
            fixed = {k: self.bits[k] for k in order[p + 1 :]}
            fixed[order[p]] = 1 - self.bits[order[p]]
            for f in range(1 << p):
                b = compose(order[:p], f, fixed)
                message = (1 << p) - 1 + f
                ref = full.at[b, c, self.rows(h), :]
                self.copy(ref, ref, sems, c, h, message, order[p]).wait_recv()

    def drain(self):
        for cp in self.pending:
            cp.wait_send()
        self.pending = []


def erf(x):
    c = jnp.clip(x, -3.832506856900711, 3.832506856900711)
    s = c * c
    top = jnp.full_like(s, 0.00022905065861350646)
    for k in (0.0034082910107109506, 0.050955695062380861, 0.18520832239976145, 1.128379143519084):
        top = top * s + k
    low = jnp.full_like(s, -1.1791602954361697e-7)
    for k in (
        0.000023547966471313185,
        0.0010179625278914885,
        0.014070470171167667,
        0.11098505178285362,
        0.49746925110067538,
        1.0,
    ):
        low = low * s + k
    return c * top / low


def gelu_pair(before):
    cumulative = 0.5 * (1.0 + erf(before * half_root))
    density = jnp.exp(-0.5 * before * before) * density_scale
    return before * cumulative, cumulative + before * density


def normalised(stream):
    centre = jnp.mean(stream, axis=-1, keepdims=True)
    centred = stream - centre
    spread = lax.rsqrt(jnp.mean(centred * centred, axis=-1, keepdims=True) + eps)
    return centred * spread, spread


def norm_back(upstream, normed, spread, gain_row):
    scaled = upstream * gain_row
    return spread * (
        scaled
        - jnp.mean(scaled, axis=-1, keepdims=True)
        - normed * jnp.mean(scaled * normed, axis=-1, keepdims=True)
    )


def chunk_of(ref, c):
    x = ref[:, c]
    return x.reshape(x.shape[0] * x.shape[1], x.shape[2])


def column_loop(width, step, fn):
    if width <= step:
        fn(pl.ds(0, width))
    else:

        def one(j, carry):
            fn(pl.ds(pl.multiple_of(j * step, step), step))
            return carry

        lax.fori_loop(0, width // step, one, 0)


def matmul_nn(x, w_ref, cols):
    return jnp.dot(x, w_ref[:, cols], preferred_element_type=F32)


def matmul_nt(x, w_ref, cols):
    return lax.dot_general(
        x, w_ref[cols, :], (((1,), (1,)), ((), ())), preferred_element_type=F32
    )


def tall(ref, cols=slice(None)):
    x = ref[..., cols]
    return x.reshape(x.shape[0] * x.shape[1] * x.shape[2], x.shape[3])


def grad_items(left, right, out, first, step=256):
    width = left.shape[3]
    step = min(step, width)

    def item(at):
        y = lax.dot_general(
            tall(left, slice(at, at + step)), tall(right), (((0,), (0,)), ((), ())), preferred_element_type=F32
        )
        out[first + at : first + at + step, :] = y.astype(BF16)

    return [functools.partial(item, at) for at in range(0, width, step)]


def with_items(ex, stage, items):
    share = -(-len(items) // ex.chunks)

    def both(c):
        for item in items[c * share : (c + 1) * share]:
            item()
        stage(c)

    return both


def rs_stages(ex, part, recv, sems):
    stages = []
    for p in range(1, ex.nbits):

        def stage(c, p=p):
            ex.rs_wait(part, recv, sems, c, p - 1)
            ex.rs_send(part, recv, sems, c, p)

        stages.append(stage)
    return stages


def ag_stages(ex, full, sems):
    stages = []
    for p in range(1, ex.nbits):

        def stage(c, p=p):
            ex.ag_wait(full, sems, c, p - 1)
            ex.ag_send(full, sems, c, p)

        stages.append(stage)
    return stages


def sizes(rows, n):
    block = rows // n
    chunks = 3 if block % 96 == 0 else (2 if block % 64 == 0 else 1)
    return block, chunks, block // chunks


class Total:
    def __init__(self, bufs, recv, sems, dp_size, n, wide):
        self.bufs, self.recv, self.sems, self.wide = bufs, recv, sems, wide
        self.axes = [(N.dp, k) for k in range(dp_size.bit_length() - 1)]
        self.axes += [(N.tensor, k) for k in range(n.bit_length() - 1)]
        self.copies = []

    def target(self, i):
        axis, k = self.axes[i]
        me = lax.axis_index(axis)
        return {axis: me + (1 - 2 * bit_of(me, k)) * (1 << k)}

    def partners(self):
        return [self.target(i) for i, (axis, _) in enumerate(self.axes) if axis == N.dp]

    def start(self, i):
        cp = pltpu.make_async_remote_copy(
            src_ref=self.bufs.at[i],
            dst_ref=self.recv.at[i],
            send_sem=self.sems.at[0, i],
            recv_sem=self.sems.at[1, i],
            device_id=self.target(i),
            device_id_type=MESH,
        )
        cp.start()
        self.copies.append(cp)

    def step(self, i):
        self.copies[i].wait_recv()
        axis, _ = self.axes[i]
        total = self.bufs[i] + self.recv[i]
        if axis == N.tensor:
            row = lax.broadcasted_iota(jnp.int32, total.shape, 0)
            total = jnp.where(row < self.wide, total, self.bufs[i])
        self.bufs[i + 1] = total
        if i + 1 < len(self.axes):
            self.start(i + 1)

    def drain(self):
        for cp in self.copies:
            cp.wait_send()


def run_stages(ex, stages, extra=()):
    extra = sorted(extra, key=lambda pair: pair[0])
    slot = 0
    for stage in stages:
        for c in range(ex.chunks):
            while extra and extra[0][0] <= slot:
                extra.pop(0)[1]()
            stage(c)
            slot += 1
    for _, thunk in extra:
        thunk()


def meet(partners):
    sem = pltpu.get_barrier_semaphore()
    for partner in partners:
        pl.semaphore_signal(sem, inc=1, device_id=partner, device_id_type=MESH)
    pl.semaphore_wait(sem, len(partners))


class Refs:
    def __init__(self):
        self.loads, self.targets, self.stores = {}, {}, []

    def need(self, *names):
        for name in names:
            if name in self.loads:
                self.loads.pop(name).wait()

    def store(self, name, index=()):
        cp = pltpu.make_async_copy(
            getattr(self, name).at[index] if index else getattr(self, name),
            self.targets[name].at[index] if index else self.targets[name],
            self.store_sems.at[len(self.stores)],
        )
        cp.start()
        self.stores.append(cp)

    def finish(self):
        self.need(*list(self.loads))
        for cp in self.stores:
            cp.wait()


def call(kernel, name, collective_id, ins, outs, scratch, flops):
    late_in = [
        (k, jax.ShapeDtypeStruct(a.shape[1:] if type(late) is int else a.shape, a.dtype))
        for k, a, late in ins
        if late is True or type(late) is int
    ]
    late_out = [(k, shape, dtype) for k, shape, dtype, late in outs if late is True]

    def entry(*refs):
        refs = list(refs)
        take = lambda count: [refs.pop(0) for _ in range(count)]
        r = Refs()
        r.sources = {}
        in_refs, out_refs = take(len(ins)), take(len(outs))
        in_bufs, out_bufs = take(len(late_in)), take(len(late_out))
        load_sems, r.store_sems = take(2)
        bufs = {k: b for (k, _), b in zip(late_in, in_bufs)}
        for (k, _, late), ref in zip(ins, in_refs):
            if late == N.far:
                r.sources[k] = ref
                continue
            fetched = late is True or type(late) is int
            setattr(r, k, bufs[k] if fetched else ref)
            if fetched:
                cp = pltpu.make_async_copy(ref.at[late] if type(late) is int else ref, bufs[k], load_sems.at[len(r.loads)])
                cp.start()
                r.loads[k] = cp
        bufs = {k: b for (k, _, _), b in zip(late_out, out_bufs)}
        for (k, _), ref in zip(scratch, take(len(scratch))):
            setattr(r, k, ref)
        for (k, _, _, late), ref in zip(outs, out_refs):
            if late == N.far:
                r.targets[k] = ref
                continue
            setattr(r, k, getattr(r, late) if isinstance(late, str) else bufs[k] if late else ref)
            if late:
                r.targets[k] = ref
        kernel(r)
        r.finish()

    space = lambda late: pl.BlockSpec(memory_space=pltpu.VMEM if late is False else pl.ANY)
    result = pl.pallas_call(
        entry,
        out_shape=[jax.ShapeDtypeStruct(shape, dtype) for _, shape, dtype, _ in outs],
        in_specs=[space(late) for _, _, late in ins],
        out_specs=[space(late) for _, _, _, late in outs],
        scratch_shapes=[pltpu.VMEM(a.shape, a.dtype) for _, a in late_in]
        + [pltpu.VMEM(shape, dtype) for _, shape, dtype in late_out]
        + [pltpu.SemaphoreType.DMA((max(len(late_in), 1),)), pltpu.SemaphoreType.DMA((64,))]
        + [spec for _, spec in scratch],
        compiler_params=pltpu.CompilerParams(
            collective_id=collective_id, has_side_effects=True, vmem_limit_bytes=VMEM_LIMIT
        ),
        cost_estimate=pl.CostEstimate(flops=flops, bytes_accessed=10**8, transcendentals=0),
        name=name,
    )(*[a for _, a, _ in ins])
    return dict(zip([k for k, _, _, _ in outs], result))


def comm_scratch(n, chunks, sub, tag):
    return [
        (N.part + tag, pltpu.VMEM((n, chunks, sub, D), BF16)),
        (N.recv + tag, pltpu.VMEM((chunks, n - 1, sub, D), BF16)),
    ]


def sem_scratch(stages, n, chunks):
    return [(N.sems, pltpu.SemaphoreType.DMA((stages, 2, chunks, 2, n - 1)))]


class Halo:
    def __init__(self, sems, dp_size):
        self.sems, self.size = sems, dp_size
        self.me = lax.axis_index(N.dp)
        self.has = (self.me < dp_size - 1, self.me > 0)
        self.pending = []

    def partners(self):
        return [{N.dp: (self.me + step) % self.size} for step in (1, self.size - 1)]

    def copy(self, src, dst, way, message):
        step = 1 if way == 0 else -1
        return pltpu.make_async_remote_copy(
            src_ref=src,
            dst_ref=dst,
            send_sem=self.sems.at[0, way, message],
            recv_sem=self.sems.at[1, way, message],
            device_id={N.dp: self.me + step},
            device_id_type=MESH,
        )

    def send(self, src, dst, way, message):
        cp = self.copy(src, dst, way, message)

        @pl.when(self.has[way])
        def _():
            cp.start()

        self.pending.append((cp, way))

    def wait(self, dst, way, message):
        @pl.when(self.has[1 - way])
        def _():
            self.copy(dst, dst, way, message).wait_recv()

    def drain(self):
        for cp, way in self.pending:

            @pl.when(self.has[way])
            def _(cp=cp):
                cp.wait_send()


class GradSum:
    def __init__(self, arrays, sems, dp_size):
        self.arrays, self.sems = arrays, sems
        self.local = {}
        self.k = dp_size.bit_length() - 1
        self.me = lax.axis_index(N.dp)
        self.bits = [bit_of(self.me, k) for k in range(self.k)]
        self.pending = []

    def partner(self, k):
        return {N.dp: self.me + (1 - 2 * self.bits[k]) * (1 << k)}

    def partners(self):
        return [self.partner(k) for k in range(self.k)]

    def offset(self, rows, k):
        return sum(self.bits[i] * (rows >> (i + 1)) for i in range(k))

    def copy(self, src, dst, a, message, k):
        return pltpu.make_async_remote_copy(
            src_ref=src,
            dst_ref=dst,
            send_sem=self.sems.at[0, a, message],
            recv_sem=self.sems.at[1, a, message],
            device_id=self.partner(k),
            device_id_type=MESH,
        )

    def recv_rows(self, a, k):
        rows, _, _, _, start, _ = self.arrays[a]
        return (rows >> start) - (rows >> k)

    def here(self, a, at, size):
        rows, _, _, _, start, _ = self.arrays[a]
        return pl.ds(pl.multiple_of(at - self.offset(rows, start), 16), size)

    def add(self, a, base, size, k):
        rows, grad, recv, _, start, _ = self.arrays[a]
        step = 32 if size % 32 == 0 else 16

        def block(i, carry):
            at = base + i * step
            here = self.here(a, at, step)
            total = grad[here, :].astype(F32)
            for j in range(start, k):
                there = at - self.offset(rows, j + 1) + self.recv_rows(a, j)
                total = total + recv[pl.ds(pl.multiple_of(there, 16), step), :].astype(F32)
            grad[here, :] = total.astype(BF16)
            return carry

        lax.fori_loop(0, size // step, block, 0)

    def merge(self, a):
        rows, grad, _, _, start, pieces = self.arrays[a]
        size = rows >> start
        step = 32 if size % 32 == 0 else 16

        def block(i, carry):
            here = pl.ds(pl.multiple_of(i * step, 16), step)
            grad[here, :] = sum(x[here, :].astype(F32) for x in pieces).astype(BF16)
            return carry

        lax.fori_loop(0, size // step, block, 0)

    def send(self, a, k):
        rows, grad, recv, _, start, _ = self.arrays[a]
        size = rows >> (k + 1)
        base = self.offset(rows, k) + (1 - self.bits[k]) * size
        if k > start:
            self.add(a, base, size, k)
        cp = self.copy(
            grad.at[self.here(a, base, size), :], recv.at[pl.ds(self.recv_rows(a, k), size), :], a, k, k
        )
        cp.start()
        self.pending.append(cp)

    def wait(self, a, k):
        rows, _, recv, _, _, _ = self.arrays[a]
        ref = recv.at[pl.ds(self.recv_rows(a, k), rows >> (k + 1)), :]
        self.copy(ref, ref, a, k, k).wait_recv()

    def split(self, a, keep, send):
        rows, grad, recv, _, _, _ = self.arrays[a]
        size = rows >> 2
        step = 32 if size % 32 == 0 else 16
        for out, bit in ((keep, self.bits[1]), (send, 1 - self.bits[1])):

            def block(i, carry, out=out, bit=bit):
                at = bit * size + i * step
                mine = grad[pl.ds(pl.multiple_of(self.bits[0] * 2 * size + at, 16), step), :].astype(F32)
                total = mine + recv[pl.ds(pl.multiple_of(at, 16), step), :].astype(F32)
                out[pl.ds(pl.multiple_of(i * step, 16), step), :] = total.astype(BF16)
                return carry

            lax.fori_loop(0, size // step, block, 0)

    def own(self, a, k, mine):
        rows, _, _, out, _, _ = self.arrays[a]
        size = rows >> (k + 1)
        base = self.offset(rows, k + 1) if mine else self.offset(rows, k) + (1 - self.bits[k]) * size
        return out.at[pl.ds(pl.multiple_of(base, 16), size), :]

    def gather_send(self, a, k):
        ref = self.own(a, k, True)
        src = ref
        if k == self.k - 1:
            rows, grad = self.arrays[a][:2]
            src = grad.at[self.here(a, self.offset(rows, self.k), rows >> self.k), :]
            self.local[a] = pltpu.make_async_copy(src, ref, self.sems.at[0, a, 2 * self.k])
            self.local[a].start()
        elif k == self.k - 2:
            self.local[a].wait()
        cp = self.copy(src, ref, a, self.k + k, k)
        cp.start()
        self.pending.append(cp)

    def gather_wait(self, a, k):
        ref = self.own(a, k, False)
        self.copy(ref, ref, a, self.k + k, k).wait_recv()

    def steps(self, a):
        last, start = self.k - 1, self.arrays[a][4]

        def first():
            if start:
                self.merge(a)
            self.send(a, start)

        def halve(k):
            self.wait(a, k - 1)
            self.send(a, k)

        def turn():
            rows = self.arrays[a][0]
            self.wait(a, last)
            self.add(a, self.offset(rows, self.k), rows >> self.k, self.k)
            self.gather_send(a, last)

        def double(k):
            self.gather_wait(a, k + 1)
            self.gather_send(a, k)

        out = [first] + [functools.partial(halve, k) for k in range(start + 1, self.k)] + [turn]
        out += [functools.partial(double, k) for k in reversed(range(last))]
        return out + [functools.partial(self.gather_wait, a, 0)]

    def drain(self):
        for cp in self.pending:
            cp.wait_send()


def grad_scratch(shapes, dp_size):
    steps = 2 * (dp_size.bit_length() - 1) + 1
    out = [
        ("grad_recv%d" % i, pltpu.VMEM(((rows >> start) - rows // dp_size, cols), BF16))
        for i, (rows, cols, start) in enumerate(shapes)
    ]
    return out + [(N.grad_sems, pltpu.SemaphoreType.DMA((2, len(shapes), steps)))]


def grad_rows(rows, dp_size):
    unit = 16 * dp_size
    return -(-rows // unit) * unit


def placed(steps, slots):
    slots = list(slots)
    while len(slots) < len(steps):
        slots.append(slots[-1] + 2)
    return list(zip(slots, steps))


def forward_kernel(n, dp_size, chunks, sub, last, r):
    ex = Exchange(n, chunks, sub)
    if last:
        meet(ex.partners())
    else:
        halo = Halo(r.halo_sems, dp_size)
        meet(ex.partners() + halo.partners())
    sems = r.sems
    row = lambda i: r.vec[i : i + 1, :]
    full2 = None if last else r.a1

    def pre(c):
        r.need(N.proj)

        def cols(j):
            y = matmul_nn(chunk_of(r.attended, c), r.proj, j)
            r.part1[:, c, :, j] = y.astype(BF16).reshape(n, sub, -1)

        column_loop(D, 256, cols)
        ex.rs_send(r.part1, r.recv1, sems.at[0], c, 0)

    def own1(c):
        r.need(N.stream)
        ex.rs_wait(r.part1, r.recv1, sems.at[0], c, ex.nbits - 1)
        u1 = ex.rs_total(r.part1, r.recv1, c) + row(0)
        r.u1[c] = u1
        middle = r.stream[c] + row(1) * u1
        r.stream[c] = middle
        hat, spread = normalised(middle)
        r.hat2[c] = hat
        r.sp2[c] = spread
        r.a2[ex.me, c] = (hat * row(2) + row(3)).astype(BF16)
        ex.ag_send(r.a2, sems.at[1], c, 0)
        r.store(N.u1, (c,))
        r.store(N.hat2, (c,))

    def mid(c):
        r.need(N.fc1, N.fc2)
        ex.ag_wait(r.a2, sems.at[1], c, ex.nbits - 1)

        def hidden(j):
            before = matmul_nn(chunk_of(r.a2, c), r.fc1, j) + r.fc1_bias[:, j]
            a, s = gelu_pair(before)
            r.act[:, c, :, j] = a.astype(BF16).reshape(n, sub, -1)
            r.slope[:, c, :, j] = s.astype(BF16).reshape(n, sub, -1)

        column_loop(r.fc1.shape[1], 256, hidden)

        def cols(j):
            y = matmul_nn(chunk_of(r.act, c), r.fc2, j)
            r.part2[:, c, :, j] = y.astype(BF16).reshape(n, sub, -1)

        column_loop(D, 256, cols)
        ex.rs_send(r.part2, r.recv2, sems.at[2], c, 0)
        for name in (N.a2, N.act, N.slope):
            r.store(name, (slice(None), c))

    def own2(c):
        ex.rs_wait(r.part2, r.recv2, sems.at[2], c, ex.nbits - 1)
        u2 = ex.rs_total(r.part2, r.recv2, c) + row(4)
        r.u2[c] = u2
        after = r.stream[c] + row(5) * u2
        r.after[c] = after.astype(r.after.dtype)
        r.store(N.after, (c,))
        r.store(N.u2, (c,))
        if not last:
            hat, spread = normalised(after)
            r.hat1[c] = hat
            r.sp1[c] = spread
            full2[ex.me, c] = (hat * row(6) + row(7)).astype(BF16)
            r.store(N.hat1, (c,))
            ex.ag_send(full2, sems.at[3], c, 0)

    def post(c):
        ex.ag_wait(full2, sems.at[3], c, ex.nbits - 1)
        r.need(N.qkv)
        x = chunk_of(full2, c)
        width = r.q.shape[3]
        for i, name in ((1, N.k), (2, N.v), (0, N.q)):
            y = jnp.dot(x, r.qkv[i], preferred_element_type=F32)
            if i != 1:
                y = y + r.qv_bias[i // 2 : i // 2 + 1, :]
            getattr(r, name)[:, c] = y.astype(BF16).reshape(n, sub, width)
            r.store(name, (slice(None), c))
            if i:
                for way in range(2):
                    halo.send(
                        getattr(r, name).at[:, c], r.targets[name + N._near].at[way, :, c], way, (i - 1) * chunks + c
                    )
        r.store(N.a1, (slice(None), c))

    run_stages(
        ex,
        [pre]
        + rs_stages(ex, r.part1, r.recv1, sems.at[0])
        + [own1]
        + ag_stages(ex, r.a2, sems.at[1])
        + [mid]
        + rs_stages(ex, r.part2, r.recv2, sems.at[2])
        + [own2]
        + ([] if last else ag_stages(ex, full2, sems.at[3]) + [post]),
    )
    if not last:
        for i, name in enumerate((N.k_near, N.v_near)):
            for c in range(chunks):
                for way in range(2):
                    halo.wait(r.targets[name].at[way, :, c], way, i * chunks + c)
        halo.drain()
    ex.drain()


def first_kernel(n, dp_size, chunks, sub, r):
    halo = Halo(r.halo_sems, dp_size)
    meet(halo.partners())
    me = lax.axis_index(N.tensor)
    r.need(N.tokens, N.qkv)
    width = r.q.shape[3]
    for c in range(chunks):

        def norm(b, carry, c=c):
            hat, _ = normalised(r.tokens[b, c].astype(F32))
            r.a1[b, c] = (hat * r.vec[0:1, :] + r.vec[1:2, :]).astype(BF16)
            return carry

        lax.fori_loop(0, n, norm, 0)
        x = chunk_of(r.a1, c)
        for i, name in ((1, N.k), (2, N.v), (0, N.q)):
            y = jnp.dot(x, r.qkv[i], preferred_element_type=F32)
            if i != 1:
                y = y + r.qv_bias[i // 2 : i // 2 + 1, :]
            getattr(r, name)[:, c] = y.astype(BF16).reshape(n, sub, width)
            r.store(name, (slice(None), c))
            if i:
                for way in range(2):
                    halo.send(
                        getattr(r, name).at[:, c], r.targets[name + N._near].at[way, :, c], way, (i - 1) * chunks + c
                    )
        r.store(N.a1, (slice(None), c))
        own = r.tokens[me, c].astype(F32)
        r.after[c] = own
        hat, spread = normalised(own)
        r.hat1[c] = hat
        r.sp1[c] = spread
    for i, name in enumerate((N.k_near, N.v_near)):
        for c in range(chunks):
            for way in range(2):
                halo.wait(r.targets[name].at[way, :, c], way, i * chunks + c)
    halo.drain()


def first_block(n, dp_size, collective_id, tokens, qkv, qv_bias, vec):
    rows = tokens.shape[0]
    _, chunks, sub = sizes(rows, n)
    width = qv_bias.shape[1]
    split = lambda cols: (n, chunks, sub, cols)
    mine = (chunks, sub, D)
    outs = [(N.after, mine, F32, False), (N.hat1, mine, F32, False), (N.sp1, (chunks, sub, 1), F32, False)]
    outs += [(N.a1, split(D), BF16, True)] + [(k, split(width), BF16, True) for k in (N.q, N.k, N.v)]
    outs += [(k, (2,) + split(width), BF16, N.far) for k in (N.k_near, N.v_near)]
    return call(
        functools.partial(first_kernel, n, dp_size, chunks, sub),
        N.first_block,
        collective_id,
        [(N.tokens, tokens.reshape(split(D)), True), (N.qkv, qkv, 0), (N.qv_bias, qv_bias, False), (N.vec, vec, False)],
        outs,
        [(N.halo_sems, pltpu.SemaphoreType.DMA((2, 2, 2 * chunks)))],
        2 * rows * D * 3 * width,
    )


def forward_block(n, dp_size, last, level, attended, proj, fc1, fc2, fc1_bias, vec, stream, qkv=None, qv_bias=None):
    rows, width = attended.shape
    block, chunks, sub = sizes(rows, n)
    hidden = fc1.shape[2]
    split = lambda cols: (n, chunks, sub, cols)
    mine = (chunks, sub, D)
    ins = [
        (N.attended, attended.reshape(split(width)), False), (N.proj, proj, level), (N.stream, stream.reshape(mine), True),
        (N.fc1, fc1, level), (N.fc2, fc2, level), (N.fc1_bias, fc1_bias, False), (N.vec, vec, False),
    ]
    outs = [
        (N.u1, mine, F32, True), (N.hat2, mine, F32, True), (N.sp2, (chunks, sub, 1), F32, False),
        (N.u2, mine, F32, True), (N.a2, split(D), BF16, True), (N.act, split(hidden), BF16, True),
        (N.slope, split(hidden), BF16, True),
    ]
    scratch = comm_scratch(n, chunks, sub, "1") + comm_scratch(n, chunks, sub, "2")
    if last:
        outs += [(N.after, mine, BF16, True)]
    else:
        ins += [(N.qkv, qkv, level + 1), (N.qv_bias, qv_bias, False)]
        outs += [(N.after, mine, F32, True), (N.hat1, mine, F32, True), (N.sp1, (chunks, sub, 1), F32, False)]
        outs += [(N.a1, split(D), BF16, True)] + [(k, split(width), BF16, True) for k in N.qkv]
        outs += [(k, (2,) + split(width), BF16, N.far) for k in (N.k_near, N.v_near)]
        scratch += [(N.halo_sems, pltpu.SemaphoreType.DMA((2, 2, 2 * chunks)))]
    return call(
        functools.partial(forward_kernel, n, dp_size, chunks, sub, last),
        N.forward_last if last else N.forward_block,
        level,
        ins,
        outs,
        scratch + sem_scratch(4, n, chunks),
        2 * rows * D * (2 * hidden + 4 * width),
    )


def add_rows(ref, i, value):
    ref[i : i + 1, :] += jnp.sum(value, axis=0, keepdims=True)


def input_norm_own(ex, r, c, gain, sums):
    r.need(N.hat1, N.gm)
    ex.rs_wait(r.part, r.recv, r.sems.at[0], c, ex.nbits - 1)
    da1 = ex.rs_total(r.part, r.recv, c)
    add_rows(sums, 6, da1 * r.hat1[c])
    add_rows(sums, 7, da1)
    return r.gm[c] + norm_back(da1, r.hat1[c], r.sp1[c], gain)


def send_home(halo, r, chunks):
    cp = pltpu.make_async_copy(r.sources[N.dkv_in].at[:, 1], r.dkv, r.dkv_sem)
    cp.start()
    r.loads[N.dkv] = cp
    for c in range(chunks):
        for way in range(2):
            for i in range(2):
                src = r.sources[N.dkv_in].at[i, 2 - 2 * way, :, c]
                halo.send(src, near_part(r, way, i, c), way, 2 * c + i)


def near_part(r, way, i, c):
    width = r.dq.shape[3]
    return r.near.at[:, c, :, pl.ds((2 * way + i) * width, width)]


def input_grad_chunk(ex, halo, r, c):
    r.need(N.dq, N.dkv, N.qkv)
    width = r.dq.shape[3]
    for way in range(2):
        for i in range(2):
            halo.wait(near_part(r, way, i, c), way, 2 * c + i)
    r.dqkv[:, c, :, :width] = r.dq[:, c]
    for i in range(2):
        cols = slice((i + 1) * width, (i + 2) * width)

        for b in range(ex.n):
            r.total_kv[...] = r.dkv[i, b, c].astype(F32)
            for way in range(2):

                @pl.when(halo.has[1 - way])
                def _():
                    first = (2 * way + i) * width
                    r.total_kv[...] += r.near[b, c, :, first : first + width].astype(F32)

            total = r.total_kv[...]
            if i:
                r.dv_sum[...] += jnp.sum(total, axis=0, keepdims=True)
            r.dqkv[b, c, :, cols] = total.astype(BF16)

    def cols(j):
        x = chunk_of(r.dqkv, c)
        y = sum(
            lax.dot_general(
                x[:, i * width : (i + 1) * width], r.qkv[i, j, :], (((1,), (1,)), ((), ())), preferred_element_type=F32
            )
            for i in range(3)
        )
        r.part[:, c, :, j] = y.astype(BF16).reshape(ex.n, ex.sub, -1)

    column_loop(D, 256, cols)
    ex.rs_send(r.part, r.recv, r.sems.at[0], c, 0)


def backward_kernel(n, dp_size, chunks, sub, first, r):
    ex = Exchange(n, chunks, sub)
    sems, part, recv = r.sems, r.part, r.recv
    row = lambda i: r.vec[i : i + 1, :]
    if first:
        meet(ex.partners() + [{N.dp: dp_partner(0)}, {N.dp: dp_partner(1)}])
    else:
        halo = Halo(r.halo_sems, dp_size)
        gs = GradSum(upper_arrays(r), r.grad_sems, dp_size)
        meet(ex.partners() + gs.partners() + halo.partners())
        r.near = r.e1
        send_home(halo, r, chunks)
        r.dv_sum[...] = jnp.zeros_like(r.dv_sum)
    first_arrays = [(x.shape[0], x, recv, None, 0, ()) for x, recv in ((r.g1, r.core_recv0), (r.g2, r.core_recv1))]
    first_sum = GradSum(first_arrays, r.core_sems, dp_size)
    r.sums[...] = jnp.zeros_like(r.sums)
    r.fc1b[...] = jnp.zeros_like(r.fc1b)
    width, hidden_size = r.proj.shape[0], r.fc1.shape[1]
    if r.g4.shape[0] > width:
        r.g4[width:, :] = jnp.zeros((r.g4.shape[0] - width, D), BF16)

    def pre(c):
        input_grad_chunk(ex, halo, r, c)

    def own0(c):
        r.need(N.u2)
        g = input_norm_own(ex, r, c, row(3), r.sums)
        add_rows(r.sums, 0, g * r.u2[c])
        add_rows(r.sums, 1, g * row(0))
        r.gm[c] = g
        r.full[ex.me, c] = (g * row(0)).astype(BF16)
        ex.ag_send(r.full, sems.at[1], c, 0)

    def mid(c):
        r.need(N.full, N.fc2, N.slope, N.fc1, N.u2, N.gm)
        if not first and c == 0:
            ex.drain()
        if first:
            g = r.full[ex.me, c].astype(F32)
            r.gm[c] = g

            def scaled(b, carry):
                r.full[b, c] = (r.full[b, c].astype(F32) * row(0)).astype(BF16)
                return carry

            lax.fori_loop(0, n, scaled, 0)
            add_rows(r.sums, 0, g * r.u2[c])
            add_rows(r.sums, 1, g * row(0))
        else:
            ex.ag_wait(r.full, sems.at[1], c, ex.nbits - 1)

        def hidden(j):
            y = matmul_nt(chunk_of(r.full, c), r.fc2, j)
            w = y.shape[1]
            db = y * r.slope[:, c, :, j].astype(F32).reshape(n * sub, w)
            r.fc1b[:, j] += jnp.sum(db, axis=0, keepdims=True)
            r.slope[:, c, :, j] = db.astype(BF16).reshape(n, sub, w)

        column_loop(hidden_size, 256, hidden)

        def cols(j):
            y = matmul_nt(chunk_of(r.slope, c), r.fc1, j)
            part[:, c, :, j] = y.astype(BF16).reshape(n, sub, -1)

        column_loop(D, 256, cols)
        ex.rs_send(part, recv, sems.at[2], c, 0)

    def own1(c):
        r.need(N.hat2, N.u1)
        ex.rs_wait(part, recv, sems.at[2], c, ex.nbits - 1)
        da2 = ex.rs_total(part, recv, c)
        hat = r.hat2[c]
        add_rows(r.sums, 2, da2 * hat)
        add_rows(r.sums, 3, da2)
        gm = r.gm[c] + norm_back(da2, hat, r.sp2[c], row(1))
        r.gm[c] = gm
        add_rows(r.sums, 4, gm * r.u1[c])
        add_rows(r.sums, 5, gm * row(2))
        r.e1[ex.me, c] = (gm * row(2)).astype(BF16)
        ex.ag_send(r.e1, sems.at[3], c, 0)
        r.store(N.gm_out, (c,))

    def post(c):
        r.need(N.proj)
        ex.ag_wait(r.e1, sems.at[3], c, ex.nbits - 1)
        y = matmul_nt(chunk_of(r.e1, c), r.proj, slice(None))
        r.datt[:, c] = y.astype(BF16).reshape(n, sub, -1)
        r.store(N.datt, (slice(None), c))

    stages, extra = [], []
    if not first:
        made = [lambda: r.need(N.a1)] + grad_items(r.a1, r.dqkv, r.up3, 0)
        stages = [pre] + rs_stages(ex, part, recv, sems.at[0]) + [own0] + ag_stages(ex, r.full, sems.at[1])
        stages[1] = with_items(ex, stages[1], made)
        r.act = r.a1.at[:, :, :, pl.ds(0, hidden_size)]

        def fetch_act():
            cp = pltpu.make_async_copy(r.sources[N.act], r.act, r.act_sem)
            cp.start()
            r.loads[N.act] = cp

        extra += [(2 * chunks, fetch_act)]
        extra += [(3, lambda: r.need(N.keep1, N.got1, N.keep2, N.got2, N.up4))]
        extra += placed_sums(gs)
    gathers = ag_stages(ex, r.e1, sems.at[3])
    sums2 = rs_stages(ex, part, recv, sems.at[2])
    sums2[0] = with_items(ex, sums2[0], [lambda: r.need(N.act)] + grad_items(r.act, r.full, r.g1, 0))
    made = [lambda: r.need(N.a2)] + grad_items(r.a2, r.slope, r.g2, 0)
    stages += [mid] + sums2 + [with_items(ex, own1, made)] + gathers + [post]
    end = len(stages) * chunks
    behind = end - chunks * (1 + len(gathers))

    def part_of(a):
        first_sum.wait(a, 0)
        names = ((N.keep1, N.send1), (N.keep2, N.send2))[a]
        first_sum.split(a, getattr(r, names[0] + N._out), getattr(r, names[1] + N._out))
        r.store(names[0] + N._out)
        got = r.targets[(N.got1_out, N.got2_out)[a]]
        cp = first_sum.copy(getattr(r, names[1] + N._out), got, a, 1, 1)
        cp.start()
        first_sum.pending.append(cp)
        arrivals.append(cp)

    arrivals = []
    extra += [(behind - chunks, lambda: first_sum.send(0, 0)), (behind - chunks + 1, lambda: part_of(0))]
    extra += [(behind, lambda: first_sum.send(1, 0)), (behind + 1, lambda: part_of(1))]
    run_stages(ex, stages, extra)
    r.need(N.attended)
    for item in grad_items(r.attended, r.e1, r.g4, 0):
        item()
    if not first:
        gs.drain()
        halo.drain()
    for cp in arrivals:
        cp.wait_recv()
    first_sum.drain()
    ex.drain()


def dp_partner(k):
    me = lax.axis_index(N.dp)
    return me + (1 - 2 * bit_of(me, k)) * (1 << k)


def tail_sums(gs):
    return (
        placed(gs.steps(0), (3, 6, 10, 13, 16))
        + placed(gs.steps(1), (4, 9, 13, 15.5, 17))
        + placed(gs.steps(2), (6, 7, 9, 12, 15, 16, 18))
        + placed(gs.steps(3), (3, 5, 7, 10, 12, 14, 17))
    )


def placed_sums(gs):
    return (
        placed(gs.steps(0), (3, 9, 15, 21, 25))
        + placed(gs.steps(1), (4, 10, 16, 22, 26))
        + placed(gs.steps(2), (6, 7, 11, 17, 20, 24, 27))
        + placed(gs.steps(3), (3, 5, 8, 12, 14, 18, 23))
    )


def upper_arrays(r):
    pieces = ((r.keep1, r.got1), (r.keep2, r.got2), (), ())
    return [
        (
            r.targets["up%d_out" % (i + 1)].shape[0],
            getattr(r, "up%d" % (i + 1)),
            getattr(r, "grad_recv%d" % i),
            r.targets["up%d_out" % (i + 1)],
            2 if x else 0,
            x,
        )
        for i, x in enumerate(pieces)
    ]


def upper_buffers(above, width, dp_size):
    shapes = [(4 * x.shape[0], x.shape[1]) for x in (above[N.keep1], above[N.keep2])]
    shapes += [(D, 3 * width), above[N.up4].shape]
    scratch = [(N.up1, pltpu.VMEM(above[N.keep1].shape, BF16)), (N.up2, pltpu.VMEM(above[N.keep2].shape, BF16))]
    scratch += [(N.up3, pltpu.VMEM(shapes[2], BF16))]
    scratch += grad_scratch([x + (start,) for x, start in zip(shapes, (2, 2, 0, 0))], dp_size)
    return scratch, [("up%d_out" % (i + 1), x, BF16, N.far) for i, x in enumerate(shapes)]


def home_buffers(n, chunks, sub, width):
    split = (n, chunks, sub)
    return [
        (N.dqkv, pltpu.VMEM(split + (3 * width,), BF16)),
        (N.total_kv, pltpu.VMEM((sub, width), F32)),
        (N.dkv, pltpu.VMEM((2,) + split + (width,), BF16)),
        (N.dkv_sem, pltpu.SemaphoreType.DMA),
        (N.halo_sems, pltpu.SemaphoreType.DMA((2, 2, 2 * chunks))),
    ]


def backward_block(n, dp_size, collective_id, source, above, fc1, fc2, proj, vec, saved):
    first = not above
    _, chunks, sub, hidden = saved[N.slope].shape
    width = proj[0].shape[1]
    split = lambda cols: (n, chunks, sub, cols)
    mine = (chunks, sub, D)
    ins = list(source.items()) + list(above.items()) + [(N.fc2, fc2), (N.slope, saved[N.slope]), (N.fc1, fc1)]
    ins += [(k, saved[k]) for k in (N.u2, N.act, N.a2, N.hat2, N.u1, N.sp2, N.attended)] + [(N.proj, proj), (N.vec, vec)]
    outs = [
        (N.datt, split(width), BF16, True), (N.gm_out, mine, F32, N.gm), (N.sums, (8, D), F32, False),
        (N.fc1b, (1, hidden), F32, False), (N.g4, (grad_rows(width, dp_size), D), BF16, False),
    ]
    quarters = []
    for i, (rows, cols) in enumerate(((hidden, D), (D, hidden))):
        keep, send, got = ((N.keep1_out, N.send1_out, N.got1_out), (N.keep2_out, N.send2_out, N.got2_out))[i]
        quarter = (rows // 4, cols)
        outs += [(keep, quarter, BF16, True)]
        quarters += [(send, pltpu.VMEM(quarter, BF16))]
        outs += [(got, quarter, BF16, N.far)]
    scratch = quarters + comm_scratch(n, chunks, sub, "") + [(N.e1, pltpu.VMEM(split(D), BF16))] + sem_scratch(4, n, chunks)
    scratch += [(N.g1, pltpu.VMEM((hidden, D), BF16)), (N.g2, pltpu.VMEM((D, hidden), BF16))]
    scratch += [(N.core_recv0, pltpu.VMEM((hidden // 2, D), BF16)), (N.core_recv1, pltpu.VMEM((D // 2, hidden), BF16))]
    scratch += [(N.core_sems, pltpu.SemaphoreType.DMA((2, 2, 2 * (dp_size.bit_length() - 1))))]
    if first:
        scratch += [(N.gm, pltpu.VMEM(mine, F32))]
    else:
        scratch += [(N.act_sem, pltpu.SemaphoreType.DMA)]
        scratch += [(N.full, pltpu.VMEM(split(D), BF16))] + home_buffers(n, chunks, sub, width)
        more, results = upper_buffers(above, width, dp_size)
        scratch += more
        outs += results + [(N.dv_sum, (1, width), F32, False)]
    return call(
        functools.partial(backward_kernel, n, dp_size, chunks, sub, first),
        N.backward_first if first else N.backward_block,
        collective_id,
        [placed_input(k, a) if first or k != N.act else (k, a, N.far) for k, a in ins],
        outs,
        scratch,
        2 * n * chunks * sub * D * (2 * hidden + 4 * width),
    )


def placed_input(name, array):
    return (name,) + (array if isinstance(array, tuple) else (array, lateness(name)))


def lateness(name):
    if name == N.dkv_in:
        return N.far
    return name not in (N.sp1, N.sp2, N.vec, N.base)


def tail_kernel(n, dp_size, chunks, sub, wide, r):
    ex = Exchange(n, chunks, sub)
    small = Total(r.bufs, r.small_recv, r.small_sems, dp_size, n, wide)
    gs = GradSum(upper_arrays(r), r.grad_sems, dp_size)
    halo = Halo(r.halo_sems, dp_size)
    meet(ex.partners() + gs.partners() + halo.partners())
    r.near = r.full
    send_home(halo, r, chunks)
    sems = r.sems
    r.dv_sum[...] = jnp.zeros_like(r.dv_sum)
    r.sums[...] = jnp.zeros_like(r.sums)

    def pre(c):
        input_grad_chunk(ex, halo, r, c)

    def own(c):
        g = input_norm_own(ex, r, c, r.vec[0:1, :], r.sums)
        r.full[ex.me, c] = g.astype(BF16)
        ex.ag_send(r.full, sems.at[1], c, 0)
        if c == chunks - 1:
            r.bufs[0] = r.base[...]
            r.bufs[0, 0:8, :] = r.sums[...]
            r.bufs[0, wide : wide + 1, : r.dv_sum.shape[1]] = r.dv_sum[...]
            small.start(0)

    def post(c):
        ex.ag_wait(r.full, sems.at[1], c, ex.nbits - 1)
        r.store(N.out, (slice(None), c))

    made = [lambda: r.need(N.a1)] + grad_items(r.a1, r.dqkv, r.up3, 0)
    stages = [pre] + rs_stages(ex, r.part, r.recv, sems.at[0]) + [own] + ag_stages(ex, r.full, sems.at[1]) + [post]
    stages[1] = with_items(ex, stages[1], made)
    after_own = chunks * (2 + ex.nbits - 1)
    extra = [(3, lambda: r.need(N.keep1, N.got1, N.keep2, N.got2, N.up4))]
    extra += tail_sums(gs)

    def spread(c, p):
        if p == 0:
            r.need(N.result)
            r.full3[ex.me, c] = r.result[c]
        else:
            ex.ag_wait(r.full3, sems.at[2], c, p - 1)
        if p < ex.nbits:
            ex.ag_send(r.full3, sems.at[2], c, p)
        else:
            r.store(N.out2, (slice(None), c))

    for p in range(ex.nbits + 1):
        slot = after_own + chunks * ex.nbits if p == ex.nbits else chunks * (1 + 2 * p)
        extra += [(slot + c, functools.partial(spread, c, p)) for c in range(chunks)]
    extra += [(after_own + 1 + i, functools.partial(small.step, i)) for i in range(len(small.axes))]
    run_stages(ex, stages, extra)
    halo.drain()
    r.total[...] = r.bufs[len(small.axes)]
    ex.drain()
    small.drain()
    gs.drain()


def backward_tail(n, dp_size, collective_id, wide, source, above, vec, base, result):
    _, chunks, sub, width = source[N.dq].shape
    split = lambda cols: (n, chunks, sub, cols)
    steps = (n * dp_size).bit_length() - 1
    ins = list(source.items()) + list(above.items()) + [(N.vec, vec), (N.base, base), (N.result, result)]
    more, results = upper_buffers(above, width, dp_size)
    outs = [(N.out, split(D), BF16, N.full), (N.out2, split(D), BF16, N.full3), (N.total, base.shape, F32, False)] + results
    scratch = comm_scratch(n, chunks, sub, "") + sem_scratch(3, n, chunks) + home_buffers(n, chunks, sub, width)
    scratch += [(N.full3, pltpu.VMEM(split(D), BF16))]
    scratch += [(N.full, pltpu.VMEM(split(D), BF16)), (N.sums, pltpu.VMEM((8, D), F32)), (N.dv_sum, pltpu.VMEM((1, width), F32))]
    scratch += [(N.bufs, pltpu.VMEM((steps + 1,) + base.shape, F32)), (N.small_recv, pltpu.VMEM((steps,) + base.shape, F32))]
    scratch += [(N.small_sems, pltpu.SemaphoreType.DMA((2, steps)))] + more
    return call(
        functools.partial(tail_kernel, n, dp_size, chunks, sub, wide),
        N.backward_tail,
        collective_id,
        [placed_input(k, a) for k, a in ins],
        outs,
        scratch,
        2 * n * chunks * sub * D * 3 * width,
    )


def id_features(ids_col, query_side):
    lane = lax.broadcasted_iota(jnp.int32, (ids_col.shape[0], HD), 1)
    bit = (ids_col >> (lane & 15)) & 1
    first = lane < 16
    second = (lane >= 16) & (lane < 32)
    inv = 1 - bit
    if query_side:
        v = jnp.where(first, bit, jnp.where(second, inv, 0)).astype(F32) * (-BIG)
    else:
        v = jnp.where(first, inv, jnp.where(second, bit, 0)).astype(F32)
    return v

def each_tile(KB, t_lo, t_hi, kn_ref, vn_ref, k_ref, v_ref, fn):
    per = k_ref.shape[0] // KB
    for segment in range(3):
        def one(t, carry, segment=segment):
            here = pl.ds(pl.multiple_of((t - segment * per) * KB, KB), KB)
            if segment == 1:
                fn(t, here, k_ref[here, :], v_ref[here, :])
            else:
                fn(t, here, kn_ref[segment // 2, here, :], vn_ref[segment // 2, here, :])
            return carry
        lax.fori_loop(jnp.maximum(t_lo, segment * per), jnp.minimum(t_hi, (segment + 1) * per), one, 0)

def fwd_kernel(HH, QB, KB, KT, nq, lo_ref, hi_ref, q_ref, kn_ref, vn_ref, k_ref, v_ref, idq_ref, idk_ref, o_ref, lse_ref, kaug, vt, qaug):
    t_lo = lo_ref[nq]
    t_hi = hi_ref[nq]
    def prep(t, here, kk, vv):
        r = pl.ds(pl.multiple_of(t * KT, KT), KT)
        feat = id_features(idk_ref[r, :], False).astype(BF16)
        for h in range(HH):
            kaug[h, r, :] = jnp.concatenate([kk[:, h * HD:(h + 1) * HD], feat], axis=1)
        vt[:, r] = vv.T
    each_tile(KT, t_lo, t_hi, kn_ref, vn_ref, k_ref, v_ref, prep)
    def qprep(t, _):
        r = pl.ds(pl.multiple_of(t * QB, QB), QB)
        feat = id_features(idq_ref[r, :], True).astype(BF16)
        qq = (q_ref[r, :] * BF16(0.125))
        for h in range(HH):
            qaug[h, :, r] = jnp.concatenate([qq[:, h * HD:(h + 1) * HD], feat], axis=1).T
        return 0
    lax.fori_loop(0, nq, qprep, 0)
    def qloop(qb, _):
        rq = pl.ds(pl.multiple_of(qb * QB, QB), QB)
        lo = lo_ref[qb]
        qts = [qaug[h, :, rq] for h in range(HH)]
        def kloop(t, c):
            r = pl.ds(pl.multiple_of(lo * KT + t * KB, KT), KB)
            new = []
            for h in range(HH):
                m, l, acc = c[h]
                s = jnp.dot(kaug[h, r, :], qts[h], preferred_element_type=F32)
                mn = jnp.maximum(m, jnp.max(s, axis=0, keepdims=True))
                p = jnp.exp(s - mn)
                al = jnp.exp(m - mn)
                l = l * al + jnp.sum(p, axis=0, keepdims=True)
                acc = acc * al + jnp.dot(vt[h * HD:(h + 1) * HD, r], p.astype(BF16), preferred_element_type=F32)
                new.append((mn, l, acc))
            return tuple(new)
        z = (jnp.full((1, QB), -3e38, F32), jnp.zeros((1, QB), F32), jnp.zeros((HD, QB), F32))
        c = lax.fori_loop(0, (hi_ref[qb] - lo) // (KB // KT), kloop, (z,) * HH)
        both = jnp.concatenate([c[h][2] / c[h][1] for h in range(HH)], axis=0)
        o_ref[rq, :] = both.T.astype(BF16)
        for h in range(HH):
            lse_ref[0, h:h + 1, rq] = c[h][0] + jnp.log(c[h][1])
        return 0
    lax.fori_loop(0, nq, qloop, 0)

def attend_fwd(q, kn, vn, k, v, idq, idk, lo, hi, HH, QB, KB, KT):
    n, cols = q.shape
    w = 3 * n
    HH = min(HH, cols // HD)
    wide = HH * HD
    near = pl.BlockSpec((2, n, wide), lambda g, *_: (0, 0, g))
    pairs = cols // wide
    nq = n // QB
    return pl.pallas_call(
        functools.partial(fwd_kernel, HH, QB, KB, KT, nq),
        grid_spec=pltpu.PrefetchScalarGridSpec(
            num_scalar_prefetch=2, grid=(pairs,),
            in_specs=[pl.BlockSpec((n, wide), lambda g, *_: (0, g)), near, near, pl.BlockSpec((n, wide), lambda g, *_: (0, g)), pl.BlockSpec((n, wide), lambda g, *_: (0, g)),
                      pl.BlockSpec((n, 1), lambda g, *_: (0, 0)), pl.BlockSpec((w, 1), lambda g, *_: (0, 0))],
            out_specs=[pl.BlockSpec((n, wide), lambda g, *_: (0, g)), pl.BlockSpec((1, HH, n), lambda g, *_: (g, 0, 0))],
            scratch_shapes=[pltpu.VMEM((HH, w, 128), BF16), pltpu.VMEM((wide, w), BF16), pltpu.VMEM((HH, 128, n), BF16)]),
        out_shape=[jax.ShapeDtypeStruct((n, cols), BF16), jax.ShapeDtypeStruct((pairs, HH, n), F32)],
        compiler_params=pltpu.CompilerParams(vmem_limit_bytes=VMEM_LIMIT),
        cost_estimate=pl.CostEstimate(flops=5 * 10**10, bytes_accessed=10**8, transcendentals=0),
        name=N.attend_fwd,
    )(lo, hi, q, kn, vn, k, v, idq, idk)

def bwd_kernel(HH, QB, KB, KT, nq, lo_ref, hi_ref, q_ref, kn_ref, vn_ref, k_ref, v_ref, idq_ref, idk_ref, o_ref, g_ref, lse_ref, dq_ref, dkv_ref, qsum_ref, kaug, vaug, kt, qaug, gaug, acc):
    w = 3 * k_ref.shape[0]
    t_lo = lo_ref[nq]
    t_hi = hi_ref[nq]
    wide = HH * HD
    lane = lax.broadcasted_iota(jnp.int32, (KT, HD), 1)
    three = ((lane >= 32) & (lane < 35))
    def zero(t, _):
        r = pl.ds(pl.multiple_of(t * KT, KT), KT)
        for i in range(2):
            dkv_ref[i, r, :] = jnp.zeros((KT, wide), BF16)
        return 0
    lax.fori_loop(0, w // KT, zero, 0)
    def prep(t, here, kk, vv):
        r = pl.ds(pl.multiple_of(t * KT, KT), KT)
        feat = jnp.where(three, 1.0, id_features(idk_ref[r, :], False)).astype(BF16)
        ones = jnp.where(three, 1.0, 0.0).astype(BF16)
        for h in range(HH):
            kaug[h, r, :] = jnp.concatenate([kk[:, h * HD:(h + 1) * HD], feat], axis=1)
            vaug[h, r, :] = jnp.concatenate([vv[:, h * HD:(h + 1) * HD], ones], axis=1)
            acc[h, r, :] = jnp.zeros((KT, 128), F32)
        kt[:, r] = kk.T
    each_tile(KT, t_lo, t_hi, kn_ref, vn_ref, k_ref, v_ref, prep)
    qsum_ref[...] = jnp.zeros((1, wide), F32)
    def pieces(x):
        a = x.astype(BF16).astype(F32)
        b = (x - a).astype(BF16).astype(F32)
        return a, b, x - a - b
    def qprep(t, _):
        r = pl.ds(pl.multiple_of(t * QB, QB), QB)
        fid = id_features(idq_ref[r, :], True).T
        row = lax.broadcasted_iota(jnp.int32, (HD, QB), 0)
        qt = (q_ref[r, :] * BF16(0.125)).T
        gg = g_ref[r, :]
        gt = gg.T
        prod = (gg.astype(F32) * o_ref[r, :].astype(F32)).T
        for h in range(HH):
            a, b, c = pieces(-lse_ref[0, h:h + 1, r])
            f = jnp.where(row == 32, a, jnp.where(row == 33, b, jnp.where(row == 34, c, fid)))
            qaug[h, :, r] = jnp.concatenate([qt[h * HD:(h + 1) * HD, :], f.astype(BF16)], axis=0)
            d = -jnp.sum(prod[h * HD:(h + 1) * HD, :], axis=0, keepdims=True)
            a, b, c = pieces(d)
            f = jnp.where(row == 32, a, jnp.where(row == 33, b, jnp.where(row == 34, c, 0.0)))
            gaug[h, :, r] = jnp.concatenate([gt[h * HD:(h + 1) * HD, :], f.astype(BF16)], axis=0)
        return 0
    lax.fori_loop(0, nq, qprep, 0)
    def qloop(qb, _):
        rq = pl.ds(pl.multiple_of(qb * QB, QB), QB)
        qq = q_ref[rq, :] * BF16(0.125)
        gg = g_ref[rq, :]
        zz = jnp.zeros((QB, HD), BF16)
        lo = lo_ref[qb]
        qts = [qaug[h, :, rq] for h in range(HH)]
        gts = [gaug[h, :, rq] for h in range(HH)]
        rhs = [jnp.concatenate([jnp.concatenate([qq[:, h * HD:(h + 1) * HD], zz], axis=1), jnp.concatenate([zz, gg[:, h * HD:(h + 1) * HD]], axis=1)], axis=0) for h in range(HH)]
        def kloop(t, c):
            r = pl.ds(pl.multiple_of(lo * KT + t * KB, KT), KB)
            new = []
            for h in range(HH):
                s = jnp.dot(kaug[h, r, :], qts[h], preferred_element_type=F32)
                dp = jnp.dot(vaug[h, r, :], gts[h], preferred_element_type=F32)
                p = jnp.exp(s)
                ds = (p * dp).astype(BF16)
                both = jnp.concatenate([ds, p.astype(BF16)], axis=1)
                acc[h, r, :] += jnp.dot(both, rhs[h], preferred_element_type=F32)
                new.append(c[h] + jnp.dot(kt[h * HD:(h + 1) * HD, r], ds, preferred_element_type=F32))
            return tuple(new)
        z = jnp.zeros((HD, QB), F32)
        c = lax.fori_loop(0, (hi_ref[qb] - lo) // (KB // KT), kloop, (z,) * HH)
        dq = (jnp.concatenate(c, axis=0) * 0.125).T
        qsum_ref[...] += jnp.sum(dq, axis=0, keepdims=True)
        dq_ref[rq, :] = dq.astype(BF16)
        return 0
    lax.fori_loop(0, nq, qloop, 0)
    def fin(t, _):
        r = pl.ds(pl.multiple_of(t * KT, KT), KT)
        sums = [acc[h, r, :] for h in range(HH)]
        for i in range(2):
            dkv_ref[i, r, :] = jnp.concatenate([x[:, i * HD:(i + 1) * HD] for x in sums], axis=1).astype(BF16)
        return 0
    lax.fori_loop(t_lo, t_hi, fin, 0)

def attend_bwd(q, kn, vn, k, v, idq, idk, lo, hi, out, grad, lse, HH, QB, KB, KT):
    n, cols = q.shape
    w = 3 * n
    HH = min(HH, cols // HD)
    wide = HH * HD
    near = pl.BlockSpec((2, n, wide), lambda g, *_: (0, 0, g))
    pairs = cols // wide
    nq = n // QB
    rows = lambda m: pl.BlockSpec((m, wide), lambda g, *_: (0, g))
    return pl.pallas_call(
        functools.partial(bwd_kernel, HH, QB, KB, KT, nq),
        grid_spec=pltpu.PrefetchScalarGridSpec(
            num_scalar_prefetch=2, grid=(pairs,),
            in_specs=[rows(n), near, near, rows(n), rows(n), pl.BlockSpec((n, 1), lambda g, *_: (0, 0)), pl.BlockSpec((w, 1), lambda g, *_: (0, 0)), rows(n), rows(n), pl.BlockSpec((1, HH, n), lambda g, *_: (g, 0, 0))],
            out_specs=[rows(n), pl.BlockSpec((2, w, wide), lambda g, *_: (0, 0, g)), pl.BlockSpec((1, wide), lambda g, *_: (0, g))],
            scratch_shapes=[pltpu.VMEM((HH, w, 128), BF16), pltpu.VMEM((HH, w, 128), BF16), pltpu.VMEM((wide, w), BF16), pltpu.VMEM((HH, 128, n), BF16), pltpu.VMEM((HH, 128, n), BF16), pltpu.VMEM((HH, w, 128), F32)]),
        out_shape=[jax.ShapeDtypeStruct((n, cols), BF16), jax.ShapeDtypeStruct((2, w, cols), BF16), jax.ShapeDtypeStruct((1, cols), F32)],
        compiler_params=pltpu.CompilerParams(vmem_limit_bytes=VMEM_LIMIT),
        cost_estimate=pl.CostEstimate(flops=5 * 10**10, bytes_accessed=10**8, transcendentals=0),
        name=N.attend_bwd,
    )(lo, hi, q, kn, vn, k, v, idq, idk, out, grad, lse)

def reach(ids_win, n, QB, KB, KT, least, most):
    w = ids_win.shape[0]
    own = ids_win[n:2 * n].reshape(n // QB, QB)
    lo = (jnp.argmax(ids_win[None, :] == own[:, :1], axis=1) // KT).astype(jnp.int32)
    hi = ((w - jnp.argmax(ids_win[::-1][None, :] == own[:, -1:], axis=1) + KT - 1) // KT).astype(jnp.int32)
    need = -(lo - hi) % (KB // KT)
    need = jnp.where(need > 0, KB // KT - need, 0)
    up = jnp.minimum(most - hi, need)
    lo, hi = lo - (need - up), hi + up
    return jnp.append(lo, jnp.min(lo)), jnp.append(hi, jnp.max(hi))


def neighbours(axis):
    peers = lax.axis_size(axis)
    up = [(i, i + 1) for i in range(peers - 1)]
    return up, [(j, i) for i, j in up]


def with_halo(array):
    up, down = neighbours(N.dp)
    return jnp.concatenate(
        [lax.ppermute(array, N.dp, up), array, lax.ppermute(array, N.dp, down)], axis=0
    )


def body(
    tokens, image_ids, cotangent, ln1_gain, ln1_bias, qkv_weight, qv_bias, proj_weight, proj_bias, scale_attn,
    ln2_gain, ln2_bias, fc1_weight, fc1_bias, fc2_weight, fc2_bias, scale_mlp,
):
    n = lax.axis_size(N.tensor)
    rows = tokens.shape[0]
    width, hidden = qkv_weight.shape[3], fc1_weight.shape[2]
    _, chunks, sub = sizes(rows, n)
    split = (n, chunks, sub)
    planes = jnp.transpose(qkv_weight, (0, 2, 1, 3))
    ids_win = with_halo(image_ids + 1)
    per = rows // TILES[3]
    place, places = lax.axis_index(N.dp), lax.axis_size(N.dp)
    least, most = jnp.where(place == 0, per, 0), jnp.where(place == places - 1, 2 * per, 3 * per)
    lo, hi = reach(ids_win, rows, *TILES[1:], least, most)
    idq, idk = ids_win[rows : 2 * rows, None], ids_win[:, None]

    dp_size = lax.axis_size(N.dp)
    made = first_block(n, dp_size, 2 * LAYERS + 1, tokens, planes, qv_bias[0], jnp.stack([ln1_gain[0], ln1_bias[0]]))
    own, hat1, sp1, a1 = made[N.after], made[N.hat1], made[N.sp1], made[N.a1]
    q, k, v = (made[name].reshape(rows, width) for name in (N.q, N.k, N.v))
    kn, vn = (made[name].reshape(2, rows, width) for name in (N.k_near, N.v_near))

    saved = []
    for level in range(LAYERS):
        kv = (kn, vn, k, v)
        attended, lse = attend_fwd(q, *kv, idq, idk, lo, hi, *TILES)
        last = level == LAYERS - 1
        after = 0 if last else level + 1
        vec = jnp.stack(
            [
                proj_bias[level], scale_attn[level], ln2_gain[level], ln2_bias[level], fc2_bias[level],
                scale_mlp[level], ln1_gain[after], ln1_bias[after],
            ]
        )
        extra = () if last else (planes, qv_bias[level + 1])
        made = forward_block(
            n, dp_size, last, level, attended, proj_weight, fc1_weight, fc2_weight, fc1_bias[level][None],
            vec, own, *extra,
        )
        keep = {name: made[name] for name in (N.u1, N.hat2, N.sp2, N.u2, N.a2, N.act, N.slope)}
        keep[N.attended] = attended.reshape(split + (width,))
        saved.append((q, kv, attended, lse, a1, hat1, sp1, keep))
        if last:
            result = made[N.after]
        else:
            own, hat1, sp1, a1 = (made[name] for name in (N.after, N.hat1, N.sp1, N.a1))
            q, k, v = (made[name].reshape(rows, width) for name in N.qkv)
            kn, vn = (made[name].reshape(2, rows, width) for name in (N.k_near, N.v_near))

    source = {N.full: cotangent.reshape(split + (D,))}
    above, grads = {}, [None] * LAYERS
    sums, narrow, dv_sums = [None] * (LAYERS + 1), [None] * LAYERS, [None] * LAYERS
    up, down = neighbours(N.dp)
    for level in reversed(range(LAYERS)):
        q, kv, attended, lse, a1, hat1, sp1, keep = saved[level]
        upper = min(level + 1, LAYERS - 1)
        vec = jnp.stack([scale_mlp[level], ln2_gain[level], scale_attn[level], ln1_gain[upper]])
        outs = backward_block(
            n, dp_size, LAYERS + level, source, above, (fc1_weight, level), (fc2_weight, level), (proj_weight, level), vec, keep,
        )
        datt, fc1b, sums[level + 1] = outs[N.datt], outs[N.fc1b], outs[N.sums]
        if above:
            grads[level + 1] = [outs["up%d_out" % (i + 1)] for i in range(4)]
            dv_sums[level + 1] = outs[N.dv_sum][0]
        above = {N.up4: outs[N.g4]}
        for name in "12":
            above[N.keep + name] = outs[N.keep + name + N._out]
            above[N.got + name] = outs[N.got + name + N._out]
        dq, dkv, q_sum = attend_bwd(
            q, *kv, idq, idk, lo, hi, attended, datt.reshape(rows, width), lse, *TILES
        )
        narrow[level] = (fc1b[0], q_sum[0])
        dkv = dkv.reshape((2, 3) + split + (width,))
        source = {
            N.dkv_in: dkv, N.dq: dq.reshape(split + (width,)), N.qkv: (planes, level), N.hat1: hat1,
            N.gm: outs[N.gm_out], N.a1: a1, N.sp1: sp1,
        }
    pad = jnp.zeros((D - width,), F32)
    flat = jnp.concatenate(
        [jnp.zeros((D,), F32)]
        + [x for i in range(1, LAYERS) for x in (dv_sums[i], pad)]
        + [x for i in range(LAYERS) for x in narrow[i]]
    )
    own_rows = -(-flat.shape[0] // (8 * D)) * 8
    flat = jnp.pad(flat, (0, own_rows * D - flat.shape[0])).reshape(own_rows, D)
    wide = 8 * (LAYERS + 1)
    base = jnp.concatenate([jnp.zeros((8, D), F32)] + sums[1:] + [flat])
    tail = backward_tail(n, dp_size, 2 * LAYERS, wide, source, above, ln1_gain[:1], base, result)
    grads[0] = [tail["up%d_out" % (i + 1)] for i in range(4)]
    grad_tokens, total = tail[N.out], tail[N.total]
    dv_total = total[wide : wide + LAYERS, :width]
    flat = total[wide + LAYERS :].reshape(-1)[: LAYERS * (hidden + width)].reshape(LAYERS, hidden + width)
    fc1b_total, qv_total = flat[:, :hidden], jnp.stack([flat[:, hidden:], dv_total], axis=1)
    stacked = lambda parts: jnp.stack([x.astype(F32) for x in parts])
    big = [
        jnp.transpose(
            stacked([x[2][:, i * width : (i + 1) * width] for x in grads for i in range(3)]).reshape(LAYERS, 3, D, width),
            (0, 2, 1, 3),
        ),
        stacked([x[3][:width] for x in grads]),
        stacked([x[1] for x in grads]),
        stacked([x[0] for x in grads]),
    ]
    total = total[:wide].reshape(LAYERS + 1, 8, D)
    upper, lower = total[1:], total[:-1]
    return (
        tail[N.out2].reshape(rows, D).astype(F32),
        grad_tokens.reshape(rows, D).astype(F32),
        lower[:, 6],
        lower[:, 7],
        big[0],
        qv_total,
        big[1],
        upper[:, 5],
        upper[:, 4],
        upper[:, 2],
        upper[:, 3],
        big[2],
        fc1b_total,
        big[3],
        upper[:, 1],
        upper[:, 0],
    )


def solution(mesh):
    cols, stack_rows = P(None, None, N.tensor), P(None, N.tensor, None)
    qkv = P(None, None, None, N.tensor)
    return jax.shard_map(
        body,
        mesh=mesh,
        in_specs=(
            P(N.dp, None), P(N.dp), P(N.dp, None), P(), P(), qkv, cols, stack_rows, P(), P(), P(), P(), cols,
            P(None, N.tensor), stack_rows, P(), P(),
        ),
        out_specs=(
            P(N.dp, None), P(N.dp, None), P(), P(), qkv, cols, stack_rows, P(), P(), P(), P(), cols,
            P(None, N.tensor), stack_rows, P(), P(),
        ),
        check_vma=False,
    )
```
